32 devices in a mesh: dp: 2 (over core), ctx: 4 (over y, x), tensor: 4 (over z).
Axes of the slice: x: 2, y: 2, z: 4, core: 2. Of those that a mesh axis runs over, the one named last changes fastest.
Arguments:
- residual: bfloat16 [2, 4096, 1536], P('dp', 'ctx'), may hold values from -6 to 6
- pre_gain: float32 [1536], replicated, may hold values from 0.1 to 1.9
- gate_weight: bfloat16 [1536, 3072], P(None, 'tensor'), may hold values from -0.15625 to 0.15625
- input_weight: bfloat16 [1536, 3072], P(None, 'tensor'), may hold values from -0.15625 to 0.15625
- state_weight: bfloat16 [1536, 256], replicated, may hold values from -0.15625 to 0.15625
- step_weight: bfloat16 [1536, 48], P(None, 'tensor'), may hold values from -0.15625 to 0.15625
- input_kernel: bfloat16 [4, 3072], P(None, 'tensor'), may hold values from -3 to 3
- state_kernel: bfloat16 [4, 256], replicated, may hold values from -3 to 3
- step_bias: float32 [48], P('tensor'), may hold values from -4.5 to -2.5
- decay_log: float32 [48], P('tensor'), may hold values from -9.5 to 0.5
- skip_gain: float32 [48], P('tensor'), may hold values from 0.5 to 2
- norm_gain: float32 [3072], P('tensor'), may hold values from 0.1 to 1.9
- out_weight: bfloat16 [3072, 1536], P('tensor'), may hold values from -0.109375 to 0.109375
- cotangent: bfloat16 [2, 4096, 1536], P('dp', 'ctx'), may hold values from -6 to 6
Outputs:
- output: bfloat16 [2, 4096, 1536], P('dp', 'ctx', 'tensor')
- input_grad: float32 [2, 4096, 1536], P('dp', 'ctx', 'tensor')
- pre_gain_grad: float32 [1536], P('tensor')
- gate_weight_grad: float32 [1536, 3072], P(None, 'tensor')
- input_weight_grad: float32 [1536, 3072], P(None, 'tensor')
- state_weight_grad: float32 [1536, 256], P(None, 'tensor')
- step_weight_grad: float32 [1536, 48], P(None, 'tensor')
- input_kernel_grad: float32 [4, 3072], P(None, 'tensor')
- state_kernel_grad: float32 [4, 256], replicated
- step_bias_grad: float32 [48], P('tensor')
- decay_log_grad: float32 [48], P('tensor')
- skip_gain_grad: float32 [48], P('tensor')
- norm_gain_grad: float32 [3072], P('tensor')
- out_weight_grad: float32 [3072, 1536], P('tensor')
The draws below stay inside these ranges and needn't reach their ends.
All inputs are finite; a program needn't handle non-finite values.
Results may differ from the reference program's by a relative error of at most 0.0024.
The reference program's roundings to bfloat16 on the way count: a program that leaves them out, or rounds other values in their place, can miss the bound.
Values may be sent and summed in bfloat16 or wider, within the bound.
No kernel may reach another device: no remote copies, remote signals or barrier semaphores. Data moves between devices by JAX's collectives and lax.ppermute only.
A program may use at most 192 MiB of HBM per device.

```python
import jax
import jax.numpy as jnp
from jax import lax

D = 1536
HEADS = 48
NSTATE = 128
CONV = 4
GROUP = 256
INNER = 3072
SEQS = 2
LENGTH = 4096


def shard_levels(own_key, dims, split, least, top_value):
    factor_of, own = 1.0, jax.random.fold_in(own_key, 6)
    for axis_at, parts in split:
        draws = jnp.exp(jax.random.uniform(jax.random.fold_in(own, axis_at), (parts,), jnp.float32, least / len(split), top_value / len(split)))
        factor_of = factor_of * jnp.repeat(draws, dims[axis_at] // parts).reshape([-1 if axis == axis_at else 1 for axis in range(len(dims))])
    return factor_of


def bell_draw(rng, dims, spread, bound, split=(), held_as=jnp.bfloat16):
    drawn = spread * jax.random.normal(rng, dims, jnp.float32)
    if split:
        drawn = drawn * shard_levels(rng, dims, split, -0.22, 0.18)
    return jnp.clip(drawn, -bound, bound).astype(held_as)


def setup_inputs(seed: int = 0) -> dict:
    arg_keys = jax.random.split(jax.random.key(seed), 15)
    residual = bell_draw(arg_keys[0], (SEQS, LENGTH, D), 1.0, 6.0, ((0, 2), (1, 4)))
    pre_gain = jnp.clip(1.0 + 0.18 * jax.random.normal(arg_keys[1], (D,), jnp.float32), 0.1, 1.9)
    gate_weight = bell_draw(arg_keys[2], (D, INNER), D ** -0.5, 0.15625, ((1, 4),))
    input_weight = bell_draw(arg_keys[3], (D, INNER), D ** -0.5, 0.15625, ((1, 4),))
    state_weight = bell_draw(arg_keys[4], (D, 2 * NSTATE), D ** -0.5, 0.15625)
    step_weight = bell_draw(arg_keys[5], (D, HEADS), D ** -0.5, 0.15625, ((1, 4),))
    input_kernel = bell_draw(arg_keys[6], (CONV, INNER), CONV ** -0.5, 3.0, ((1, 4),))
    state_kernel = bell_draw(arg_keys[7], (CONV, 2 * NSTATE), CONV ** -0.5, 3.0)
    step_bias = jnp.clip(-4.5 + 2.0 * jax.random.uniform(arg_keys[8], (HEADS,), jnp.float32) ** shard_levels(arg_keys[8], (HEADS,), ((0, 4),), -0.2, 0.2), -4.5, -2.5)
    decay_log = jnp.clip(-9.5 + 10.0 * jax.random.uniform(arg_keys[9], (HEADS,), jnp.float32) ** shard_levels(arg_keys[9], (HEADS,), ((0, 4),), -0.2, 0.2), -9.5, 0.5)
    skip_gain = jnp.clip(0.5 + 1.5 * jax.random.uniform(arg_keys[10], (HEADS,), jnp.float32) ** shard_levels(arg_keys[10], (HEADS,), ((0, 4),), -0.2, 0.2), 0.5, 2.0)
    norm_gain = jnp.clip(1.0 + 0.18 * jax.random.normal(arg_keys[11], (INNER,), jnp.float32), 0.1, 1.9)
    out_weight = bell_draw(arg_keys[12], (INNER, D), INNER ** -0.5, 0.109375, ((0, 4),))
    cotangent = bell_draw(arg_keys[13], (SEQS, LENGTH, D), 1.0, 6.0, ((0, 2), (1, 4)))
    return {"residual": residual, "pre_gain": pre_gain, "gate_weight": gate_weight, "input_weight": input_weight, "state_weight": state_weight, "step_weight": step_weight, "input_kernel": input_kernel, "state_kernel": state_kernel, "step_bias": step_bias, "decay_log": decay_log, "skip_gain": skip_gain, "norm_gain": norm_gain, "out_weight": out_weight, "cotangent": cotangent}


epsilon = 1e-05
highest = lax.Precision.HIGHEST

@jax.custom_vjp
def low(v):
    return lax.optimization_barrier(v.astype(jnp.bfloat16)).astype(jnp.float32)

@jax.custom_vjp
def low_back(v):
    return v

def low_keep(v):
    return (low(v), None)

def low_pass(kept, grad):
    return (grad,)

def back_keep(v):
    return (v, None)

def back_low(kept, grad):
    return (low(grad),)
low.defvjp(low_keep, low_pass)
low_back.defvjp(back_keep, back_low)

def silu_gate(value):
    return value * jax.nn.sigmoid(value)

def causal_conv(extended, kernel):
    span_rows = extended.shape[-2] - kernel.shape[0] + 1
    summed = kernel[0] * extended[..., 0:span_rows, :]
    for offset in range(1, kernel.shape[0]):
        summed = summed + kernel[offset] * extended[..., offset:offset + span_rows, :]
    return silu_gate(summed)

def ssd_block(carry_state, pieces):
    driven, b_block, c_block, decay_block = pieces
    cumulative = jnp.cumsum(decay_block, axis=0)
    block_size = decay_block.shape[0]
    row_index = lax.broadcasted_iota(jnp.int32, (block_size, block_size), 0)
    column_index = lax.broadcasted_iota(jnp.int32, (block_size, block_size), 1)
    causal = (row_index >= column_index)[:, :, None]
    log_gap = jnp.where(causal, cumulative[:, None, :] - cumulative[None, :, :], 0.0)
    scores = jnp.dot(c_block, b_block.T, precision=highest)
    mixing = jnp.where(causal, jnp.exp(log_gap), 0.0) * scores[:, :, None]
    inner_out = jnp.einsum('tsh,shp->thp', mixing, driven, precision=highest)
    carried = jnp.einsum('tn,hpn->thp', c_block, carry_state, precision=highest) * jnp.exp(cumulative)[:, :, None]
    tail_decay = jnp.exp(cumulative[-1][None, :] - cumulative)
    new_state = carry_state * jnp.exp(cumulative[-1])[:, None, None] + jnp.einsum('sh,shp,sn->hpn', tail_decay, driven, b_block, precision=highest)
    return (new_state, inner_out + carried)

def ssd_scan(driven, b_rows, c_rows, decay_rates, start_state):
    blocks = driven.shape[0] // GROUP
    pieces = (driven.reshape(blocks, GROUP, driven.shape[1], driven.shape[2]), b_rows.reshape(blocks, GROUP, b_rows.shape[1]), c_rows.reshape(blocks, GROUP, c_rows.shape[1]), decay_rates.reshape(blocks, GROUP, decay_rates.shape[1]))
    final_state, outputs = lax.scan(jax.checkpoint(ssd_block), start_state, pieces)
    return (final_state, outputs.reshape(driven.shape))

def mamba_layer(residual, params):
    pre_gain, gate_weight, input_weight, state_weight, step_weight, input_kernel, state_kernel, step_bias, decay_log, skip_gain, norm_gain, out_weight = params
    heads = step_weight.shape[1]
    state_size = state_weight.shape[1] // 2
    scaling = lax.rsqrt(lax.optimization_barrier(jnp.mean(residual * residual, axis=-1, keepdims=True)) + epsilon)
    normed = low(residual * scaling * pre_gain)
    gate_in = low_back(jnp.dot(normed, gate_weight, precision=highest))
    value_in = low(low_back(jnp.dot(normed, input_weight, precision=highest)))
    state_in = low(low_back(jnp.dot(normed, state_weight, precision=highest)))
    step_raw = low_back(jnp.dot(normed, step_weight, precision=highest))
    value_pad = jnp.zeros((CONV - 1, value_in.shape[1]), value_in.dtype)
    conv_values = causal_conv(jnp.concatenate([value_pad, value_in], axis=0), input_kernel)
    conv_values = conv_values.reshape(conv_values.shape[0], heads, -1)
    state_pad = jnp.zeros((CONV - 1, state_in.shape[1]), state_in.dtype)
    state_rows = causal_conv(jnp.concatenate([state_pad, state_in], axis=0), state_kernel)
    step_size = jax.nn.softplus(step_raw + step_bias)
    decay_rates = -step_size * jnp.exp(decay_log)
    start_state = jnp.zeros((heads, conv_values.shape[2], state_size), conv_values.dtype)
    unused_state, mixed = ssd_scan(conv_values * step_size[:, :, None], state_rows[:, :state_size], state_rows[:, state_size:], decay_rates, start_state)
    mixed = mixed + skip_gain[:, None] * conv_values
    mixed = mixed.reshape(mixed.shape[0], -1)
    gated = mixed * silu_gate(gate_in)
    rms_inv = lax.rsqrt(lax.optimization_barrier(jnp.mean(gated * gated, axis=-1, keepdims=True)) + epsilon)
    normed_out = low(gated * rms_inv * norm_gain)
    return residual + jnp.dot(normed_out, out_weight, precision=highest)

def reference(residual, pre_gain, gate_weight, input_weight, state_weight, step_weight, input_kernel, state_kernel, step_bias, decay_log, skip_gain, norm_gain, out_weight, cotangent):
    params = tuple((weight_arg.astype(jnp.float32) for weight_arg in (pre_gain, gate_weight, input_weight, state_weight, step_weight, input_kernel, state_kernel, step_bias, decay_log, skip_gain, norm_gain, out_weight)))
    zero_grads = tuple((jnp.zeros_like(weight_arg) for weight_arg in params))

    def one_sequence(totals, pair):
        seq_input, seq_cotangent = pair
        result, pullback = jax.vjp(mamba_layer, seq_input.astype(jnp.float32), params)
        input_part, weight_parts = pullback(seq_cotangent.astype(jnp.float32))
        new_totals = jax.tree.map(lambda running, extra_grad: running + extra_grad, totals, weight_parts)
        return (new_totals, (result.astype(jnp.bfloat16), input_part))
    totals, stacked = lax.scan(one_sequence, zero_grads, (residual, cotangent))
    return (stacked[0], stacked[1], totals[0], totals[1], totals[2], totals[3], totals[4], totals[5], totals[6], totals[7], totals[8], totals[9], totals[10], totals[11])
```

```python
import functools

import jax
import jax.numpy as jnp
from jax import lax
from jax.experimental import pallas as pl
from jax.experimental.pallas import tpu as pltpu
from jax.sharding import PartitionSpec as P

HEAD_DIM = 64
CONV = 4
EDGE = 8
BLOCK = 128
LANES = 128
epsilon = 1e-05
f32 = jnp.float32
bf16 = jnp.bfloat16

NN = (((1,), (0,)), ((), ()))
NT = (((1,), (1,)), ((), ()))
TN = (((0,), (0,)), ((), ()))


def dot(a, b, dims=NN):
    return lax.dot_general(a, b, dims, preferred_element_type=f32)


def split2(x):
    high = x.astype(bf16)
    return high, (x - high.astype(f32)).astype(bf16)


def split3(x):
    high = x.astype(bf16)
    rest = x - high.astype(f32)
    middle = rest.astype(bf16)
    return high, middle, (rest - middle.astype(f32)).astype(bf16)


def dot3(a, b, dims=NN):
    ah, al = split2(a)
    bh, bl = split2(b)
    return dot(ah, bh, dims) + (dot(ah, bl, dims) + dot(al, bh, dims))


def dot_exact(x, ones, dims):
    high, middle, low = split3(x)
    return dot(high, ones, dims) + (dot(middle, ones, dims) + dot(low, ones, dims))


def exact_dot(ones, x, dims):
    high, middle, low = split3(x)
    return dot(ones, high, dims) + (dot(ones, middle, dims) + dot(ones, low, dims))


def iota(shape, axis):
    return lax.broadcasted_iota(jnp.int32, shape, axis)


def head_map(width):
    return (iota((LANES, width), 0) == iota((LANES, width), 1) // HEAD_DIM).astype(f32).astype(bf16)


def spread(per_head, heads):
    return dot_exact(per_head, heads, NN)


def gather_heads(per_channel, heads):
    return dot_exact(per_channel, heads, NT)


def padded(row):
    return jnp.concatenate([row, jnp.zeros((1, LANES - row.shape[1]), f32)], axis=1)


def sig(v):
    return jax.nn.sigmoid(v)


def params(limit=56):
    return pltpu.CompilerParams(
        dimension_semantics=("arbitrary",), vmem_limit_bytes=limit * 1024 * 1024
    )


def whole(shape):
    return pl.BlockSpec(shape, lambda b: (0,) * len(shape))


def rows(size, width, count=0):
    if count:
        return pl.BlockSpec((size, width), lambda b: (count - 1 - b, 0))
    return pl.BlockSpec((size, width), lambda b: (b, 0))


def norm_rows(x, gain):
    scaling = lax.rsqrt(jnp.mean(x * x, axis=-1, keepdims=True) + epsilon)
    return (x * scaling * gain).astype(bf16)


def project_kernel(x_ref, gain_ref, gate_ref, value_ref, state_ref, step_ref, normed_out, gate_out, value_out, state_out, step_out):
    normed = norm_rows(x_ref[...].astype(f32), gain_ref[...])
    normed_out[...] = normed
    value_out[...] = dot(normed, value_ref[...]).astype(bf16)
    state_out[...] = dot(normed, state_ref[...]).astype(bf16)
    step_out[...] = jnp.zeros(step_out.shape, f32)
    step_out[:, : step_ref.shape[1]] = dot(normed, step_ref[...])
    gate_out[...] = dot(normed, gate_ref[...])


def project(residual, pre_gain, gate_weight, input_weight, state_weight, step_weight):
    tokens, width = residual.shape
    inner, state2 = gate_weight.shape[1], state_weight.shape[1]
    tile = min(tokens, 256)
    return pl.pallas_call(
        project_kernel,
        grid=(tokens // tile,),
        in_specs=[
            rows(tile, width),
            whole((1, width)),
            whole(gate_weight.shape),
            whole(input_weight.shape),
            whole(state_weight.shape),
            whole(step_weight.shape),
        ],
        out_specs=[rows(tile, width), rows(tile, inner), rows(tile, inner), rows(tile, state2), rows(tile, LANES)],
        out_shape=[
            jax.ShapeDtypeStruct((tokens, width), bf16),
            jax.ShapeDtypeStruct((tokens, inner), f32),
            jax.ShapeDtypeStruct((tokens, inner), bf16),
            jax.ShapeDtypeStruct((tokens, state2), bf16),
            jax.ShapeDtypeStruct((tokens, LANES), f32),
        ],
        compiler_params=params(),
        cost_estimate=pl.CostEstimate(
            flops=2 * tokens * width * (2 * inner + state2 + LANES),
            bytes_accessed=4 * tokens * width + 4 * width * inner + 6 * tokens * inner,
            transcendentals=0,
        ),
    )(residual, pre_gain, gate_weight, input_weight, state_weight, step_weight)


def convolve(before, here, kernel):
    extended = jnp.concatenate([before, here], axis=0)
    count = here.shape[0]
    first = EDGE - CONV + 1
    summed = kernel[0:1] * extended[first : first + count]
    for k in range(1, CONV):
        summed = summed + kernel[k : k + 1] * extended[first + k : first + k + count]
    return summed


def local_kernel(
    value_ref, state_ref, step_ref, halo_ref, gain_ref, value_w, state_w, value_k, state_k, bias_ref, log_ref,
    conv_out, pre_out, rows_out, spre_out, dt_out, cum_out, cumt_out, held_out, message_out, vhalo_out,
    value_before, state_before, held, total,
):
    b = pl.program_id(0)
    width = value_ref.shape[1]

    @pl.when(b == 0)
    def _():
        normed = norm_rows(halo_ref[...].astype(f32), gain_ref[...])
        value_halo = dot(normed, value_w[...]).astype(bf16)
        state_halo = dot(normed, state_w[...]).astype(bf16)
        vhalo_out[...] = value_halo
        value_before[...] = value_halo.astype(f32)[-EDGE:]
        state_before[...] = state_halo.astype(f32)[-EDGE:]
        held[...] = jnp.zeros(held.shape, f32)
        total[...] = jnp.zeros(total.shape, f32)

    value = value_ref[...].astype(f32)
    state = state_ref[...].astype(f32)
    pre = convolve(value_before[...], value, value_k[...].astype(f32))
    spre = convolve(state_before[...], state, state_k[...].astype(f32))
    value_before[...] = value[-EDGE:]
    state_before[...] = state[-EDGE:]
    conv = pre * sig(pre)
    mixed_rows = spre * sig(spre)
    pre_out[...] = pre
    spre_out[...] = spre
    conv_out[...] = conv
    rows_out[...] = mixed_rows

    dt = jax.nn.softplus(step_ref[...] + padded(bias_ref[...]))
    decay = -dt * jnp.exp(padded(log_ref[...]))
    size = value.shape[0]
    lower = (iota((size, size), 0) >= iota((size, size), 1)).astype(f32).astype(bf16)
    cum = exact_dot(lower, decay, NN)
    dt_out[...] = dt
    cum_out[...] = cum
    cumt_out[...] = cum.T[: cumt_out.shape[0]]

    heads = head_map(width)
    cum_wide = spread(cum, heads)
    last = cum_wide[size - 1 : size]
    weighted = conv * spread(dt, heads) * jnp.exp(last - cum_wide)
    held_out[0] = held[...]
    new = jnp.exp(last) * held[...] + dot3(mixed_rows[:, :LANES], weighted, TN)
    held[...] = new
    total[...] = total[...] + last

    @pl.when(b == pl.num_programs(0) - 1)
    def _():
        message_out[:LANES] = new
        message_out[LANES:] = total[...]


def local_states(value_in, state_in, step_raw, halo, pre_gain, input_weight, state_weight, input_kernel, state_kernel, step_bias, decay_log):
    tokens, inner = value_in.shape
    state2 = state_in.shape[1]
    state = state2 // 2
    blocks = tokens // BLOCK
    headrows = 16
    return pl.pallas_call(
        local_kernel,
        grid=(blocks,),
        in_specs=[
            rows(BLOCK, inner),
            rows(BLOCK, state2),
            rows(BLOCK, LANES),
            whole(halo.shape),
            whole(pre_gain.shape),
            whole(input_weight.shape),
            whole(state_weight.shape),
            whole(input_kernel.shape),
            whole(state_kernel.shape),
            whole(step_bias.shape),
            whole(decay_log.shape),
        ],
        out_specs=[
            rows(BLOCK, inner),
            rows(BLOCK, inner),
            rows(BLOCK, state2),
            rows(BLOCK, state2),
            rows(BLOCK, LANES),
            rows(BLOCK, LANES),
            pl.BlockSpec((headrows, BLOCK), lambda b: (0, b)),
            pl.BlockSpec((1, state, inner), lambda b: (b, 0, 0)),
            whole((state + EDGE, inner)),
            whole((halo.shape[0], inner)),
        ],
        out_shape=[
            jax.ShapeDtypeStruct((tokens, inner), f32),
            jax.ShapeDtypeStruct((tokens, inner), f32),
            jax.ShapeDtypeStruct((tokens, state2), f32),
            jax.ShapeDtypeStruct((tokens, state2), f32),
            jax.ShapeDtypeStruct((tokens, LANES), f32),
            jax.ShapeDtypeStruct((tokens, LANES), f32),
            jax.ShapeDtypeStruct((headrows, tokens), f32),
            jax.ShapeDtypeStruct((blocks, state, inner), f32),
            jax.ShapeDtypeStruct((state + EDGE, inner), f32),
            jax.ShapeDtypeStruct((halo.shape[0], inner), bf16),
        ],
        scratch_shapes=[
            pltpu.VMEM((EDGE, inner), f32),
            pltpu.VMEM((EDGE, state2), f32),
            pltpu.VMEM((state, inner), f32),
            pltpu.VMEM((EDGE, inner), f32),
        ],
        compiler_params=params(),
        cost_estimate=pl.CostEstimate(flops=2 * tokens * inner * 1500, bytes_accessed=tokens * inner * 14, transcendentals=tokens * inner * 2),
    )(value_in, state_in, step_raw, halo, pre_gain, input_weight, state_weight, input_kernel, state_kernel, step_bias, decay_log)


def pairs_of(heads_count):
    return heads_count * HEAD_DIM // LANES


def inner_kernel(heads_count, conv_ref, dt_ref, rows_ref, cum_ref, cumt_ref, out_ref):
    size, width = conv_ref.shape
    heads = head_map(width)
    driven = conv_ref[...] * spread(dt_ref[...], heads)
    high, low = split2(driven)
    scores = dot3(rows_ref[:, LANES:], rows_ref[:, :LANES], NT)
    causal = iota((size, size), 0) >= iota((size, size), 1)
    left = iota((size, LANES), 1) < HEAD_DIM
    cum = cum_ref[...]
    cumt = cumt_ref[...]
    for pair in range(pairs_of(heads_count)):
        span = slice(pair * LANES, (pair + 1) * LANES)
        across = jnp.concatenate([high[:, span], low[:, span]], axis=1)
        right_side = jnp.concatenate([across, across], axis=0)
        mixes = []
        for h in (2 * pair, 2 * pair + 1):
            gap = cum[:, h : h + 1] - cumt[h : h + 1, :]
            mix = jnp.exp(jnp.where(causal, gap, -1e30)) * scores
            mixes.append(jnp.concatenate(split2(mix), axis=1))
        both = dot(jnp.concatenate(mixes, axis=0), right_side)
        both = both[:, :LANES] + both[:, LANES:]
        out_ref[:, span] = jnp.where(left, both[:size], both[size:])


def inner_forward(heads_count, conv, dt, state_rows, cum, cumt):
    tokens, inner = conv.shape
    return pl.pallas_call(
        functools.partial(inner_kernel, heads_count),
        grid=(tokens // BLOCK,),
        in_specs=[
            rows(BLOCK, inner),
            rows(BLOCK, LANES),
            rows(BLOCK, state_rows.shape[1]),
            rows(BLOCK, LANES),
            pl.BlockSpec((cumt.shape[0], BLOCK), lambda b: (0, b)),
        ],
        out_specs=rows(BLOCK, inner),
        out_shape=jax.ShapeDtypeStruct((tokens, inner), f32),
        compiler_params=params(),
        cost_estimate=pl.CostEstimate(flops=2 * tokens * inner * 2000, bytes_accessed=tokens * inner * 8, transcendentals=tokens * BLOCK * heads_count),
    )(conv, dt, state_rows, cum, cumt)


def combine_kernel(
    count, intra_ref, conv_ref, rows_ref, cum_ref, held_ref, own_ref, *refs
):
    message_refs, (gate_ref, grad_ref, gain_ref, skip_ref, mixed_out, sums_out, held_out, end_out, start, total) = refs[:count], refs[count:]
    b = pl.program_id(0)
    size, width = conv_ref.shape
    state = held_ref.shape[1]

    @pl.when(b == 0)
    def _():
        entering = jnp.zeros((state, width), f32)
        passed = jnp.zeros((EDGE, width), f32)
        for ref in message_refs:
            entering = entering + jnp.exp(passed[0:1]) * ref[:state]
            passed = passed + ref[state:]
        start[...] = entering
        total[...] = jnp.zeros(total.shape, f32)
        end_out[...] = own_ref[:state] + jnp.exp(own_ref[state : state + 1]) * entering

    heads = head_map(width)
    cum_wide = spread(cum_ref[...], heads)
    held = held_ref[0] + jnp.exp(total[0:1]) * start[...]
    held_out[0] = held
    total[...] = total[...] + cum_wide[size - 1 : size]
    skip = spread(jnp.broadcast_to(padded(skip_ref[...]), (EDGE, LANES)), heads)[0:1]
    carried = jnp.exp(cum_wide) * dot3(rows_ref[:, LANES:], held)
    mixed = (intra_ref[...] + carried) + skip * conv_ref[...]
    mixed_out[...] = mixed
    gate = gate_ref[...]
    gated = mixed * (gate * sig(gate))
    ones = jnp.ones((EDGE, width), bf16)
    square = exact_dot(ones, gated * gated, NT)
    inner = exact_dot(ones, grad_ref[...] * gain_ref[...] * gated, NT)
    sums_out[...] = jnp.where(iota(square.shape, 0) == 0, square, inner)


def combine(intra, conv, state_rows, cum, held, own, messages, gate_in, grad_normed, norm_gain, skip_gain):
    tokens, inner = conv.shape
    blocks, state, _ = held.shape
    state_block = pl.BlockSpec((1, state, inner), lambda b: (b, 0, 0))
    return pl.pallas_call(
        functools.partial(combine_kernel, len(messages)),
        grid=(blocks,),
        in_specs=[
            rows(BLOCK, inner),
            rows(BLOCK, inner),
            rows(BLOCK, state_rows.shape[1]),
            rows(BLOCK, LANES),
            state_block,
            whole(own.shape),
            *[whole(own.shape) for _ in messages],
            rows(BLOCK, inner),
            rows(BLOCK, inner),
            whole(norm_gain.shape),
            whole(skip_gain.shape),
        ],
        out_specs=[
            rows(BLOCK, inner),
            pl.BlockSpec((EDGE, BLOCK), lambda b: (0, b)),
            state_block,
            whole((state, inner)),
        ],
        out_shape=[
            jax.ShapeDtypeStruct((tokens, inner), f32),
            jax.ShapeDtypeStruct((EDGE, tokens), f32),
            jax.ShapeDtypeStruct(held.shape, f32),
            jax.ShapeDtypeStruct((state, inner), f32),
        ],
        scratch_shapes=[pltpu.VMEM((state, inner), f32), pltpu.VMEM((EDGE, inner), f32)],
        compiler_params=params(),
        cost_estimate=pl.CostEstimate(flops=2 * tokens * inner * 1000, bytes_accessed=tokens * inner * 28, transcendentals=tokens * inner * 2),
    )(intra, conv, state_rows, cum, held, own, *messages, gate_in, grad_normed, norm_gain, skip_gain)


def column(row, width):
    return jnp.concatenate([jnp.broadcast_to(row, (LANES, row.shape[1])).T] * (width // LANES), axis=1)


def gate_back_kernel(count, inner_total, mixed_ref, gate_ref, grad_ref, rows_ref, cum_ref, gain_ref, *refs):
    sums_refs, (normed_out, gate_out, dmix_out, later_out, message_out, gain_out, later, total) = refs[:count], refs[count:]
    b = pl.program_id(0)
    size, width = mixed_ref.shape

    @pl.when(b == 0)
    def _():
        later[...] = jnp.zeros(later.shape, f32)
        total[...] = jnp.zeros(total.shape, f32)
        gain_out[...] = jnp.zeros(gain_out.shape, f32)

    sums = sums_refs[0][...]
    for ref in sums_refs[1:]:
        sums = sums + ref[...]
    rms_row = lax.rsqrt(sums[0:1] / inner_total + epsilon)
    pull_row = rms_row * rms_row * rms_row * sums[1:2] / inner_total
    rms = column(rms_row, width)
    pull = column(pull_row, width)
    gain = gain_ref[...]
    gate = gate_ref[...]
    mixed = mixed_ref[...]
    grad = grad_ref[...]
    gate_sig = sig(gate)
    gate_silu = gate * gate_sig
    gated = mixed * gate_silu
    normed_out[...] = (gated * rms * gain).astype(bf16)
    gain_part = (grad * gated * rms).reshape(size // EDGE, EDGE, width)
    gain_out[...] = gain_out[...] + jnp.sum(gain_part, axis=0)
    grad_gated = rms * gain * grad - gated * pull
    gate_out[...] = (grad_gated * mixed * gate_sig * (1.0 + gate * (1.0 - gate_sig))).astype(bf16)
    grad_mixed = grad_gated * gate_silu
    dmix_out[...] = grad_mixed

    cum_wide = spread(cum_ref[...], head_map(width))
    last = cum_wide[size - 1 : size]
    later_out[0] = later[...]
    new = jnp.exp(last) * later[...] + dot3(rows_ref[:, LANES:], jnp.exp(cum_wide) * grad_mixed, TN)
    later[...] = new
    total[...] = total[...] + last

    @pl.when(b == pl.num_programs(0) - 1)
    def _():
        message_out[:LANES] = new
        message_out[LANES:] = total[...]


def gate_back(mixed, gate_in, grad_normed, state_rows, cum, norm_gain, sums, inner_total):
    tokens, inner = mixed.shape
    blocks = tokens // BLOCK
    state = state_rows.shape[1] // 2
    return pl.pallas_call(
        functools.partial(gate_back_kernel, len(sums), inner_total),
        grid=(blocks,),
        in_specs=[
            rows(BLOCK, inner, blocks),
            rows(BLOCK, inner, blocks),
            rows(BLOCK, inner, blocks),
            rows(BLOCK, 2 * state, blocks),
            rows(BLOCK, LANES, blocks),
            whole(norm_gain.shape),
            *[pl.BlockSpec((EDGE, BLOCK), lambda b: (0, blocks - 1 - b)) for _ in sums],
        ],
        out_specs=[
            rows(BLOCK, inner, blocks),
            rows(BLOCK, inner, blocks),
            rows(BLOCK, inner, blocks),
            pl.BlockSpec((1, state, inner), lambda b: (blocks - 1 - b, 0, 0)),
            whole((state + EDGE, inner)),
            whole((EDGE, inner)),
        ],
        out_shape=[
            jax.ShapeDtypeStruct((tokens, inner), bf16),
            jax.ShapeDtypeStruct((tokens, inner), bf16),
            jax.ShapeDtypeStruct((tokens, inner), f32),
            jax.ShapeDtypeStruct((blocks, state, inner), f32),
            jax.ShapeDtypeStruct((state + EDGE, inner), f32),
            jax.ShapeDtypeStruct((EDGE, inner), f32),
        ],
        scratch_shapes=[pltpu.VMEM((state, inner), f32), pltpu.VMEM((EDGE, inner), f32)],
        compiler_params=params(),
        cost_estimate=pl.CostEstimate(flops=2 * tokens * inner * 1000, bytes_accessed=tokens * inner * 26, transcendentals=tokens * inner * 2),
    )(mixed, gate_in, grad_normed, state_rows, cum, norm_gain, *sums)


def inner_back_kernel(heads_count, conv_ref, dt_ref, rows_ref, cum_ref, cumt_ref, dmix_ref, driven_out, rows_out):
    size, width = conv_ref.shape
    heads = head_map(width)
    driven = conv_ref[...] * spread(dt_ref[...], heads)
    dmix_high, dmix_low = split2(dmix_ref[...])
    b_rows = rows_ref[:, :LANES]
    c_rows = rows_ref[:, LANES:]
    scores = dot3(b_rows, c_rows, NT)
    causal = iota((size, size), 1) >= iota((size, size), 0)
    left = iota((size, LANES), 1) < HEAD_DIM
    cum = cum_ref[...]
    cumt = cumt_ref[...]
    score_grad = jnp.zeros((size, size), f32)
    for pair in range(pairs_of(heads_count)):
        span = slice(pair * LANES, (pair + 1) * LANES)
        across = jnp.concatenate([dmix_high[:, span], dmix_low[:, span]], axis=1)
        right_side = jnp.concatenate([across, across], axis=0)
        taking = jnp.concatenate([dmix_high[:, span], dmix_high[:, span], dmix_low[:, span]], axis=1)
        mixes = []
        for h in (2 * pair, 2 * pair + 1):
            mine = left if h % 2 == 0 else jnp.logical_not(left)
            own_high, own_low = split2(jnp.where(mine, driven[:, span], 0.0))
            mix_grad = dot(jnp.concatenate([own_high, own_low, own_high], axis=1), taking, NT)
            gap = cumt[h : h + 1, :] - cum[:, h : h + 1]
            kept = jnp.exp(jnp.where(causal, gap, -1e30))
            score_grad = score_grad + mix_grad * kept
            mixes.append(jnp.concatenate(split2(kept * scores), axis=1))
        both = dot(jnp.concatenate(mixes, axis=0), right_side)
        both = both[:, :LANES] + both[:, LANES:]
        driven_out[:, span] = jnp.where(left, both[:size], both[size:])
    rows_out[:, :LANES] = dot3(score_grad, c_rows, NN)
    rows_out[:, LANES:] = dot3(score_grad, b_rows, TN)


def inner_back(heads_count, conv, dt, state_rows, cum, cumt, grad_mixed):
    tokens, inner = conv.shape
    return pl.pallas_call(
        functools.partial(inner_back_kernel, heads_count),
        grid=(tokens // BLOCK,),
        in_specs=[
            rows(BLOCK, inner),
            rows(BLOCK, LANES),
            rows(BLOCK, state_rows.shape[1]),
            rows(BLOCK, LANES),
            pl.BlockSpec((cumt.shape[0], BLOCK), lambda b: (0, b)),
            rows(BLOCK, inner),
        ],
        out_specs=[rows(BLOCK, inner), rows(BLOCK, state_rows.shape[1])],
        out_shape=[
            jax.ShapeDtypeStruct((tokens, inner), f32),
            jax.ShapeDtypeStruct(state_rows.shape, f32),
        ],
        compiler_params=params(),
        cost_estimate=pl.CostEstimate(flops=2 * tokens * inner * 3000, bytes_accessed=tokens * inner * 12, transcendentals=tokens * BLOCK * heads_count),
    )(conv, dt, state_rows, cum, cumt, grad_mixed)


def finish_kernel(
    count, driven_ref, drows_ref, dmix_ref, mixed_ref, conv_ref, pre_ref, value_ref, dt_ref, cum_ref, step_ref, rows_ref,
    held_ref, end_ref, later_ref, *refs
):
    message_refs = refs[:count]
    (
        vhalo_ref, kernel_ref, skip_ref, bias_ref, log_ref,
        grad_value_out, grad_rows_out, grad_step_out, last_out, first_out, kernel_out, small_out,
        entering, total, held_next, pre_next, skip_sum,
    ) = refs[count:]
    b = pl.program_id(0)
    size, width = conv_ref.shape
    state = held_ref.shape[1]
    heads = head_map(width)

    @pl.when(b == 0)
    def _():
        coming = jnp.zeros((state, width), f32)
        passed = jnp.zeros((EDGE, width), f32)
        for ref in message_refs:
            coming = coming + jnp.exp(passed[0:1]) * ref[:state]
            passed = passed + ref[state:]
        entering[...] = coming
        total[...] = jnp.zeros(total.shape, f32)
        held_next[...] = end_ref[...]
        pre_next[...] = jnp.zeros(pre_next.shape, f32)
        kernel_out[...] = jnp.zeros(kernel_out.shape, f32)
        small_out[...] = jnp.zeros(small_out.shape, f32)
        skip_sum[...] = jnp.zeros(skip_sum.shape, f32)

    b_rows = rows_ref[:, :LANES]
    cum_wide = spread(cum_ref[...], heads)
    last = cum_wide[size - 1 : size]
    dt = dt_ref[...]
    dt_wide = spread(dt, heads)
    conv = conv_ref[...]
    dmix = dmix_ref[...]
    driven = conv * dt_wide
    later = later_ref[0] + jnp.exp(total[0:1]) * entering[...]
    total[...] = total[...] + last
    tail = jnp.exp(last - cum_wide)
    ddriven = driven_ref[...] + tail * dot3(b_rows, later)
    held = held_ref[0]
    grad_rows_out[:, :LANES] = drows_ref[:, :LANES] + dot3(tail * driven, later, NT)
    grad_rows_out[:, LANES:] = drows_ref[:, LANES:] + dot3(jnp.exp(cum_wide) * dmix, held, NT)

    skip = spread(jnp.broadcast_to(padded(skip_ref[...]), (EDGE, LANES)), heads)[0:1]
    from_skip = dmix * conv
    skip_sum[...] = skip_sum[...] + jnp.sum(from_skip.reshape(size // EDGE, EDGE, width), axis=0)
    level = gather_heads(dmix * (mixed_ref[...] - skip * conv) - driven * ddriven, heads)
    through = gather_heads(ddriven * conv, heads)
    boundary = jnp.sum((later * held_next[...]).reshape(state // EDGE, EDGE, width), axis=0)
    boundary = jnp.sum(gather_heads(boundary, heads), axis=0, keepdims=True)
    held_next[...] = held
    upper = (iota((size, size), 1) >= iota((size, size), 0)).astype(f32).astype(bf16)
    ddecay = exact_dot(upper, level, NN) + boundary
    rate = jnp.exp(padded(log_ref[...]))
    dstep = (through - ddecay * rate) * sig(step_ref[...] + padded(bias_ref[...]))
    grad_step_out[...] = dstep[:, : grad_step_out.shape[1]].astype(bf16)
    dlog = jnp.sum(-ddecay * dt * rate, axis=0, keepdims=True)
    small_out[1:2] = small_out[1:2] + jnp.sum(dstep, axis=0, keepdims=True)
    small_out[2:3] = small_out[2:3] + dlog

    pre = pre_ref[...]
    pre_sig = sig(pre)
    dpre = (ddriven * dt_wide + skip * dmix) * (pre_sig * (1.0 + pre * (1.0 - pre_sig)))
    extended = jnp.concatenate([dpre, pre_next[...]], axis=0)
    value = value_ref[...].astype(f32)
    taps = kernel_ref[...].astype(f32)
    dvalue = jnp.zeros((size, width), f32)
    for k in range(CONV):
        shifted = extended[CONV - 1 - k : CONV - 1 - k + size]
        dvalue = dvalue + taps[k : k + 1] * shifted
        kernel_out[k : k + 1] = kernel_out[k : k + 1] + jnp.sum(value * shifted, axis=0, keepdims=True)
    grad_value_out[...] = dvalue.astype(bf16)
    pre_next[...] = dpre[:EDGE]

    @pl.when(b == 0)
    def _():
        last_out[...] = dvalue[-2 * EDGE :]

    @pl.when(b == pl.num_programs(0) - 1)
    def _():
        first_out[...] = dpre[:EDGE]
        ahead = jnp.concatenate([jnp.zeros((EDGE, width), f32), dpre[:EDGE]], axis=0)
        halo = vhalo_ref[...].astype(f32)[-EDGE:]
        for k in range(CONV):
            shifted = ahead[CONV - 1 - k : CONV - 1 - k + EDGE]
            kernel_out[k : k + 1] = kernel_out[k : k + 1] + jnp.sum(halo * shifted, axis=0, keepdims=True)
        small_out[0:1] = jnp.sum(gather_heads(skip_sum[...], heads), axis=0, keepdims=True)


def finish(grad_driven, grad_rows, grad_mixed, mixed, conv, pre, value_in, dt, cum, step_raw, state_rows, held, end_state, later,
           messages, vhalo, input_kernel, skip_gain, step_bias, decay_log):
    tokens, inner = conv.shape
    blocks, state, _ = held.shape
    head_count = skip_gain.shape[1]
    state_block = pl.BlockSpec((1, state, inner), lambda b: (blocks - 1 - b, 0, 0))
    wide = rows(BLOCK, inner, blocks)
    narrow = rows(BLOCK, LANES, blocks)
    return pl.pallas_call(
        functools.partial(finish_kernel, len(messages)),
        grid=(blocks,),
        in_specs=[
            wide, rows(BLOCK, 2 * state, blocks), wide, wide, wide, wide, wide, narrow, narrow, narrow,
            rows(BLOCK, 2 * state, blocks),
            state_block, whole(end_state.shape), state_block,
            *[whole(m.shape) for m in messages],
            whole(vhalo.shape), whole(input_kernel.shape), whole(skip_gain.shape), whole(step_bias.shape), whole(decay_log.shape),
        ],
        out_specs=[
            wide,
            rows(BLOCK, 2 * state, blocks),
            rows(BLOCK, head_count, blocks),
            whole((2 * EDGE, inner)),
            whole((EDGE, inner)),
            whole((EDGE, inner)),
            whole((EDGE, LANES)),
        ],
        out_shape=[
            jax.ShapeDtypeStruct((tokens, inner), bf16),
            jax.ShapeDtypeStruct((tokens, 2 * state), f32),
            jax.ShapeDtypeStruct((tokens, head_count), bf16),
            jax.ShapeDtypeStruct((2 * EDGE, inner), f32),
            jax.ShapeDtypeStruct((EDGE, inner), f32),
            jax.ShapeDtypeStruct((EDGE, inner), f32),
            jax.ShapeDtypeStruct((EDGE, LANES), f32),
        ],
        scratch_shapes=[
            pltpu.VMEM((state, inner), f32),
            pltpu.VMEM((EDGE, inner), f32),
            pltpu.VMEM((state, inner), f32),
            pltpu.VMEM((EDGE, inner), f32),
            pltpu.VMEM((EDGE, inner), f32),
        ],
        compiler_params=params(),
        cost_estimate=pl.CostEstimate(flops=2 * tokens * inner * 3000, bytes_accessed=tokens * inner * 36, transcendentals=tokens * inner * 3),
    )(grad_driven, grad_rows, grad_mixed, mixed, conv, pre, value_in, dt, cum, step_raw, state_rows, held, end_state, later,
      *messages, vhalo, input_kernel, skip_gain, step_bias, decay_log)


def from_before(value, axis, by=1):
    count = lax.axis_size(axis)
    return lax.ppermute(value, axis, [(i, i + by) for i in range(count - by)])


def from_after(value, axis, by=1):
    count = lax.axis_size(axis)
    return lax.ppermute(value, axis, [(i + by, i) for i in range(count - by)])


def from_all(value, axis):
    count = lax.axis_size(axis)
    return [lax.ppermute(value, axis, [(i, (i + by) % count) for i in range(count)]) for by in range(1, count)]


def own_part(array, axis_name, dim):
    size = array.shape[dim] // lax.axis_size(axis_name)
    return lax.dynamic_slice_in_dim(array, lax.axis_index(axis_name) * size, size, dim)


def state_conv_back(grad_rows, spre, taps, state_in, shalo, spre_after, grad_after):
    def through(grad, pre):
        s = sig(pre)
        return grad * (s * (1.0 + pre * (1.0 - s)))

    tokens = grad_rows.shape[0]
    dpre = through(grad_rows, spre)
    after = through(grad_after, spre_after)
    extended = jnp.concatenate([dpre, after], axis=0)
    dstate = sum(taps[k : k + 1] * extended[CONV - 1 - k : CONV - 1 - k + tokens] for k in range(CONV))
    inputs = jnp.concatenate([shalo, state_in], axis=0).astype(f32)
    first = shalo.shape[0] - CONV + 1
    dtaps = jnp.stack([jnp.sum(dpre * inputs[first + k : first + k + tokens], axis=0) for k in range(CONV)])
    return dstate.astype(bf16), dtaps


def per_device(residual, pre_gain, gate_weight, input_weight, state_weight, step_weight, input_kernel, state_kernel,
               step_bias, decay_log, skip_gain, norm_gain, out_weight, cotangent):
    seqs, tokens, width = residual.shape
    outs = [
        one_sequence(residual[i], pre_gain, gate_weight, input_weight, state_weight, step_weight, input_kernel, state_kernel,
                     step_bias, decay_log, skip_gain, norm_gain, out_weight, cotangent[i])
        for i in range(seqs)
    ]
    output = jnp.stack([o[0] for o in outs])
    input_grad = jnp.stack([o[1] for o in outs])
    sums = [functools.reduce(jnp.add, parts) for parts in zip(*[o[2:] for o in outs])]
    sums = lax.psum(tuple(sums), ("dp", "ctx"))
    state_taps = sums[6]
    spread_taps = lax.dynamic_update_slice_in_dim(
        jnp.zeros((CONV, state_weight.shape[1]), f32), state_taps, lax.axis_index("tensor") * state_taps.shape[1], 1
    )
    return (output, input_grad, *sums[:6], lax.psum(spread_taps, "tensor"), *sums[7:])


def one_sequence(residual, pre_gain, gate_weight, input_weight, state_weight, step_weight, input_kernel, state_kernel,
                 step_bias, decay_log, skip_gain, norm_gain, out_weight, cotangent):
    tokens, width = residual.shape
    tensor_size = lax.axis_size("tensor")
    ctx_size = lax.axis_size("ctx")
    inner = gate_weight.shape[1]
    inner_total = inner * tensor_size
    head_count = step_weight.shape[1]
    row = lambda v: v.reshape(1, -1)

    halo = from_before(residual[-2 * EDGE :], "ctx")
    normed, gate_in, value_in, state_in, step_raw = project(
        residual, row(pre_gain), gate_weight, input_weight, state_weight, step_weight
    )
    conv, pre, state_rows, spre, dt, cum, cumt, held, message, vhalo = local_states(
        value_in, state_in, step_raw, halo, row(pre_gain), input_weight, state_weight, input_kernel, state_kernel,
        row(step_bias), row(decay_log)
    )
    messages = [from_before(message, "ctx", by) for by in range(1, ctx_size)]
    intra = inner_forward(head_count, conv, dt, state_rows, cum, cumt)
    grad_normed = dot(cotangent, out_weight, NT)
    mixed, sums, held, end_state = combine(
        intra, conv, state_rows, cum, held, message, messages, gate_in, grad_normed, row(norm_gain), row(skip_gain)
    )
    all_sums = [sums, *from_all(sums, "tensor")]
    normed_out, grad_gate, grad_mixed, later, message, gain_grad = gate_back(
        mixed, gate_in, grad_normed, state_rows, cum, row(norm_gain), all_sums, inner_total
    )
    messages = [from_after(message, "ctx", by) for by in range(1, ctx_size)]

    resid_part = own_part(residual, "tensor", 1).astype(f32)
    partial_out = dot(normed_out, out_weight)
    branch = lax.psum_scatter(partial_out, "tensor", scatter_dimension=1, tiled=True)
    output = (resid_part + branch).astype(bf16)
    out_weight_grad = dot(normed_out, cotangent, TN)
    gate_weight_grad = dot(normed, grad_gate, TN)

    grad_driven, grad_rows = inner_back(head_count, conv, dt, state_rows, cum, cumt, grad_mixed)
    grad_value, grad_rows, grad_step, last_rows, first_rows, kernel_grad, small = finish(
        grad_driven, grad_rows, grad_mixed, mixed, conv, pre, value_in, dt, cum, step_raw, state_rows, held, end_state, later,
        messages, vhalo, input_kernel, row(skip_gain), row(step_bias), row(decay_log)
    )
    ahead = from_after(first_rows, "ctx")
    taps = input_kernel.astype(f32)
    ahead = jnp.concatenate([jnp.zeros((2 * EDGE, inner), f32), ahead], axis=0)
    fixed = last_rows + sum(taps[k : k + 1] * ahead[CONV - 1 - k : CONV - 1 - k + 2 * EDGE] for k in range(CONV))
    grad_value = lax.dynamic_update_slice_in_dim(grad_value, fixed.astype(bf16), tokens - 2 * EDGE, 0)

    part = state_weight.shape[1] // tensor_size
    shalo = from_before(own_part(state_in[-2 * EDGE :], "tensor", 1), "ctx")
    spre_after = from_after(own_part(spre[:EDGE], "tensor", 1), "ctx")
    grad_after = from_after(grad_rows[:EDGE], "ctx")
    quarter = lax.psum_scatter(jnp.concatenate([grad_rows, grad_after], axis=0), "tensor", scatter_dimension=1, tiled=True)
    grad_state, state_taps_grad = state_conv_back(
        quarter[:tokens], own_part(spre, "tensor", 1), own_part(state_kernel, "tensor", 1).astype(f32),
        own_part(state_in, "tensor", 1), shalo, spre_after, quarter[tokens:]
    )
    input_partial = dot(grad_gate, gate_weight, NT) + dot(grad_value, input_weight, NT) + dot(grad_step, step_weight, NT)
    input_partial = input_partial + dot(grad_state, own_part(state_weight, "tensor", 1), NT)
    normed_grad = lax.psum_scatter(input_partial, "tensor", scatter_dimension=1, tiled=True)
    flat = residual.astype(f32)
    scaling = lax.rsqrt(jnp.mean(flat * flat, axis=-1, keepdims=True) + epsilon)
    gain_part = own_part(pre_gain, "tensor", 0)
    row_total = lax.psum(jnp.sum(normed_grad * gain_part * resid_part, axis=-1), "tensor")
    grad_part = own_part(cotangent, "tensor", 1).astype(f32)
    input_grad = (
        grad_part + scaling * gain_part * normed_grad - resid_part * (scaling * scaling * scaling) * row_total[:, None] / width
    )
    pre_gain_grad = jnp.sum(normed_grad * resid_part * scaling, axis=0)
    return (
        output,
        input_grad,
        pre_gain_grad,
        gate_weight_grad,
        dot(normed, grad_value, TN),
        dot(normed, grad_state, TN),
        dot(normed, grad_step, TN),
        kernel_grad[:CONV],
        state_taps_grad,
        small[1, :head_count],
        small[2, :head_count],
        small[0, :head_count],
        jnp.sum(gain_grad, axis=0),
        out_weight_grad,
    )


def solution(mesh):
    in_specs = (
        P("dp", "ctx", None),
        P(),
        P(None, "tensor"),
        P(None, "tensor"),
        P(),
        P(None, "tensor"),
        P(None, "tensor"),
        P(),
        P("tensor"),
        P("tensor"),
        P("tensor"),
        P("tensor"),
        P("tensor", None),
        P("dp", "ctx", None),
    )
    out_specs = (
        P("dp", "ctx", "tensor"),
        P("dp", "ctx", "tensor"),
        P("tensor"),
        P(None, "tensor"),
        P(None, "tensor"),
        P(None, "tensor"),
        P(None, "tensor"),
        P(None, "tensor"),
        P(),
        P("tensor"),
        P("tensor"),
        P("tensor"),
        P("tensor"),
        P("tensor", None),
    )
    return jax.shard_map(per_device, mesh=mesh, in_specs=in_specs, out_specs=out_specs, check_vma=False)
```

```python
import functools

import jax
import jax.numpy as jnp
from jax import lax
from jax.experimental import pallas as pl
from jax.experimental.pallas import tpu as pltpu
from jax.sharding import PartitionSpec as P

HEAD_DIM = 64
CONV = 4
EDGE = 8
BLOCK = 128
LANES = 128
epsilon = 1e-05
f32 = jnp.float32
bf16 = jnp.bfloat16

NN = (((1,), (0,)), ((), ()))
NT = (((1,), (1,)), ((), ()))
TN = (((0,), (0,)), ((), ()))


def dot(a, b, dims=NN):
    return lax.dot_general(a, b, dims, preferred_element_type=f32)


def split2(x):
    high = x.astype(bf16)
    return high, (x - high.astype(f32)).astype(bf16)


def split3(x):
    high = x.astype(bf16)
    rest = x - high.astype(f32)
    middle = rest.astype(bf16)
    return high, middle, (rest - middle.astype(f32)).astype(bf16)


def dot3(a, b, dims=NN):
    ah, al = split2(a)
    bh, bl = split2(b)
    return dot(ah, bh, dims) + (dot(ah, bl, dims) + dot(al, bh, dims))


def dot_exact(x, ones, dims):
    high, middle, low = split3(x)
    return dot(high, ones, dims) + (dot(middle, ones, dims) + dot(low, ones, dims))


def exact_dot(ones, x, dims):
    high, middle, low = split3(x)
    return dot(ones, high, dims) + (dot(ones, middle, dims) + dot(ones, low, dims))


def iota(shape, axis):
    return lax.broadcasted_iota(jnp.int32, shape, axis)


def head_map(width):
    return (iota((LANES, width), 0) == iota((LANES, width), 1) // HEAD_DIM).astype(f32).astype(bf16)


def spread(per_head, heads):
    return dot_exact(per_head, heads, NN)


def gather_heads(per_channel, heads):
    return dot_exact(per_channel, heads, NT)


def padded(row):
    return jnp.concatenate([row, jnp.zeros((1, LANES - row.shape[1]), f32)], axis=1)


def sig(v):
    return jax.nn.sigmoid(v)


def params(limit=56):
    return pltpu.CompilerParams(
        dimension_semantics=("arbitrary",), vmem_limit_bytes=limit * 1024 * 1024
    )


def whole(shape):
    return pl.BlockSpec(shape, lambda b: (0,) * len(shape))


def rows(size, width, count=0):
    if count:
        return pl.BlockSpec((size, width), lambda b: (count - 1 - b, 0))
    return pl.BlockSpec((size, width), lambda b: (b, 0))


def norm_rows(x, gain):
    scaling = lax.rsqrt(jnp.mean(x * x, axis=-1, keepdims=True) + epsilon)
    return (x * scaling * gain).astype(bf16)


def project_kernel(x_ref, gain_ref, gate_ref, value_ref, state_ref, step_ref, normed_out, gate_out, value_out, state_out, step_out):
    normed = norm_rows(x_ref[...].astype(f32), gain_ref[...])
    normed_out[...] = normed
    value_out[...] = dot(normed, value_ref[...]).astype(bf16)
    state_out[...] = dot(normed, state_ref[...]).astype(bf16)
    step_out[...] = jnp.zeros(step_out.shape, f32)
    step_out[:, : step_ref.shape[1]] = dot(normed, step_ref[...])
    gate_out[...] = dot(normed, gate_ref[...])


def project(residual, pre_gain, gate_weight, input_weight, state_weight, step_weight):
    tokens, width = residual.shape
    inner, state2 = gate_weight.shape[1], state_weight.shape[1]
    tile = min(tokens, 256)
    return pl.pallas_call(
        project_kernel,
        grid=(tokens // tile,),
        in_specs=[
            rows(tile, width),
            whole((1, width)),
            whole(gate_weight.shape),
            whole(input_weight.shape),
            whole(state_weight.shape),
            whole(step_weight.shape),
        ],
        out_specs=[rows(tile, width), rows(tile, inner), rows(tile, inner), rows(tile, state2), rows(tile, LANES)],
        out_shape=[
            jax.ShapeDtypeStruct((tokens, width), bf16),
            jax.ShapeDtypeStruct((tokens, inner), f32),
            jax.ShapeDtypeStruct((tokens, inner), bf16),
            jax.ShapeDtypeStruct((tokens, state2), bf16),
            jax.ShapeDtypeStruct((tokens, LANES), f32),
        ],
        compiler_params=params(),
        cost_estimate=pl.CostEstimate(
            flops=2 * tokens * width * (2 * inner + state2 + LANES),
            bytes_accessed=4 * tokens * width + 4 * width * inner + 6 * tokens * inner,
            transcendentals=0,
        ),
    )(residual, pre_gain, gate_weight, input_weight, state_weight, step_weight)


def convolve(before, here, kernel):
    extended = jnp.concatenate([before, here], axis=0)
    count = here.shape[0]
    first = EDGE - CONV + 1
    summed = kernel[0:1] * extended[first : first + count]
    for k in range(1, CONV):
        summed = summed + kernel[k : k + 1] * extended[first + k : first + k + count]
    return summed


def local_kernel(
    value_ref, state_ref, step_ref, halo_ref, gain_ref, value_w, state_w, value_k, state_k, bias_ref, log_ref,
    conv_out, pre_out, rows_out, spre_out, dt_out, cum_out, cumt_out, held_out, message_out, vhalo_out, shalo_out,
    value_before, state_before, held, total,
):
    b = pl.program_id(0)
    width = value_ref.shape[1]

    @pl.when(b == 0)
    def _():
        normed = norm_rows(halo_ref[...].astype(f32), gain_ref[...])
        value_halo = dot(normed, value_w[...]).astype(bf16)
        state_halo = dot(normed, state_w[...]).astype(bf16)
        vhalo_out[...] = value_halo
        shalo_out[...] = state_halo
        value_before[...] = value_halo.astype(f32)[-EDGE:]
        state_before[...] = state_halo.astype(f32)[-EDGE:]
        held[...] = jnp.zeros(held.shape, f32)
        total[...] = jnp.zeros(total.shape, f32)

    value = value_ref[...].astype(f32)
    state = state_ref[...].astype(f32)
    pre = convolve(value_before[...], value, value_k[...].astype(f32))
    spre = convolve(state_before[...], state, state_k[...].astype(f32))
    value_before[...] = value[-EDGE:]
    state_before[...] = state[-EDGE:]
    conv = pre * sig(pre)
    mixed_rows = spre * sig(spre)
    pre_out[...] = pre
    spre_out[...] = spre
    conv_out[...] = conv
    rows_out[...] = mixed_rows

    dt = jax.nn.softplus(step_ref[...] + padded(bias_ref[...]))
    decay = -dt * jnp.exp(padded(log_ref[...]))
    size = value.shape[0]
    lower = (iota((size, size), 0) >= iota((size, size), 1)).astype(f32).astype(bf16)
    cum = exact_dot(lower, decay, NN)
    dt_out[...] = dt
    cum_out[...] = cum
    cumt_out[...] = cum.T[: cumt_out.shape[0]]

    heads = head_map(width)
    cum_wide = spread(cum, heads)
    last = cum_wide[size - 1 : size]
    weighted = conv * spread(dt, heads) * jnp.exp(last - cum_wide)
    held_out[0] = held[...]
    new = jnp.exp(last) * held[...] + dot3(mixed_rows[:, :LANES], weighted, TN)
    held[...] = new
    total[...] = total[...] + last

    @pl.when(b == pl.num_programs(0) - 1)
    def _():
        message_out[:LANES] = new
        message_out[LANES:] = total[...]


def local_states(value_in, state_in, step_raw, halo, pre_gain, input_weight, state_weight, input_kernel, state_kernel, step_bias, decay_log):
    tokens, inner = value_in.shape
    state2 = state_in.shape[1]
    state = state2 // 2
    blocks = tokens // BLOCK
    headrows = 16
    return pl.pallas_call(
        local_kernel,
        grid=(blocks,),
        in_specs=[
            rows(BLOCK, inner),
            rows(BLOCK, state2),
            rows(BLOCK, LANES),
            whole(halo.shape),
            whole(pre_gain.shape),
            whole(input_weight.shape),
            whole(state_weight.shape),
            whole(input_kernel.shape),
            whole(state_kernel.shape),
            whole(step_bias.shape),
            whole(decay_log.shape),
        ],
        out_specs=[
            rows(BLOCK, inner),
            rows(BLOCK, inner),
            rows(BLOCK, state2),
            rows(BLOCK, state2),
            rows(BLOCK, LANES),
            rows(BLOCK, LANES),
            pl.BlockSpec((headrows, BLOCK), lambda b: (0, b)),
            pl.BlockSpec((1, state, inner), lambda b: (b, 0, 0)),
            whole((state + EDGE, inner)),
            whole((halo.shape[0], inner)),
            whole((halo.shape[0], state2)),
        ],
        out_shape=[
            jax.ShapeDtypeStruct((tokens, inner), f32),
            jax.ShapeDtypeStruct((tokens, inner), f32),
            jax.ShapeDtypeStruct((tokens, state2), f32),
            jax.ShapeDtypeStruct((tokens, state2), f32),
            jax.ShapeDtypeStruct((tokens, LANES), f32),
            jax.ShapeDtypeStruct((tokens, LANES), f32),
            jax.ShapeDtypeStruct((headrows, tokens), f32),
            jax.ShapeDtypeStruct((blocks, state, inner), f32),
            jax.ShapeDtypeStruct((state + EDGE, inner), f32),
            jax.ShapeDtypeStruct((halo.shape[0], inner), bf16),
            jax.ShapeDtypeStruct((halo.shape[0], state2), bf16),
        ],
        scratch_shapes=[
            pltpu.VMEM((EDGE, inner), f32),
            pltpu.VMEM((EDGE, state2), f32),
            pltpu.VMEM((state, inner), f32),
            pltpu.VMEM((EDGE, inner), f32),
        ],
        compiler_params=params(),
        cost_estimate=pl.CostEstimate(flops=2 * tokens * inner * 1500, bytes_accessed=tokens * inner * 14, transcendentals=tokens * inner * 2),
    )(value_in, state_in, step_raw, halo, pre_gain, input_weight, state_weight, input_kernel, state_kernel, step_bias, decay_log)


def pairs_of(heads_count):
    return heads_count * HEAD_DIM // LANES


def inner_kernel(heads_count, conv_ref, dt_ref, rows_ref, cum_ref, cumt_ref, out_ref):
    size, width = conv_ref.shape
    heads = head_map(width)
    driven = conv_ref[...] * spread(dt_ref[...], heads)
    high, low = split2(driven)
    scores = dot3(rows_ref[:, LANES:], rows_ref[:, :LANES], NT)
    causal = iota((size, size), 0) >= iota((size, size), 1)
    left = iota((size, LANES), 1) < HEAD_DIM
    cum = cum_ref[...]
    cumt = cumt_ref[...]
    for pair in range(pairs_of(heads_count)):
        span = slice(pair * LANES, (pair + 1) * LANES)
        across = jnp.concatenate([high[:, span], low[:, span]], axis=1)
        right_side = jnp.concatenate([across, across], axis=0)
        mixes = []
        for h in (2 * pair, 2 * pair + 1):
            gap = cum[:, h : h + 1] - cumt[h : h + 1, :]
            mix = jnp.exp(jnp.where(causal, gap, -1e30)) * scores
            mixes.append(jnp.concatenate(split2(mix), axis=1))
        both = dot(jnp.concatenate(mixes, axis=0), right_side)
        both = both[:, :LANES] + both[:, LANES:]
        out_ref[:, span] = jnp.where(left, both[:size], both[size:])


def inner_forward(heads_count, conv, dt, state_rows, cum, cumt):
    tokens, inner = conv.shape
    return pl.pallas_call(
        functools.partial(inner_kernel, heads_count),
        grid=(tokens // BLOCK,),
        in_specs=[
            rows(BLOCK, inner),
            rows(BLOCK, LANES),
            rows(BLOCK, state_rows.shape[1]),
            rows(BLOCK, LANES),
            pl.BlockSpec((cumt.shape[0], BLOCK), lambda b: (0, b)),
        ],
        out_specs=rows(BLOCK, inner),
        out_shape=jax.ShapeDtypeStruct((tokens, inner), f32),
        compiler_params=params(),
        cost_estimate=pl.CostEstimate(flops=2 * tokens * inner * 2000, bytes_accessed=tokens * inner * 8, transcendentals=tokens * BLOCK * heads_count),
    )(conv, dt, state_rows, cum, cumt)


def combine_kernel(
    count, intra_ref, conv_ref, rows_ref, cum_ref, held_ref, own_ref, *refs
):
    message_refs, (gate_ref, grad_ref, gain_ref, skip_ref, mixed_out, sums_out, held_out, end_out, start, total) = refs[:count], refs[count:]
    b = pl.program_id(0)
    size, width = conv_ref.shape
    state = held_ref.shape[1]

    @pl.when(b == 0)
    def _():
        entering = jnp.zeros((state, width), f32)
        passed = jnp.zeros((EDGE, width), f32)
        for ref in message_refs:
            entering = entering + jnp.exp(passed[0:1]) * ref[:state]
            passed = passed + ref[state:]
        start[...] = entering
        total[...] = jnp.zeros(total.shape, f32)
        end_out[...] = own_ref[:state] + jnp.exp(own_ref[state : state + 1]) * entering

    heads = head_map(width)
    cum_wide = spread(cum_ref[...], heads)
    held = held_ref[0] + jnp.exp(total[0:1]) * start[...]
    held_out[0] = held
    total[...] = total[...] + cum_wide[size - 1 : size]
    skip = spread(jnp.broadcast_to(padded(skip_ref[...]), (EDGE, LANES)), heads)[0:1]
    carried = jnp.exp(cum_wide) * dot3(rows_ref[:, LANES:], held)
    mixed = (intra_ref[...] + carried) + skip * conv_ref[...]
    mixed_out[...] = mixed
    gate = gate_ref[...]
    gated = mixed * (gate * sig(gate))
    ones = jnp.ones((EDGE, width), bf16)
    square = exact_dot(ones, gated * gated, NT)
    inner = exact_dot(ones, grad_ref[...] * gain_ref[...] * gated, NT)
    sums_out[...] = jnp.where(iota(square.shape, 0) == 0, square, inner)


def combine(intra, conv, state_rows, cum, held, own, messages, gate_in, grad_normed, norm_gain, skip_gain):
    tokens, inner = conv.shape
    blocks, state, _ = held.shape
    state_block = pl.BlockSpec((1, state, inner), lambda b: (b, 0, 0))
    return pl.pallas_call(
        functools.partial(combine_kernel, len(messages)),
        grid=(blocks,),
        in_specs=[
            rows(BLOCK, inner),
            rows(BLOCK, inner),
            rows(BLOCK, state_rows.shape[1]),
            rows(BLOCK, LANES),
            state_block,
            whole(own.shape),
            *[whole(own.shape) for _ in messages],
            rows(BLOCK, inner),
            rows(BLOCK, inner),
            whole(norm_gain.shape),
            whole(skip_gain.shape),
        ],
        out_specs=[
            rows(BLOCK, inner),
            pl.BlockSpec((EDGE, BLOCK), lambda b: (0, b)),
            state_block,
            whole((state, inner)),
        ],
        out_shape=[
            jax.ShapeDtypeStruct((tokens, inner), f32),
            jax.ShapeDtypeStruct((EDGE, tokens), f32),
            jax.ShapeDtypeStruct(held.shape, f32),
            jax.ShapeDtypeStruct((state, inner), f32),
        ],
        scratch_shapes=[pltpu.VMEM((state, inner), f32), pltpu.VMEM((EDGE, inner), f32)],
        compiler_params=params(),
        cost_estimate=pl.CostEstimate(flops=2 * tokens * inner * 1000, bytes_accessed=tokens * inner * 28, transcendentals=tokens * inner * 2),
    )(intra, conv, state_rows, cum, held, own, *messages, gate_in, grad_normed, norm_gain, skip_gain)


def column(row, width):
    return jnp.concatenate([jnp.broadcast_to(row, (LANES, row.shape[1])).T] * (width // LANES), axis=1)


def gate_back_kernel(count, inner_total, mixed_ref, gate_ref, grad_ref, rows_ref, cum_ref, gain_ref, *refs):
    sums_refs, (normed_out, gate_out, dmix_out, later_out, message_out, gain_out, later, total) = refs[:count], refs[count:]
    b = pl.program_id(0)
    size, width = mixed_ref.shape

    @pl.when(b == 0)
    def _():
        later[...] = jnp.zeros(later.shape, f32)
        total[...] = jnp.zeros(total.shape, f32)
        gain_out[...] = jnp.zeros(gain_out.shape, f32)

    sums = sums_refs[0][...]
    for ref in sums_refs[1:]:
        sums = sums + ref[...]
    rms_row = lax.rsqrt(sums[0:1] / inner_total + epsilon)
    pull_row = rms_row * rms_row * rms_row * sums[1:2] / inner_total
    rms = column(rms_row, width)
    pull = column(pull_row, width)
    gain = gain_ref[...]
    gate = gate_ref[...]
    mixed = mixed_ref[...]
    grad = grad_ref[...]
    gate_sig = sig(gate)
    gate_silu = gate * gate_sig
    gated = mixed * gate_silu
    normed_out[...] = (gated * rms * gain).astype(bf16)
    gain_part = (grad * gated * rms).reshape(size // EDGE, EDGE, width)
    gain_out[...] = gain_out[...] + jnp.sum(gain_part, axis=0)
    grad_gated = rms * gain * grad - gated * pull
    gate_out[...] = (grad_gated * mixed * gate_sig * (1.0 + gate * (1.0 - gate_sig))).astype(bf16)
    grad_mixed = grad_gated * gate_silu
    dmix_out[...] = grad_mixed

    cum_wide = spread(cum_ref[...], head_map(width))
    last = cum_wide[size - 1 : size]
    later_out[0] = later[...]
    new = jnp.exp(last) * later[...] + dot3(rows_ref[:, LANES:], jnp.exp(cum_wide) * grad_mixed, TN)
    later[...] = new
    total[...] = total[...] + last

    @pl.when(b == pl.num_programs(0) - 1)
    def _():
        message_out[:LANES] = new
        message_out[LANES:] = total[...]


def gate_back(mixed, gate_in, grad_normed, state_rows, cum, norm_gain, sums, inner_total):
    tokens, inner = mixed.shape
    blocks = tokens // BLOCK
    state = state_rows.shape[1] // 2
    return pl.pallas_call(
        functools.partial(gate_back_kernel, len(sums), inner_total),
        grid=(blocks,),
        in_specs=[
            rows(BLOCK, inner, blocks),
            rows(BLOCK, inner, blocks),
            rows(BLOCK, inner, blocks),
            rows(BLOCK, 2 * state, blocks),
            rows(BLOCK, LANES, blocks),
            whole(norm_gain.shape),
            *[pl.BlockSpec((EDGE, BLOCK), lambda b: (0, blocks - 1 - b)) for _ in sums],
        ],
        out_specs=[
            rows(BLOCK, inner, blocks),
            rows(BLOCK, inner, blocks),
            rows(BLOCK, inner, blocks),
            pl.BlockSpec((1, state, inner), lambda b: (blocks - 1 - b, 0, 0)),
            whole((state + EDGE, inner)),
            whole((EDGE, inner)),
        ],
        out_shape=[
            jax.ShapeDtypeStruct((tokens, inner), bf16),
            jax.ShapeDtypeStruct((tokens, inner), bf16),
            jax.ShapeDtypeStruct((tokens, inner), f32),
            jax.ShapeDtypeStruct((blocks, state, inner), f32),
            jax.ShapeDtypeStruct((state + EDGE, inner), f32),
            jax.ShapeDtypeStruct((EDGE, inner), f32),
        ],
        scratch_shapes=[pltpu.VMEM((state, inner), f32), pltpu.VMEM((EDGE, inner), f32)],
        compiler_params=params(),
        cost_estimate=pl.CostEstimate(flops=2 * tokens * inner * 1000, bytes_accessed=tokens * inner * 26, transcendentals=tokens * inner * 2),
    )(mixed, gate_in, grad_normed, state_rows, cum, norm_gain, *sums)


def inner_back_kernel(heads_count, conv_ref, dt_ref, rows_ref, cum_ref, cumt_ref, dmix_ref, driven_out, rows_out):
    size, width = conv_ref.shape
    heads = head_map(width)
    driven = conv_ref[...] * spread(dt_ref[...], heads)
    dmix_high, dmix_low = split2(dmix_ref[...])
    b_rows = rows_ref[:, :LANES]
    c_rows = rows_ref[:, LANES:]
    scores = dot3(b_rows, c_rows, NT)
    causal = iota((size, size), 1) >= iota((size, size), 0)
    left = iota((size, LANES), 1) < HEAD_DIM
    cum = cum_ref[...]
    cumt = cumt_ref[...]
    score_grad = jnp.zeros((size, size), f32)
    for pair in range(pairs_of(heads_count)):
        span = slice(pair * LANES, (pair + 1) * LANES)
        across = jnp.concatenate([dmix_high[:, span], dmix_low[:, span]], axis=1)
        right_side = jnp.concatenate([across, across], axis=0)
        taking = jnp.concatenate([dmix_high[:, span], dmix_high[:, span], dmix_low[:, span]], axis=1)
        mixes = []
        for h in (2 * pair, 2 * pair + 1):
            mine = left if h % 2 == 0 else jnp.logical_not(left)
            own_high, own_low = split2(jnp.where(mine, driven[:, span], 0.0))
            mix_grad = dot(jnp.concatenate([own_high, own_low, own_high], axis=1), taking, NT)
            gap = cumt[h : h + 1, :] - cum[:, h : h + 1]
            kept = jnp.exp(jnp.where(causal, gap, -1e30))
            score_grad = score_grad + mix_grad * kept
            mixes.append(jnp.concatenate(split2(kept * scores), axis=1))
        both = dot(jnp.concatenate(mixes, axis=0), right_side)
        both = both[:, :LANES] + both[:, LANES:]
        driven_out[:, span] = jnp.where(left, both[:size], both[size:])
    rows_out[:, :LANES] = dot3(score_grad, c_rows, NN)
    rows_out[:, LANES:] = dot3(score_grad, b_rows, TN)


def inner_back(heads_count, conv, dt, state_rows, cum, cumt, grad_mixed):
    tokens, inner = conv.shape
    return pl.pallas_call(
        functools.partial(inner_back_kernel, heads_count),
        grid=(tokens // BLOCK,),
        in_specs=[
            rows(BLOCK, inner),
            rows(BLOCK, LANES),
            rows(BLOCK, state_rows.shape[1]),
            rows(BLOCK, LANES),
            pl.BlockSpec((cumt.shape[0], BLOCK), lambda b: (0, b)),
            rows(BLOCK, inner),
        ],
        out_specs=[rows(BLOCK, inner), rows(BLOCK, state_rows.shape[1])],
        out_shape=[
            jax.ShapeDtypeStruct((tokens, inner), f32),
            jax.ShapeDtypeStruct(state_rows.shape, f32),
        ],
        compiler_params=params(),
        cost_estimate=pl.CostEstimate(flops=2 * tokens * inner * 3000, bytes_accessed=tokens * inner * 12, transcendentals=tokens * BLOCK * heads_count),
    )(conv, dt, state_rows, cum, cumt, grad_mixed)


def finish_kernel(
    count, driven_ref, drows_ref, dmix_ref, mixed_ref, conv_ref, pre_ref, value_ref, dt_ref, cum_ref, step_ref, rows_ref,
    held_ref, end_ref, later_ref, *refs
):
    message_refs = refs[:count]
    (
        vhalo_ref, kernel_ref, skip_ref, bias_ref, log_ref,
        grad_value_out, grad_rows_out, grad_step_out, last_out, first_out, kernel_out, small_out,
        entering, total, held_next, pre_next, skip_sum,
    ) = refs[count:]
    b = pl.program_id(0)
    size, width = conv_ref.shape
    state = held_ref.shape[1]
    heads = head_map(width)

    @pl.when(b == 0)
    def _():
        coming = jnp.zeros((state, width), f32)
        passed = jnp.zeros((EDGE, width), f32)
        for ref in message_refs:
            coming = coming + jnp.exp(passed[0:1]) * ref[:state]
            passed = passed + ref[state:]
        entering[...] = coming
        total[...] = jnp.zeros(total.shape, f32)
        held_next[...] = end_ref[...]
        pre_next[...] = jnp.zeros(pre_next.shape, f32)
        kernel_out[...] = jnp.zeros(kernel_out.shape, f32)
        small_out[...] = jnp.zeros(small_out.shape, f32)
        skip_sum[...] = jnp.zeros(skip_sum.shape, f32)

    b_rows = rows_ref[:, :LANES]
    cum_wide = spread(cum_ref[...], heads)
    last = cum_wide[size - 1 : size]
    dt = dt_ref[...]
    dt_wide = spread(dt, heads)
    conv = conv_ref[...]
    dmix = dmix_ref[...]
    driven = conv * dt_wide
    later = later_ref[0] + jnp.exp(total[0:1]) * entering[...]
    total[...] = total[...] + last
    tail = jnp.exp(last - cum_wide)
    ddriven = driven_ref[...] + tail * dot3(b_rows, later)
    held = held_ref[0]
    grad_rows_out[:, :LANES] = drows_ref[:, :LANES] + dot3(tail * driven, later, NT)
    grad_rows_out[:, LANES:] = drows_ref[:, LANES:] + dot3(jnp.exp(cum_wide) * dmix, held, NT)

    skip = spread(jnp.broadcast_to(padded(skip_ref[...]), (EDGE, LANES)), heads)[0:1]
    from_skip = dmix * conv
    skip_sum[...] = skip_sum[...] + jnp.sum(from_skip.reshape(size // EDGE, EDGE, width), axis=0)
    level = gather_heads(dmix * (mixed_ref[...] - skip * conv) - driven * ddriven, heads)
    through = gather_heads(ddriven * conv, heads)
    boundary = jnp.sum((later * held_next[...]).reshape(state // EDGE, EDGE, width), axis=0)
    boundary = jnp.sum(gather_heads(boundary, heads), axis=0, keepdims=True)
    held_next[...] = held
    upper = (iota((size, size), 1) >= iota((size, size), 0)).astype(f32).astype(bf16)
    ddecay = exact_dot(upper, level, NN) + boundary
    rate = jnp.exp(padded(log_ref[...]))
    dstep = (through - ddecay * rate) * sig(step_ref[...] + padded(bias_ref[...]))
    grad_step_out[...] = dstep[:, : grad_step_out.shape[1]].astype(bf16)
    dlog = jnp.sum(-ddecay * dt * rate, axis=0, keepdims=True)
    small_out[1:2] = small_out[1:2] + jnp.sum(dstep, axis=0, keepdims=True)
    small_out[2:3] = small_out[2:3] + dlog

    pre = pre_ref[...]
    pre_sig = sig(pre)
    dpre = (ddriven * dt_wide + skip * dmix) * (pre_sig * (1.0 + pre * (1.0 - pre_sig)))
    extended = jnp.concatenate([dpre, pre_next[...]], axis=0)
    value = value_ref[...].astype(f32)
    taps = kernel_ref[...].astype(f32)
    dvalue = jnp.zeros((size, width), f32)
    for k in range(CONV):
        shifted = extended[CONV - 1 - k : CONV - 1 - k + size]
        dvalue = dvalue + taps[k : k + 1] * shifted
        kernel_out[k : k + 1] = kernel_out[k : k + 1] + jnp.sum(value * shifted, axis=0, keepdims=True)
    grad_value_out[...] = dvalue.astype(bf16)
    pre_next[...] = dpre[:EDGE]

    @pl.when(b == 0)
    def _():
        last_out[...] = dvalue[-2 * EDGE :]

    @pl.when(b == pl.num_programs(0) - 1)
    def _():
        first_out[...] = dpre[:EDGE]
        ahead = jnp.concatenate([jnp.zeros((EDGE, width), f32), dpre[:EDGE]], axis=0)
        halo = vhalo_ref[...].astype(f32)[-EDGE:]
        for k in range(CONV):
            shifted = ahead[CONV - 1 - k : CONV - 1 - k + EDGE]
            kernel_out[k : k + 1] = kernel_out[k : k + 1] + jnp.sum(halo * shifted, axis=0, keepdims=True)
        small_out[0:1] = jnp.sum(gather_heads(skip_sum[...], heads), axis=0, keepdims=True)


def finish(grad_driven, grad_rows, grad_mixed, mixed, conv, pre, value_in, dt, cum, step_raw, state_rows, held, end_state, later,
           messages, vhalo, input_kernel, skip_gain, step_bias, decay_log):
    tokens, inner = conv.shape
    blocks, state, _ = held.shape
    head_count = skip_gain.shape[1]
    state_block = pl.BlockSpec((1, state, inner), lambda b: (blocks - 1 - b, 0, 0))
    wide = rows(BLOCK, inner, blocks)
    narrow = rows(BLOCK, LANES, blocks)
    return pl.pallas_call(
        functools.partial(finish_kernel, len(messages)),
        grid=(blocks,),
        in_specs=[
            wide, rows(BLOCK, 2 * state, blocks), wide, wide, wide, wide, wide, narrow, narrow, narrow,
            rows(BLOCK, 2 * state, blocks),
            state_block, whole(end_state.shape), state_block,
            *[whole(m.shape) for m in messages],
            whole(vhalo.shape), whole(input_kernel.shape), whole(skip_gain.shape), whole(step_bias.shape), whole(decay_log.shape),
        ],
        out_specs=[
            wide,
            rows(BLOCK, 2 * state, blocks),
            rows(BLOCK, head_count, blocks),
            whole((2 * EDGE, inner)),
            whole((EDGE, inner)),
            whole((EDGE, inner)),
            whole((EDGE, LANES)),
        ],
        out_shape=[
            jax.ShapeDtypeStruct((tokens, inner), bf16),
            jax.ShapeDtypeStruct((tokens, 2 * state), f32),
            jax.ShapeDtypeStruct((tokens, head_count), bf16),
            jax.ShapeDtypeStruct((2 * EDGE, inner), f32),
            jax.ShapeDtypeStruct((EDGE, inner), f32),
            jax.ShapeDtypeStruct((EDGE, inner), f32),
            jax.ShapeDtypeStruct((EDGE, LANES), f32),
        ],
        scratch_shapes=[
            pltpu.VMEM((state, inner), f32),
            pltpu.VMEM((EDGE, inner), f32),
            pltpu.VMEM((state, inner), f32),
            pltpu.VMEM((EDGE, inner), f32),
            pltpu.VMEM((EDGE, inner), f32),
        ],
        compiler_params=params(),
        cost_estimate=pl.CostEstimate(flops=2 * tokens * inner * 3000, bytes_accessed=tokens * inner * 36, transcendentals=tokens * inner * 3),
    )(grad_driven, grad_rows, grad_mixed, mixed, conv, pre, value_in, dt, cum, step_raw, state_rows, held, end_state, later,
      *messages, vhalo, input_kernel, skip_gain, step_bias, decay_log)


def from_before(value, axis, by=1):
    count = lax.axis_size(axis)
    return lax.ppermute(value, axis, [(i, i + by) for i in range(count - by)])


def from_after(value, axis, by=1):
    count = lax.axis_size(axis)
    return lax.ppermute(value, axis, [(i + by, i) for i in range(count - by)])


def from_all(value, axis):
    count = lax.axis_size(axis)
    return [lax.ppermute(value, axis, [(i, (i + by) % count) for i in range(count)]) for by in range(1, count)]


def swapped(value, axis, flip):
    return lax.ppermute(value, axis, [(i, i ^ flip) for i in range(lax.axis_size(axis))])


def own_part(array, axis_name, dim):
    size = array.shape[dim] // lax.axis_size(axis_name)
    return lax.dynamic_slice_in_dim(array, lax.axis_index(axis_name) * size, size, dim)


def input_kernel_body(pieces, gate_ref, value_ref, step_ref, fixed_ref, x_ref, gain_ref, gate_w, value_w, step_w, out_ref, row_out, col_out):
    b = pl.program_id(0)
    size = x_ref.shape[0]

    @pl.when(b == 0)
    def _():
        col_out[...] = jnp.zeros(col_out.shape, f32)

    gate = gate_ref[...]
    value = value_ref[...]
    edge = fixed_ref.shape[0]
    patched = jnp.concatenate([value[: size - edge], fixed_ref[...]], axis=0)
    value = jnp.where(b == pl.num_programs(0) - 1, patched, value)
    step = step_ref[...]
    x = x_ref[...].astype(f32)
    scaling = lax.rsqrt(jnp.mean(x * x, axis=-1, keepdims=True) + epsilon)
    part = x.shape[1] // pieces
    row = jnp.zeros((size, LANES), f32)
    for j in range(pieces):
        span = slice(j * part, (j + 1) * part)
        partial = dot(gate, gate_w[span, :], NT) + dot(value, value_w[span, :], NT) + dot(step, step_w[span, :], NT)
        out_ref[j] = partial
        pulled = partial * x[:, span]
        gained = pulled * gain_ref[:, span]
        for i in range(part // LANES):
            row = row + gained[:, i * LANES : (i + 1) * LANES]
        col_out[:, span] = col_out[:, span] + jnp.sum((pulled * scaling).reshape(size // EDGE, EDGE, part), axis=0)
    row_out[...] = exact_dot(jnp.ones((EDGE, LANES), bf16), row, NT)


def input_partials(pieces, grad_gate, grad_value, grad_step, fixed, residual, pre_gain, gate_weight, input_weight, step_weight):
    tokens, width = residual.shape
    inner = grad_gate.shape[1]
    part = width // pieces
    tile = min(tokens, 256)
    return pl.pallas_call(
        functools.partial(input_kernel_body, pieces),
        grid=(tokens // tile,),
        in_specs=[
            rows(tile, inner),
            rows(tile, inner),
            rows(tile, grad_step.shape[1]),
            whole(fixed.shape),
            rows(tile, width),
            whole(pre_gain.shape),
            whole(gate_weight.shape),
            whole(input_weight.shape),
            whole(step_weight.shape),
        ],
        out_specs=[
            pl.BlockSpec((pieces, tile, part), lambda b: (0, b, 0)),
            pl.BlockSpec((EDGE, tile), lambda b: (0, b)),
            whole((EDGE, width)),
        ],
        out_shape=[
            jax.ShapeDtypeStruct((pieces, tokens, part), f32),
            jax.ShapeDtypeStruct((EDGE, tokens), f32),
            jax.ShapeDtypeStruct((EDGE, width), f32),
        ],
        compiler_params=params(),
        cost_estimate=pl.CostEstimate(flops=4 * tokens * width * inner, bytes_accessed=tokens * width * 10, transcendentals=0),
    )(grad_gate, grad_value, grad_step, fixed, residual, pre_gain, gate_weight, input_weight, step_weight)


def line_sum(parts, axis):
    count = lax.axis_size(axis)
    place = lax.axis_index(axis)

    def part(k):
        return lax.dynamic_index_in_dim(parts, jnp.clip(k, 0, count - 1), 0, False)

    up = down = 0.0
    for s in range(1, count):
        up = (part(count - s + place) + up).astype(bf16)
        down = (part(s - count + place) + down).astype(bf16)
        up = lax.ppermute(up, axis, [(k, k + 1) for k in range(s)]).astype(f32)
        down = lax.ppermute(down, axis, [(count - 1 - k, count - 2 - k) for k in range(s)]).astype(f32)
    return part(place) + up + down


def state_kernel_body(pieces_count, *refs):
    grads = refs[:pieces_count]
    spre_ref, after_ref, input_ref, halo_ref, taps_ref, w_ref, x_ref, gain_ref, out_ref, taps_out, row_out, col_out = refs[pieces_count:]
    tokens = input_ref.shape[0]
    total = grads[0][...]
    for ref in grads[1:]:
        total = total + ref[...]
    pre = jnp.concatenate([spre_ref[...], after_ref[...]], axis=0)
    s = sig(pre)
    through = total * (s * (1.0 + pre * (1.0 - s)))
    taps = taps_ref[...].astype(f32)
    grad = jnp.zeros((tokens, pre.shape[1]), f32)
    extended = jnp.concatenate([halo_ref[...].astype(f32)[-EDGE:], input_ref[...].astype(f32)], axis=0)
    own = through[:tokens]
    first = EDGE - CONV + 1
    taps_out[...] = jnp.zeros(taps_out.shape, f32)
    for k in range(CONV):
        grad = grad + taps[k : k + 1] * through[CONV - 1 - k : CONV - 1 - k + tokens]
        taps_out[k : k + 1] = jnp.sum(own * extended[first + k : first + k + tokens], axis=0, keepdims=True)
    rounded = grad.astype(bf16)
    out_ref[...] = rounded
    col = jnp.zeros((EDGE, x_ref.shape[1]), f32)
    tile = min(tokens, 256)
    for r in range(tokens // tile):
        span = slice(r * tile, (r + 1) * tile)
        x = x_ref[span].astype(f32)
        scaling = lax.rsqrt(jnp.mean(x * x, axis=-1, keepdims=True) + epsilon)
        pulled = dot(rounded[span], w_ref[...], NT) * x
        gained = pulled * gain_ref[...]
        row = jnp.zeros((tile, LANES), f32)
        for i in range(x.shape[1] // LANES):
            row = row + gained[:, i * LANES : (i + 1) * LANES]
        col = col + jnp.sum((pulled * scaling).reshape(tile // EDGE, EDGE, x.shape[1]), axis=0)
        row_out[:, span] = exact_dot(jnp.ones((EDGE, LANES), bf16), row, NT)
    col_out[...] = col


def state_back(grads, spre, spre_after, state_in, halo, taps, weight, residual, pre_gain):
    tokens, part = state_in.shape
    width = residual.shape[1]
    return pl.pallas_call(
        functools.partial(state_kernel_body, len(grads)),
        out_shape=[
            jax.ShapeDtypeStruct((tokens, part), bf16),
            jax.ShapeDtypeStruct((EDGE, part), f32),
            jax.ShapeDtypeStruct((EDGE, tokens), f32),
            jax.ShapeDtypeStruct((EDGE, width), f32),
        ],
        compiler_params=pltpu.CompilerParams(vmem_limit_bytes=56 * 1024 * 1024),
        cost_estimate=pl.CostEstimate(flops=2 * tokens * width * part, bytes_accessed=tokens * width * 4, transcendentals=tokens * part),
    )(*grads, spre, spre_after, state_in, halo, taps, weight, residual, pre_gain)


def tile_products(plan, left, right, tiles, left_map, right_map, shape, adds=()):
    tokens = left[0].shape[0]
    in_specs = []
    operands = []
    for i in range(len(left)):
        in_specs.append(pl.BlockSpec((tokens, shape[0]), functools.partial(left_map, i)))
        in_specs.append(pl.BlockSpec((tokens, shape[1]), functools.partial(right_map, i)))
        operands += [left[i], right[i]]
    fixed = pl.BlockSpec(shape, lambda j, plan: (0, 0))
    in_specs += [fixed for _ in adds]

    def body(plan_ref, *refs):
        pairs = refs[: 2 * len(left)]
        add_refs = refs[2 * len(left) : 2 * len(left) + len(adds)]
        outs = refs[2 * len(left) + len(adds) :]
        j = pl.program_id(0)
        for i in range(len(left)):

            @pl.when(plan_ref[0] == i)
            def _(i=i):
                total = dot(pairs[2 * i][...], pairs[2 * i + 1][...], TN)
                for k in range(tiles):

                    @pl.when(j == k)
                    def _(k=k):
                        outs[k][...] = total + add_refs[k][...] if adds else total

    return pl.pallas_call(
        body,
        grid_spec=pltpu.PrefetchScalarGridSpec(
            num_scalar_prefetch=1,
            grid=(tiles,),
            in_specs=in_specs,
            out_specs=[fixed for _ in range(tiles)],
        ),
        out_shape=[jax.ShapeDtypeStruct(shape, f32) for _ in range(tiles)],
        compiler_params=params(),
        cost_estimate=pl.CostEstimate(
            flops=2 * tokens * tiles * shape[0] * shape[1], bytes_accessed=tiles * (2 * tokens * (shape[0] + shape[1]) + 4 * shape[0] * shape[1]), transcendentals=0
        ),
    )(plan, *operands, *adds)


def reduce_tiles(kept):
    place = lax.axis_index("ctx")
    lower, higher = place % 2, place // 2
    chunks = []
    arrived = [swapped(kept[1], "ctx", 1), swapped(kept[3], "ctx", 2)]
    for own, got, bit, flip in ((kept[0], arrived[0], higher, 2), (kept[2], arrived[1], lower, 1)):
        half = own.shape[0] // 2
        take = lambda a, at: lax.dynamic_slice_in_dim(a, at * half, half, 0)
        away = take(own, 1 - bit) + take(got, 1 - bit)
        stay = take(own, bit) + take(got, bit)
        chunks.append(stay + swapped(away, "ctx", flip))
    total = jnp.concatenate(chunks, axis=0)
    step = 2
    while step < lax.axis_size("dp"):
        total = total + swapped(total, "dp", step)
        step *= 2
    return total.astype(bf16)


def spread_chunks(chunk):
    here = jnp.concatenate([chunk, *[swapped(chunk, "ctx", k) for k in range(1, lax.axis_size("ctx"))]], axis=0)
    return here, swapped(here, "dp", 1)


def put_together(plan, here, there, shapes, out_map):
    cols = here.shape[1]
    size = here.shape[0] // 8
    merged = len(shapes) == 1

    def body(plan_ref, here_ref, there_ref, *outs):
        a, t = pl.program_id(0), pl.program_id(1)
        side, high, low = t // 4, (t // 2) % 2, t % 2
        lower = jnp.where(side == 0, high, low)
        higher = jnp.where(side == 0, low, high)
        k = jnp.bitwise_xor(higher * 2 + lower, plan_ref[1])
        start = pl.multiple_of(k * (2 * size) + side * size, 16)
        for part in range(2):

            @pl.when(a == part)
            def _(part=part):
                out = outs[0] if merged else outs[part]

                @pl.when(plan_ref[0] == part)
                def _():
                    out[...] = here_ref[pl.ds(start, size)].astype(f32)

                @pl.when(plan_ref[0] != part)
                def _():
                    out[...] = there_ref[pl.ds(start, size)].astype(f32)

    every = pl.BlockSpec(here.shape, lambda a, t, plan: (0, 0))
    return pl.pallas_call(
        body,
        grid_spec=pltpu.PrefetchScalarGridSpec(
            num_scalar_prefetch=1,
            grid=(2, 8),
            in_specs=[every, every],
            out_specs=[pl.BlockSpec((size, cols), functools.partial(out_map, i)) for i in range(len(shapes))],
        ),
        out_shape=[jax.ShapeDtypeStruct(s, f32) for s in shapes],
        compiler_params=pltpu.CompilerParams(dimension_semantics=("arbitrary", "arbitrary"), vmem_limit_bytes=56 * 1024 * 1024),
        cost_estimate=pl.CostEstimate(flops=0, bytes_accessed=here.shape[0] * cols * 12, transcendentals=0),
    )(plan, here, there)


def per_device(residual, pre_gain, gate_weight, input_weight, state_weight, step_weight, input_kernel, state_kernel,
               step_bias, decay_log, skip_gain, norm_gain, out_weight, cotangent):
    residual, cotangent = residual[0], cotangent[0]
    tokens, width = residual.shape
    tensor_size = lax.axis_size("tensor")
    tensor_place = lax.axis_index("tensor")
    ctx_size = lax.axis_size("ctx")
    inner = gate_weight.shape[1]
    inner_total = inner * tensor_size
    head_count = step_weight.shape[1]
    state2 = state_weight.shape[1]
    state_part = state2 // tensor_size
    width_part = width // tensor_size
    row = lambda v: v.reshape(1, -1)
    core = lax.axis_index("dp") % 2
    place = lax.axis_index("ctx")
    lower, higher = place % 2, place // 2
    plan = jnp.stack([core, lower, higher]).astype(jnp.int32)
    other = jnp.stack([1 - core, lower, higher]).astype(jnp.int32)

    halo = from_before(residual[-2 * EDGE :], "ctx")
    normed, gate_in, value_in, state_in, step_raw = project(
        residual, row(pre_gain), gate_weight, input_weight, state_weight, step_weight
    )
    conv, pre, state_rows, spre, dt, cum, cumt, held, message, vhalo, shalo = local_states(
        value_in, state_in, step_raw, halo, row(pre_gain), input_weight, state_weight, input_kernel, state_kernel,
        row(step_bias), row(decay_log)
    )
    messages = [from_before(message, "ctx", by) for by in range(1, ctx_size)]
    intra = inner_forward(head_count, conv, dt, state_rows, cum, cumt)
    grad_normed = dot(cotangent, out_weight, NT)
    mixed, sums, held, end_state = combine(
        intra, conv, state_rows, cum, held, message, messages, gate_in, grad_normed, row(norm_gain), row(skip_gain)
    )
    all_sums = [sums, *from_all(sums, "tensor")]
    normed_out, grad_gate, grad_mixed, later, message, gain_grad = gate_back(
        mixed, gate_in, grad_normed, state_rows, cum, row(norm_gain), all_sums, inner_total
    )
    messages = [from_after(message, "ctx", by) for by in range(1, ctx_size)]

    resid_part = own_part(residual, "tensor", 1).astype(f32)
    partial_out = dot(normed_out, out_weight)
    branch = lax.psum_scatter(partial_out, "tensor", scatter_dimension=1, tiled=True)
    output = (resid_part + branch).astype(bf16)

    tile = width // 4
    half = inner // tile

    def wide_left(i, j, plan):
        tile_at = tile_order(j, plan)
        return (0, jnp.where(plan[0] == i, tile_at if i == 0 else tile_at % half, 0))

    def wide_right(i, j, plan):
        tile_at = tile_order(j, plan)
        return (0, 0 if i == 0 else jnp.where(plan[0] == i, tile_at // half, 0))

    def tile_order(j, plan):
        bit = jnp.where(j < 2, plan[1], plan[2])
        return (j // 2) * 2 + jnp.where(j % 2 == 0, bit, 1 - bit)

    pair = ([normed, normed_out], [grad_gate, cotangent])
    away = tile_products(other, *pair, 4, wide_left, wide_right, (tile, inner))
    away = [swapped(a, "dp", 1) for a in away]

    grad_driven, grad_rows = inner_back(head_count, conv, dt, state_rows, cum, cumt, grad_mixed)
    wide = tile_products(plan, *pair, 4, wide_left, wide_right, (tile, inner), away)
    wide_chunk = reduce_tiles(wide)
    grad_value, grad_rows, grad_step, last_rows, first_rows, kernel_grad, small = finish(
        grad_driven, grad_rows, grad_mixed, mixed, conv, pre, value_in, dt, cum, step_raw, state_rows, held, end_state, later,
        messages, vhalo, input_kernel, row(skip_gain), row(step_bias), row(decay_log)
    )
    ahead = from_after(jnp.concatenate([first_rows, grad_rows[:EDGE], spre[:EDGE]], axis=1), "ctx")
    taps = input_kernel.astype(f32)
    ahead_value = jnp.concatenate([jnp.zeros((2 * EDGE, inner), f32), ahead[:, :inner]], axis=0)
    fixed = last_rows + sum(taps[k : k + 1] * ahead_value[CONV - 1 - k : CONV - 1 - k + 2 * EDGE] for k in range(CONV))
    fixed = fixed.astype(bf16)

    rows_ext = jnp.concatenate([grad_rows, ahead[:, inner : inner + state2]], axis=0)
    span_of = lambda a, k: lax.dynamic_slice_in_dim(a, ((tensor_place + k) % tensor_size) * state_part, state_part, 1)
    arrived = [
        lax.ppermute(span_of(rows_ext, k), "tensor", [(i, (i + k) % tensor_size) for i in range(tensor_size)])
        for k in range(1, tensor_size)
    ]

    parts, row_sums, col_sums = input_partials(
        tensor_size, grad_gate, grad_value, grad_step, fixed, residual, row(pre_gain), gate_weight, input_weight, step_weight
    )
    normed_grad = line_sum(parts, "tensor")

    grad_value = lax.dynamic_update_slice_in_dim(grad_value, fixed, tokens - 2 * EDGE, 0)
    narrow_left = lambda i, j, plan: (0, tile_order(j, plan))
    narrow_right = lambda i, j, plan: (0, plan[3])
    pair = ([normed], [grad_value])
    zero = jnp.zeros((), jnp.int32)
    away = tile_products(jnp.stack([zero, lower, higher, 1 - core]), *pair, 4, narrow_left, narrow_right, (tile, inner // 2))
    away = [swapped(a, "dp", 1) for a in away]
    narrow = tile_products(jnp.stack([zero, lower, higher, core]), *pair, 4, narrow_left, narrow_right, (tile, inner // 2), away)
    narrow_chunk = reduce_tiles(narrow)

    grad_state, taps_grad, state_row, state_col = state_back(
        [span_of(rows_ext, 0), *arrived], span_of(spre, 0), span_of(ahead[:, inner + state2 :], 0), span_of(state_in, 0),
        span_of(shalo, 0), span_of(state_kernel, 0), span_of(state_weight, 0), residual, row(pre_gain)
    )
    col = jnp.sum(col_sums + state_col, axis=0)
    taps_wide = lax.dynamic_update_slice_in_dim(jnp.zeros((CONV, state2), f32), taps_grad[:CONV], tensor_place * state_part, 1)
    lanes = tokens
    count = -(-(width + CONV * state2) // lanes)
    flat = jnp.concatenate([col, taps_wide.reshape(-1), jnp.zeros((count * lanes - width - CONV * state2,), f32)]).reshape(count, lanes)
    packed = jnp.concatenate([row_sums[:1] + state_row[:1], flat], axis=0)
    packed = sum(from_all(packed, "tensor"), packed)
    row_total = packed[0]
    flat = packed[1:].reshape(-1)
    pre_gain_sum = own_part(flat[:width], "tensor", 0)
    taps_sum = flat[width : width + CONV * state2]

    states = [grad_state, *from_all(grad_state, "tensor")]
    weight_part = own_part(state_weight, "tensor", 0)
    span_from = lambda k: lax.dynamic_slice_in_dim(weight_part, ((tensor_place - k) % tensor_size) * state_part, state_part, 1)
    for k in range(tensor_size):
        normed_grad = normed_grad + dot(states[k], span_from(k), NT)

    state_step = jnp.concatenate([dot(normed, grad_state, TN), dot(normed, grad_step, TN)], axis=1)
    pieces = [
        state_step.reshape(-1), kernel_grad[:CONV].reshape(-1), small[:3, :head_count].reshape(-1),
        jnp.sum(gain_grad, axis=0), pre_gain_sum, taps_sum,
    ]
    total = sum(p.shape[0] for p in pieces)
    fill = -total % (EDGE * LANES)
    packed = jnp.concatenate([*pieces, jnp.zeros((fill,), f32)]).reshape(-1, LANES)
    step = 1
    while step < lax.axis_size("dp"):
        packed = packed + swapped(packed, "dp", step)
        step *= 2
    packed = sum([swapped(packed, "ctx", k) for k in range(1, ctx_size)], packed).reshape(-1)
    done = []
    at = 0
    for p in pieces:
        done.append(packed[at : at + p.shape[0]])
        at += p.shape[0]
    state_step = done[0].reshape(width, -1)
    small = done[2].reshape(3, head_count)

    where = jnp.stack([core, place]).astype(jnp.int32)
    gate_weight_grad, out_weight_grad = put_together(
        where, *spread_chunks(wide_chunk), [(width, inner), (inner, width)],
        lambda i, a, t, plan: (jnp.where(a == 0, t, 7), 0) if i == 0 else (jnp.where(a == 1, t % 4, 0), jnp.where(a == 1, t // 4, 0)),
    )
    (input_weight_grad,) = put_together(where, *spread_chunks(narrow_chunk), [(width, inner)], lambda i, a, t, plan: (t, a))

    x = residual.astype(f32)
    scaling = lax.rsqrt(jnp.mean(x * x, axis=-1, keepdims=True) + epsilon)
    grad_part = own_part(cotangent, "tensor", 1).astype(f32)
    input_grad = (
        grad_part + scaling * own_part(pre_gain, "tensor", 0) * normed_grad
        - resid_part * (scaling * scaling * scaling) * row_total[:, None] / width
    )
    return (
        output[None],
        input_grad[None],
        done[4],
        gate_weight_grad,
        input_weight_grad,
        state_step[:, :state_part],
        state_step[:, state_part:],
        done[1].reshape(CONV, inner),
        done[5].reshape(CONV, state2),
        small[1],
        small[2],
        small[0],
        done[3],
        out_weight_grad,
    )


def solution(mesh):
    in_specs = (
        P("dp", "ctx", None),
        P(),
        P(None, "tensor"),
        P(None, "tensor"),
        P(),
        P(None, "tensor"),
        P(None, "tensor"),
        P(),
        P("tensor"),
        P("tensor"),
        P("tensor"),
        P("tensor"),
        P("tensor", None),
        P("dp", "ctx", None),
    )
    out_specs = (
        P("dp", "ctx", "tensor"),
        P("dp", "ctx", "tensor"),
        P("tensor"),
        P(None, "tensor"),
        P(None, "tensor"),
        P(None, "tensor"),
        P(None, "tensor"),
        P(None, "tensor"),
        P(),
        P("tensor"),
        P("tensor"),
        P("tensor"),
        P("tensor"),
        P("tensor", None),
    )
    return jax.shard_map(per_device, mesh=mesh, in_specs=in_specs, out_specs=out_specs, check_vma=False)
```

```python
import functools

import jax
import jax.numpy as jnp
from jax import lax
from jax.experimental import pallas as pl
from jax.experimental.pallas import tpu as pltpu
from jax.sharding import PartitionSpec as P

HEAD_DIM = 64
CONV = 4
EDGE = 8
BLOCK = 128
LANES = 128
epsilon = 1e-05
f32 = jnp.float32
bf16 = jnp.bfloat16

NN = (((1,), (0,)), ((), ()))
NT = (((1,), (1,)), ((), ()))
TN = (((0,), (0,)), ((), ()))


def dot(a, b, dims=NN):
    return lax.dot_general(a, b, dims, preferred_element_type=f32)


def split2(x):
    high = x.astype(bf16)
    return high, (x - high.astype(f32)).astype(bf16)


def split3(x):
    high = x.astype(bf16)
    rest = x - high.astype(f32)
    middle = rest.astype(bf16)
    return high, middle, (rest - middle.astype(f32)).astype(bf16)


def dot3(a, b, dims=NN):
    ah, al = split2(a)
    bh, bl = split2(b)
    return dot(ah, bh, dims) + (dot(ah, bl, dims) + dot(al, bh, dims))


def both_parts(x):
    return jnp.concatenate(split2(x), axis=1)


def fold(product):
    half = product.shape[1] // 2
    return product[:, :half] + product[:, half:]


def wide_dot(parts, x):
    across = both_parts(x)
    return fold(dot(parts, jnp.concatenate([across, across], axis=0)))


def exact_dot(ones, x, dims):
    high, middle, low = split3(x)
    return dot(ones, high, dims) + (dot(ones, middle, dims) + dot(ones, low, dims))


def iota(shape, axis):
    return lax.broadcasted_iota(jnp.int32, shape, axis)


REPEAT = 16


def head_map(width):
    lane = iota((LANES, width), 0)
    mine = (lane % REPEAT == iota((LANES, width), 1) // HEAD_DIM) & (lane < 3 * REPEAT)
    return mine.astype(f32).astype(bf16)


def spread(per_head, heads):
    high = per_head.astype(bf16).astype(f32)
    rest = per_head - high
    middle = rest.astype(bf16).astype(f32)
    group = iota(per_head.shape, 1) // REPEAT
    parts = jnp.where(group == 0, high, jnp.where(group == 1, middle, rest - middle))
    return dot(parts.astype(bf16), heads)


def repeated(row):
    group = jnp.concatenate([row, jnp.zeros((1, REPEAT - row.shape[1]), f32)], axis=1)
    return jnp.concatenate([group] * (LANES // REPEAT), axis=1)


def sig(v):
    return jax.nn.sigmoid(v)


def cost(micros):
    return pl.CostEstimate(flops=micros * 900_000_000, bytes_accessed=micros * 3_000_000, transcendentals=0)


def params(limit=20):
    return pltpu.CompilerParams(
        dimension_semantics=("arbitrary",), vmem_limit_bytes=limit * 1024 * 1024
    )


def whole(shape):
    return pl.BlockSpec(shape, lambda b: (0,) * len(shape))


def rows(size, width, count=0):
    if count:
        return pl.BlockSpec((size, width), lambda b: (count - 1 - b, 0))
    return pl.BlockSpec((size, width), lambda b: (b, 0))


def spans(width):
    return [slice(i * LANES, (i + 1) * LANES) for i in range(width // LANES)]


def by_eights(x):
    return jnp.sum(x.reshape(x.shape[0] // EDGE, EDGE, x.shape[1]), axis=0)


def norm_rows(x, gain):
    scaling = lax.rsqrt(jnp.mean(x * x, axis=-1, keepdims=True) + epsilon)
    return (x * scaling * gain).astype(bf16)


def project_kernel(x_ref, gain_ref, value_ref, state_ref, step_ref, normed_out, value_out, state_out, step_out, step_w):
    @pl.when(pl.program_id(0) == 0)
    def _():
        count = step_ref.shape[0]
        copies = (iota((LANES, count), 0) % REPEAT == iota((LANES, count), 1)).astype(f32).astype(bf16)
        step_w[...] = dot(copies, step_ref[...]).astype(bf16)

    normed = norm_rows(x_ref[...].astype(f32), gain_ref[...])
    normed_out[...] = normed
    value_out[...] = dot(normed, value_ref[...]).astype(bf16)
    state_out[...] = dot(normed, state_ref[...]).astype(bf16)
    step_out[...] = dot(normed, step_w[...], NT)


def project(residual, pre_gain, input_weight, state_weight, step_weight):
    tokens, width = residual.shape
    inner, state2 = input_weight.shape[1], state_weight.shape[1]
    tile = min(tokens, 256)
    return pl.pallas_call(
        project_kernel,
        grid=(tokens // tile,),
        in_specs=[
            rows(tile, width),
            whole((1, width)),
            whole(input_weight.shape),
            whole(state_weight.shape),
            whole(step_weight.shape),
        ],
        out_specs=[rows(tile, width), rows(tile, inner), rows(tile, state2), rows(tile, LANES)],
        out_shape=[
            jax.ShapeDtypeStruct((tokens, width), bf16),
            jax.ShapeDtypeStruct((tokens, inner), bf16),
            jax.ShapeDtypeStruct((tokens, state2), bf16),
            jax.ShapeDtypeStruct((tokens, LANES), f32),
        ],
        scratch_shapes=[pltpu.VMEM((LANES, width), bf16)],
        compiler_params=params(24),
        cost_estimate=cost(6),
    )(residual, pre_gain, input_weight, state_weight, step_weight)


def beside_kernel(normed_ref, gate_w, cot_ref, out_w, gate_out, grad_out):
    gate_out[...] = dot(normed_ref[...], gate_w[...])
    grad_out[...] = dot(cot_ref[...], out_w[...], NT)


def beside(normed, gate_weight, cotangent, out_weight):
    tokens, width = normed.shape
    inner = gate_weight.shape[1]
    tile = min(tokens, 256)
    return pl.pallas_call(
        beside_kernel,
        grid=(tokens // tile,),
        in_specs=[rows(tile, width), whole(gate_weight.shape), rows(tile, width), whole(out_weight.shape)],
        out_specs=[rows(tile, inner), rows(tile, inner)],
        out_shape=[jax.ShapeDtypeStruct((tokens, inner), f32), jax.ShapeDtypeStruct((tokens, inner), f32)],
        compiler_params=params(20),
        cost_estimate=cost(6),
    )(normed, gate_weight, cotangent, out_weight)


def convolve(before, here, kernel):
    extended = jnp.concatenate([before, here], axis=0)
    count = here.shape[0]
    first = EDGE - CONV + 1
    summed = kernel[0:1] * extended[first : first + count]
    for k in range(1, CONV):
        summed = summed + kernel[k : k + 1] * extended[first + k : first + k + count]
    return summed


def local_kernel(
    value_ref, state_ref, step_ref, halo_ref, gain_ref, value_w, state_w, value_k, state_k, bias_ref, log_ref,
    conv_out, pre_out, rows_out, spre_out, dt_out, cum_out, cumt_out, held_out, message_out, vhalo_out, shalo_out,
    value_before, state_before, held, total, heads,
):
    b = pl.program_id(0)
    width = value_ref.shape[1]

    @pl.when(b == 0)
    def _():
        normed = norm_rows(halo_ref[...].astype(f32), gain_ref[...])
        value_halo = dot(normed, value_w[...]).astype(bf16)
        state_halo = dot(normed, state_w[...]).astype(bf16)
        vhalo_out[...] = value_halo
        shalo_out[...] = state_halo
        value_before[...] = value_halo.astype(f32)[-EDGE:]
        state_before[...] = state_halo.astype(f32)[-EDGE:]
        held[...] = jnp.zeros(held.shape, f32)
        total[...] = jnp.zeros(total.shape, f32)
        heads[...] = head_map(width)

    dt = jax.nn.softplus(step_ref[...] + repeated(bias_ref[...]))
    decay = -dt * jnp.exp(repeated(log_ref[...]))
    size = value_ref.shape[0]
    lower = (iota((size, size), 0) >= iota((size, size), 1)).astype(f32).astype(bf16)
    cum = exact_dot(lower, decay, NN)
    dt_out[...] = dt
    cum_out[...] = cum
    cumt_out[...] = cum.T[: cumt_out.shape[0]]
    last = cum[size - 1 : size]
    wide = spread(jnp.concatenate([dt, cum], axis=0), heads[...])

    state = state_ref[...].astype(f32)
    spre = convolve(state_before[...], state, state_k[...].astype(f32))
    state_before[...] = state[-EDGE:]
    mixed_rows = spre * sig(spre)
    spre_out[...] = spre
    rows_out[...] = mixed_rows
    b_parts = both_parts(mixed_rows[:, :LANES].T)

    taps = value_k[...].astype(f32)
    held_out[0] = held[...]
    for span in spans(width):
        value = value_ref[:, span].astype(f32)
        pre = convolve(value_before[:, span], value, taps[:, span])
        value_before[:, span] = value[-EDGE:]
        conv = pre * sig(pre)
        pre_out[:, span] = pre
        conv_out[:, span] = conv
        cum_wide = wide[size:, span]
        end = cum_wide[size - 1 : size]
        weighted = conv * wide[:size, span] * jnp.exp(end - cum_wide)
        held[:, span] = jnp.exp(end) * held[:, span] + wide_dot(b_parts, weighted)
        total[:, span] = total[:, span] + end

    @pl.when(b == pl.num_programs(0) - 1)
    def _():
        message_out[:LANES] = held[...]
        message_out[LANES:] = total[...]


def local_states(value_in, state_in, step_raw, halo, pre_gain, input_weight, state_weight, input_kernel, state_kernel, step_bias, decay_log):
    tokens, inner = value_in.shape
    state2 = state_in.shape[1]
    state = state2 // 2
    blocks = tokens // BLOCK
    headrows = 16
    return pl.pallas_call(
        local_kernel,
        grid=(blocks,),
        in_specs=[
            rows(BLOCK, inner),
            rows(BLOCK, state2),
            rows(BLOCK, LANES),
            whole(halo.shape),
            whole(pre_gain.shape),
            whole(input_weight.shape),
            whole(state_weight.shape),
            whole(input_kernel.shape),
            whole(state_kernel.shape),
            whole(step_bias.shape),
            whole(decay_log.shape),
        ],
        out_specs=[
            rows(BLOCK, inner),
            rows(BLOCK, inner),
            rows(BLOCK, state2),
            rows(BLOCK, state2),
            rows(BLOCK, LANES),
            rows(BLOCK, LANES),
            pl.BlockSpec((headrows, BLOCK), lambda b: (0, b)),
            pl.BlockSpec((1, state, inner), lambda b: (b, 0, 0)),
            whole((state + EDGE, inner)),
            whole((halo.shape[0], inner)),
            whole((halo.shape[0], state2)),
        ],
        out_shape=[
            jax.ShapeDtypeStruct((tokens, inner), f32),
            jax.ShapeDtypeStruct((tokens, inner), f32),
            jax.ShapeDtypeStruct((tokens, state2), f32),
            jax.ShapeDtypeStruct((tokens, state2), f32),
            jax.ShapeDtypeStruct((tokens, LANES), f32),
            jax.ShapeDtypeStruct((tokens, LANES), f32),
            jax.ShapeDtypeStruct((headrows, tokens), f32),
            jax.ShapeDtypeStruct((blocks, state, inner), f32),
            jax.ShapeDtypeStruct((state + EDGE, inner), f32),
            jax.ShapeDtypeStruct((halo.shape[0], inner), bf16),
            jax.ShapeDtypeStruct((halo.shape[0], state2), bf16),
        ],
        scratch_shapes=[
            pltpu.VMEM((EDGE, inner), f32),
            pltpu.VMEM((EDGE, state2), f32),
            pltpu.VMEM((state, inner), f32),
            pltpu.VMEM((EDGE, inner), f32),
            pltpu.VMEM((LANES, inner), bf16),
        ],
        compiler_params=params(),
        cost_estimate=cost(10),
    )(value_in, state_in, step_raw, halo, pre_gain, input_weight, state_weight, input_kernel, state_kernel, step_bias, decay_log)


def inner_kernel(heads_count, conv_ref, dt_ref, rows_ref, cum_ref, cumt_ref, skip_ref, out_ref, heads):
    size, width = conv_ref.shape

    @pl.when(pl.program_id(0) == 0)
    def _():
        heads[...] = head_map(width)

    skip = jnp.broadcast_to(repeated(skip_ref[...]), (EDGE, LANES))
    wide = spread(jnp.concatenate([dt_ref[...], skip], axis=0), heads[...])
    scores = dot3(rows_ref[:, LANES:], rows_ref[:, :LANES], NT)
    causal = iota((size, size), 0) >= iota((size, size), 1)
    left = iota((size, LANES), 1) < HEAD_DIM
    cum = cum_ref[...]
    cumt = cumt_ref[...]
    for pair, span in enumerate(spans(width)):
        conv = conv_ref[:, span]
        mixes = []
        for h in (2 * pair, 2 * pair + 1):
            gap = cum[:, h : h + 1] - cumt[h : h + 1, :]
            mixes.append(both_parts(jnp.exp(jnp.where(causal, gap, -1e30)) * scores))
        both = wide_dot(jnp.concatenate(mixes, axis=0), conv * wide[:size, span])
        out_ref[:, span] = jnp.where(left, both[:size], both[size:]) + wide[size : size + 1, span] * conv


def inner_forward(heads_count, conv, dt, state_rows, cum, cumt, skip_gain):
    tokens, inner = conv.shape
    return pl.pallas_call(
        functools.partial(inner_kernel, heads_count),
        grid=(tokens // BLOCK,),
        in_specs=[
            rows(BLOCK, inner),
            rows(BLOCK, LANES),
            rows(BLOCK, state_rows.shape[1]),
            rows(BLOCK, LANES),
            pl.BlockSpec((cumt.shape[0], BLOCK), lambda b: (0, b)),
            whole(skip_gain.shape),
        ],
        out_specs=rows(BLOCK, inner),
        out_shape=jax.ShapeDtypeStruct((tokens, inner), f32),
        scratch_shapes=[pltpu.VMEM((LANES, inner), bf16)],
        compiler_params=params(12),
        cost_estimate=cost(6),
    )(conv, dt, state_rows, cum, cumt, skip_gain)


def combine_kernel(count, intra_ref, rows_ref, cum_ref, held_ref, own_ref, *refs):
    message_refs, (gate_ref, grad_ref, gain_ref, mixed_out, sums_out, held_out, end_out, start, total, heads) = refs[:count], refs[count:]
    b = pl.program_id(0)
    size, width = intra_ref.shape
    state = held_ref.shape[1]

    @pl.when(b == 0)
    def _():
        heads[...] = head_map(width)
        total[...] = jnp.zeros(total.shape, f32)
        for span in spans(width):
            entering = jnp.zeros((state, LANES), f32)
            passed = jnp.zeros((EDGE, LANES), f32)
            for ref in message_refs:
                entering = entering + jnp.exp(passed[0:1]) * ref[:state, span]
                passed = passed + ref[state:, span]
            start[:, span] = entering
            end_out[:, span] = own_ref[:state, span] + jnp.exp(own_ref[state : state + 1, span]) * entering

    cum_wide = spread(cum_ref[...], heads[...])
    c_parts = both_parts(rows_ref[:, LANES:])
    square = jnp.zeros((size, LANES), f32)
    inner = jnp.zeros((size, LANES), f32)
    for span in spans(width):
        held = held_ref[0, :, span] + jnp.exp(total[0:1, span]) * start[:, span]
        held_out[0, :, span] = held
        cum_part = cum_wide[:, span]
        total[:, span] = total[:, span] + cum_part[size - 1 : size]
        mixed = intra_ref[:, span] + jnp.exp(cum_part) * wide_dot(c_parts, held)
        mixed_out[:, span] = mixed
        gate = gate_ref[:, span]
        gated = mixed * (gate * sig(gate))
        square = square + gated * gated
        inner = inner + grad_ref[:, span] * gain_ref[:, span] * gated
    ones = jnp.ones((EDGE, LANES), bf16)
    square = exact_dot(ones, square, NT)
    inner = exact_dot(ones, inner, NT)
    sums_out[...] = jnp.where(iota(square.shape, 0) == 0, square, inner)


def combine(intra, state_rows, cum, held, own, messages, gate_in, grad_normed, norm_gain):
    tokens, inner = intra.shape
    blocks, state, _ = held.shape
    state_block = pl.BlockSpec((1, state, inner), lambda b: (b, 0, 0))
    return pl.pallas_call(
        functools.partial(combine_kernel, len(messages)),
        grid=(blocks,),
        in_specs=[
            rows(BLOCK, inner),
            rows(BLOCK, state_rows.shape[1]),
            rows(BLOCK, LANES),
            state_block,
            whole(own.shape),
            *[whole(own.shape) for _ in messages],
            rows(BLOCK, inner),
            rows(BLOCK, inner),
            whole(norm_gain.shape),
        ],
        out_specs=[
            rows(BLOCK, inner),
            pl.BlockSpec((EDGE, BLOCK), lambda b: (0, b)),
            state_block,
            whole((state, inner)),
        ],
        out_shape=[
            jax.ShapeDtypeStruct((tokens, inner), f32),
            jax.ShapeDtypeStruct((EDGE, tokens), f32),
            jax.ShapeDtypeStruct(held.shape, f32),
            jax.ShapeDtypeStruct((state, inner), f32),
        ],
        scratch_shapes=[pltpu.VMEM((state, inner), f32), pltpu.VMEM((EDGE, inner), f32), pltpu.VMEM((LANES, inner), bf16)],
        compiler_params=params(),
        cost_estimate=cost(5),
    )(intra, state_rows, cum, held, own, *messages, gate_in, grad_normed, norm_gain)


def column(row):
    return jnp.broadcast_to(row, (LANES, row.shape[1])).T


def gate_back_kernel(count, inner_total, mixed_ref, gate_ref, grad_ref, rows_ref, cum_ref, gain_ref, *refs):
    sums_refs, (normed_out, gate_out, dmix_out, later_out, message_out, gain_out, later, total, heads) = refs[:count], refs[count:]
    b = pl.program_id(0)
    size, width = mixed_ref.shape

    @pl.when(b == 0)
    def _():
        later[...] = jnp.zeros(later.shape, f32)
        total[...] = jnp.zeros(total.shape, f32)
        gain_out[...] = jnp.zeros(gain_out.shape, f32)
        heads[...] = head_map(width)

    sums = sums_refs[0][...]
    for ref in sums_refs[1:]:
        sums = sums + ref[...]
    rms_row = lax.rsqrt(sums[0:1] / inner_total + epsilon)
    pull_row = rms_row * rms_row * rms_row * sums[1:2] / inner_total
    rms = column(rms_row)
    pull = column(pull_row)
    cum_wide = spread(cum_ref[...], heads[...])
    c_parts = both_parts(rows_ref[:, LANES:].T)
    later_out[0] = later[...]
    for span in spans(width):
        gain = gain_ref[:, span]
        gate = gate_ref[:, span]
        mixed = mixed_ref[:, span]
        grad = grad_ref[:, span]
        gate_sig = sig(gate)
        gate_silu = gate * gate_sig
        gated = mixed * gate_silu
        normed_out[:, span] = (gated * rms * gain).astype(bf16)
        gain_out[:, span] = gain_out[:, span] + by_eights(grad * gated * rms)
        grad_gated = rms * gain * grad - gated * pull
        gate_out[:, span] = (grad_gated * mixed * gate_sig * (1.0 + gate * (1.0 - gate_sig))).astype(bf16)
        grad_mixed = grad_gated * gate_silu
        dmix_out[:, span] = grad_mixed
        cum_part = cum_wide[:, span]
        end = cum_part[size - 1 : size]
        later[:, span] = jnp.exp(end) * later[:, span] + wide_dot(c_parts, jnp.exp(cum_part) * grad_mixed)
        total[:, span] = total[:, span] + end

    @pl.when(b == pl.num_programs(0) - 1)
    def _():
        message_out[:LANES] = later[...]
        message_out[LANES:] = total[...]


def gate_back(mixed, gate_in, grad_normed, state_rows, cum, norm_gain, sums, inner_total):
    tokens, inner = mixed.shape
    blocks = tokens // BLOCK
    state = state_rows.shape[1] // 2
    return pl.pallas_call(
        functools.partial(gate_back_kernel, len(sums), inner_total),
        grid=(blocks,),
        in_specs=[
            rows(BLOCK, inner, blocks),
            rows(BLOCK, inner, blocks),
            rows(BLOCK, inner, blocks),
            rows(BLOCK, 2 * state, blocks),
            rows(BLOCK, LANES, blocks),
            whole(norm_gain.shape),
            *[pl.BlockSpec((EDGE, BLOCK), lambda b: (0, blocks - 1 - b)) for _ in sums],
        ],
        out_specs=[
            rows(BLOCK, inner, blocks),
            rows(BLOCK, inner, blocks),
            rows(BLOCK, inner, blocks),
            pl.BlockSpec((1, state, inner), lambda b: (blocks - 1 - b, 0, 0)),
            whole((state + EDGE, inner)),
            whole((EDGE, inner)),
        ],
        out_shape=[
            jax.ShapeDtypeStruct((tokens, inner), bf16),
            jax.ShapeDtypeStruct((tokens, inner), bf16),
            jax.ShapeDtypeStruct((tokens, inner), f32),
            jax.ShapeDtypeStruct((blocks, state, inner), f32),
            jax.ShapeDtypeStruct((state + EDGE, inner), f32),
            jax.ShapeDtypeStruct((EDGE, inner), f32),
        ],
        scratch_shapes=[pltpu.VMEM((state, inner), f32), pltpu.VMEM((EDGE, inner), f32), pltpu.VMEM((LANES, inner), bf16)],
        compiler_params=params(),
        cost_estimate=cost(7),
    )(mixed, gate_in, grad_normed, state_rows, cum, norm_gain, *sums)


def inner_back_kernel(heads_count, conv_ref, dt_ref, rows_ref, cum_ref, cumt_ref, dmix_ref, driven_out, rows_out, heads):
    size, width = conv_ref.shape

    @pl.when(pl.program_id(0) == 0)
    def _():
        heads[...] = head_map(width)

    dt_wide = spread(dt_ref[...], heads[...])
    b_rows = rows_ref[:, :LANES]
    c_rows = rows_ref[:, LANES:]
    scores = dot3(b_rows, c_rows, NT)
    causal = iota((size, size), 1) >= iota((size, size), 0)
    left = iota((size, LANES), 1) < HEAD_DIM
    cum = cum_ref[...]
    cumt = cumt_ref[...]
    score_grad = jnp.zeros((size, size), f32)
    for pair, span in enumerate(spans(width)):
        dmix_high, dmix_low = split2(dmix_ref[:, span])
        across = jnp.concatenate([dmix_high, dmix_low], axis=1)
        right_side = jnp.concatenate([across, across], axis=0)
        taking = jnp.concatenate([dmix_high, dmix_high, dmix_low], axis=1)
        driven = conv_ref[:, span] * dt_wide[:, span]
        owns = []
        for mine in (left, jnp.logical_not(left)):
            own_high, own_low = split2(jnp.where(mine, driven, 0.0))
            owns.append(jnp.concatenate([own_high, own_low, own_high], axis=1))
        mix_grads = dot(jnp.concatenate(owns, axis=0), taking, NT)
        mixes = []
        for side in range(2):
            h = 2 * pair + side
            gap = cumt[h : h + 1, :] - cum[:, h : h + 1]
            kept = jnp.exp(jnp.where(causal, gap, -1e30))
            score_grad = score_grad + mix_grads[side * size : (side + 1) * size] * kept
            mixes.append(both_parts(kept * scores))
        both = fold(dot(jnp.concatenate(mixes, axis=0), right_side))
        driven_out[:, span] = jnp.where(left, both[:size], both[size:])
    rows_out[:, :LANES] = dot3(score_grad, c_rows, NN)
    rows_out[:, LANES:] = dot3(score_grad, b_rows, TN)


def inner_back(heads_count, conv, dt, state_rows, cum, cumt, grad_mixed):
    tokens, inner = conv.shape
    return pl.pallas_call(
        functools.partial(inner_back_kernel, heads_count),
        grid=(tokens // BLOCK,),
        in_specs=[
            rows(BLOCK, inner),
            rows(BLOCK, LANES),
            rows(BLOCK, state_rows.shape[1]),
            rows(BLOCK, LANES),
            pl.BlockSpec((cumt.shape[0], BLOCK), lambda b: (0, b)),
            rows(BLOCK, inner),
        ],
        out_specs=[rows(BLOCK, inner), rows(BLOCK, state_rows.shape[1])],
        out_shape=[
            jax.ShapeDtypeStruct((tokens, inner), f32),
            jax.ShapeDtypeStruct(state_rows.shape, f32),
        ],
        scratch_shapes=[pltpu.VMEM((LANES, inner), bf16)],
        compiler_params=params(16),
        cost_estimate=cost(9),
    )(conv, dt, state_rows, cum, cumt, grad_mixed)


def stacked(high, low):
    return jnp.concatenate([jnp.concatenate([high, high], axis=1), jnp.concatenate([low, low], axis=1)], axis=0)


def finish_kernel(
    count, driven_ref, drows_ref, dmix_ref, mixed_ref, pre_ref, value_ref, dt_ref, cum_ref, step_ref, rows_ref,
    held_ref, end_ref, later_ref, *refs
):
    message_refs = refs[:count]
    (
        spre_ref, vhalo_ref, kernel_ref, skip_ref, bias_ref, log_ref,
        grad_value_out, grad_rows_out, grad_step_out, last_out, first_out, kernel_out, small_out,
        entering, total, held_next, pre_next, skip_sum, heads, kernel_sum, heads_t, edge_rows,
    ) = refs[count:]
    b = pl.program_id(0)
    size, width = mixed_ref.shape
    state = held_ref.shape[1]
    final = b == pl.num_programs(0) - 1

    @pl.when(b == 0)
    def _():
        heads[...] = head_map(width)
        heads_t[...] = (iota((width, LANES), 1) == iota((width, LANES), 0) // HEAD_DIM).astype(f32).astype(bf16)
        for span in spans(width):
            coming = jnp.zeros((state, LANES), f32)
            passed = jnp.zeros((EDGE, LANES), f32)
            for ref in message_refs:
                coming = coming + jnp.exp(passed[0:1]) * ref[:state, span]
                passed = passed + ref[state:, span]
            entering[:, span] = coming
        total[...] = jnp.zeros(total.shape, f32)
        held_next[...] = end_ref[...]
        pre_next[...] = jnp.zeros(pre_next.shape, f32)
        kernel_sum[...] = jnp.zeros(kernel_sum.shape, f32)
        small_out[...] = jnp.zeros(small_out.shape, f32)
        skip_sum[...] = jnp.zeros(skip_sum.shape, f32)

    dt = dt_ref[...]
    cum = cum_ref[...]
    skip_row = jnp.broadcast_to(repeated(skip_ref[...]), (EDGE, LANES))
    wide = spread(jnp.concatenate([cum, dt, skip_row], axis=0), heads[...])
    b_parts = both_parts(rows_ref[:, :LANES])
    taps = kernel_ref[...].astype(f32)
    toward_b, toward_c, laters, helds, levels, throughs, boundaries = [], [], [], [], [], [], []
    for span in spans(width):
        cum_part = wide[:size, span]
        dt_wide = wide[size : 2 * size, span]
        skip = wide[2 * size : 2 * size + 1, span]
        end = cum_part[size - 1 : size]
        later = later_ref[0, :, span] + jnp.exp(total[0:1, span]) * entering[:, span]
        total[:, span] = total[:, span] + end
        held = held_ref[0, :, span]
        tail = jnp.exp(end - cum_part)
        dmix = dmix_ref[:, span]
        pre = pre_ref[:, span]
        pre_sig = sig(pre)
        conv = pre * pre_sig
        driven = conv * dt_wide
        later_high, later_low = split2(later)
        across = jnp.concatenate([later_high, later_low], axis=1)
        ddriven = driven_ref[:, span] + tail * fold(dot(b_parts, jnp.concatenate([across, across], axis=0)))
        toward_b.append(both_parts(tail * driven))
        laters.append(stacked(later_high, later_low))
        toward_c.append(both_parts(jnp.exp(cum_part) * dmix))
        helds.append(stacked(*split2(held)))
        skip_sum[:, span] = skip_sum[:, span] + by_eights(dmix * conv)
        levels.append(both_parts(dmix * (mixed_ref[:, span] - skip * conv) - driven * ddriven))
        throughs.append(both_parts(ddriven * conv))
        boundaries.append(both_parts(by_eights(later * held_next[:, span])))
        held_next[:, span] = held

        dpre = (ddriven * dt_wide + skip * dmix) * (pre_sig * (1.0 + pre * (1.0 - pre_sig)))
        extended = jnp.concatenate([dpre, pre_next[:, span]], axis=0)
        pre_next[:, span] = dpre[:EDGE]
        value = value_ref[:, span].astype(f32)
        dvalue = jnp.zeros((size, LANES), f32)
        for k in range(CONV):
            shifted = extended[CONV - 1 - k : CONV - 1 - k + size]
            dvalue = dvalue + taps[k : k + 1, span] * shifted
            kernel_sum[k, :, span] = kernel_sum[k, :, span] + by_eights(value * shifted)
        grad_value_out[:, span] = dvalue.astype(bf16)
        edge_rows[:, span] = dvalue[-2 * EDGE :]

    side = lambda parts: jnp.concatenate(parts, axis=1)
    grad_b = dot(side(toward_b), side(laters), NT)
    grad_c = dot(side(toward_c), side(helds), NT)
    picks = jnp.concatenate([heads_t[span] for span in spans(width) for _ in range(2)], axis=0)
    reduced = dot(jnp.concatenate([side(levels), side(throughs), side(boundaries)], axis=0), picks)
    level, through, boundary = reduced[:size], reduced[size : 2 * size], reduced[2 * size :]
    grad_rows_out[:, :LANES] = drows_ref[:, :LANES] + fold(grad_b)
    grad_rows_out[:, LANES:] = drows_ref[:, LANES:] + fold(grad_c)
    boundary = jnp.sum(boundary, axis=0, keepdims=True)
    upper = (iota((size, size), 1) >= iota((size, size), 0)).astype(f32).astype(bf16)
    ddecay = exact_dot(upper, level, NN) + boundary
    rate = jnp.exp(repeated(log_ref[...]))
    dstep = (through - ddecay * rate) * sig(step_ref[...] + repeated(bias_ref[...]))
    grad_step_out[...] = dstep[:, : grad_step_out.shape[1]].astype(bf16)
    small_out[1:2] = small_out[1:2] + jnp.sum(dstep, axis=0, keepdims=True)
    small_out[2:3] = small_out[2:3] + jnp.sum(-ddecay * dt * rate, axis=0, keepdims=True)

    @pl.when(b == 0)
    def _():
        last_out[...] = edge_rows[...]

    @pl.when(final)
    def _():
        first = pre_next[...]
        first_out[:, :width] = first
        first_out[:, width : width + 2 * LANES] = grad_rows_out[:EDGE]
        first_out[:, width + 2 * LANES :] = spre_ref[...]
        ahead = jnp.concatenate([jnp.zeros((EDGE, width), f32), first], axis=0)
        halo = vhalo_ref[...].astype(f32)[-EDGE:]
        kernel_out[...] = jnp.zeros(kernel_out.shape, f32)
        for k in range(CONV):
            shifted = ahead[CONV - 1 - k : CONV - 1 - k + EDGE]
            kernel_out[k : k + 1] = jnp.sum(kernel_sum[k] + halo * shifted, axis=0, keepdims=True)
        high, middle, low = split3(skip_sum[...])
        summed = dot(high, heads[...], NT) + (dot(middle, heads[...], NT) + dot(low, heads[...], NT))
        small_out[0:1] = jnp.sum(summed, axis=0, keepdims=True)


def finish(grad_driven, grad_rows, grad_mixed, mixed, pre, value_in, dt, cum, step_raw, state_rows, held, end_state, later,
           messages, spre, vhalo, input_kernel, skip_gain, step_bias, decay_log):
    tokens, inner = mixed.shape
    blocks, state, _ = held.shape
    head_count = skip_gain.shape[1]
    state_block = pl.BlockSpec((1, state, inner), lambda b: (blocks - 1 - b, 0, 0))
    wide = rows(BLOCK, inner, blocks)
    narrow = rows(BLOCK, LANES, blocks)
    return pl.pallas_call(
        functools.partial(finish_kernel, len(messages)),
        grid=(blocks,),
        in_specs=[
            wide, rows(BLOCK, 2 * state, blocks), wide, wide, wide, wide, narrow, narrow, narrow,
            rows(BLOCK, 2 * state, blocks),
            state_block, whole(end_state.shape), state_block,
            *[whole(m.shape) for m in messages],
            pl.BlockSpec((EDGE, 2 * state), lambda b: (0, 0)), whole(vhalo.shape), whole(input_kernel.shape), whole(skip_gain.shape), whole(step_bias.shape), whole(decay_log.shape),
        ],
        out_specs=[
            wide,
            rows(BLOCK, 2 * state, blocks),
            rows(BLOCK, head_count, blocks),
            whole((2 * EDGE, inner)),
            whole((EDGE, inner + 4 * state)),
            whole((EDGE, inner)),
            whole((EDGE, LANES)),
        ],
        out_shape=[
            jax.ShapeDtypeStruct((tokens, inner), bf16),
            jax.ShapeDtypeStruct((tokens, 2 * state), f32),
            jax.ShapeDtypeStruct((tokens, head_count), bf16),
            jax.ShapeDtypeStruct((2 * EDGE, inner), f32),
            jax.ShapeDtypeStruct((EDGE, inner + 4 * state), f32),
            jax.ShapeDtypeStruct((EDGE, inner), f32),
            jax.ShapeDtypeStruct((EDGE, LANES), f32),
        ],
        scratch_shapes=[
            pltpu.VMEM((state, inner), f32),
            pltpu.VMEM((EDGE, inner), f32),
            pltpu.VMEM((state, inner), f32),
            pltpu.VMEM((EDGE, inner), f32),
            pltpu.VMEM((EDGE, inner), f32),
            pltpu.VMEM((LANES, inner), bf16),
            pltpu.VMEM((CONV, EDGE, inner), f32),
            pltpu.VMEM((inner, LANES), bf16),
            pltpu.VMEM((2 * EDGE, inner), f32),
        ],
        compiler_params=params(56),
        cost_estimate=cost(16),
    )(grad_driven, grad_rows, grad_mixed, mixed, pre, value_in, dt, cum, step_raw, state_rows, held, end_state, later,
      *messages, spre, vhalo, input_kernel, skip_gain, step_bias, decay_log)


def from_before(value, axis, by=1):
    count = lax.axis_size(axis)
    return lax.ppermute(value, axis, [(i, i + by) for i in range(count - by)])


def from_after(value, axis, by=1):
    count = lax.axis_size(axis)
    return lax.ppermute(value, axis, [(i + by, i) for i in range(count - by)])


def from_all(value, axis):
    count = lax.axis_size(axis)
    return [lax.ppermute(value, axis, [(i, (i + by) % count) for i in range(count)]) for by in range(1, count)]


def after(first, then):
    return lax.optimization_barrier((first, then))[1]


def swapped(value, axis, flip):
    return lax.ppermute(value, axis, [(i, i ^ flip) for i in range(lax.axis_size(axis))])


def own_part(array, axis_name, dim):
    size = array.shape[dim] // lax.axis_size(axis_name)
    return lax.dynamic_slice_in_dim(array, lax.axis_index(axis_name) * size, size, dim)


def line_kernel(arrived, plan_ref, up_ref, down_ref, *refs):
    up, down = up_ref[0], down_ref[0]
    if arrived:
        up = up + refs[0][...].astype(f32)
        down = down + refs[1][...].astype(f32)
    refs[-2][...] = up.astype(bf16)
    refs[-1][...] = down.astype(bf16)


def line_step(parts, step, arrived, axis):
    count, tokens, width = parts.shape
    place = lax.axis_index(axis)
    plan = jnp.clip(jnp.stack([count - step + place, step - count + place]), 0, count - 1).astype(jnp.int32)
    tile = min(tokens, 512)
    block = pl.BlockSpec((tile, width), lambda b, plan: (b, 0))
    up, down = pl.pallas_call(
        functools.partial(line_kernel, len(arrived)),
        grid_spec=pltpu.PrefetchScalarGridSpec(
            num_scalar_prefetch=1,
            grid=(tokens // tile,),
            in_specs=[
                pl.BlockSpec((1, tile, width), lambda b, plan: (plan[0], b, 0)),
                pl.BlockSpec((1, tile, width), lambda b, plan: (plan[1], b, 0)),
                *[block for _ in arrived],
            ],
            out_specs=[block, block],
        ),
        out_shape=[jax.ShapeDtypeStruct((tokens, width), bf16)] * 2,
        compiler_params=params(12),
        cost_estimate=cost(2),
    )(plan, parts, parts, *arrived)
    return (up, down), [
        lax.ppermute(up, axis, [(k, k + 1) for k in range(step)]),
        lax.ppermute(down, axis, [(count - 1 - k, count - 2 - k) for k in range(step)]),
    ]


def input_kernel_body(pieces, gate_ref, value_ref, step_ref, last_ref, ahead_ref, taps_ref, x_ref, gain_ref, gate_w, value_w, step_w, *outs):
    part_out, value_out, row_out, col_out, fixed_out = outs
    b = pl.program_id(0)
    size, inner = value_ref.shape

    @pl.when(b == 0)
    def _():
        col_out[...] = jnp.zeros(col_out.shape, f32)
        fixed = last_ref[...]
        taps = taps_ref[...].astype(f32)
        extended = jnp.concatenate([jnp.zeros((2 * EDGE, inner), f32), ahead_ref[:, :inner]], axis=0)
        for k in range(CONV):
            fixed = fixed + taps[k : k + 1] * extended[CONV - 1 - k : CONV - 1 - k + 2 * EDGE]
        fixed_out[...] = fixed.astype(bf16)

    gate = gate_ref[...]
    value = value_ref[...]
    patched = jnp.concatenate([value[: size - 2 * EDGE], fixed_out[...]], axis=0)
    value = jnp.where(b == pl.num_programs(0) - 1, patched, value)
    value_out[...] = value
    step = step_ref[...]
    x = x_ref[...].astype(f32)
    scaling = lax.rsqrt(jnp.mean(x * x, axis=-1, keepdims=True) + epsilon)
    part = x.shape[1] // pieces
    row = jnp.zeros((size, LANES), f32)
    for j in range(pieces):
        span = slice(j * part, (j + 1) * part)
        partial = dot(gate, gate_w[span, :], NT) + dot(value, value_w[span, :], NT) + dot(step, step_w[:, span])
        part_out[j] = partial
        pulled = partial * x[:, span]
        gained = pulled * gain_ref[:, span]
        for inside in spans(part):
            row = row + gained[:, inside]
        col_out[:, span] = col_out[:, span] + by_eights(pulled * scaling)
    row_out[...] = exact_dot(jnp.ones((EDGE, LANES), bf16), row, NT)


def input_partials(pieces, grad_gate, grad_value, grad_step, last_rows, ahead, input_kernel, residual, pre_gain, gate_weight, input_weight, step_weight):
    tokens, width = residual.shape
    inner = grad_gate.shape[1]
    part = width // pieces
    tile = min(tokens, 256)
    return pl.pallas_call(
        functools.partial(input_kernel_body, pieces),
        grid=(tokens // tile,),
        in_specs=[
            rows(tile, inner),
            rows(tile, inner),
            rows(tile, grad_step.shape[1]),
            whole(last_rows.shape),
            whole(ahead.shape),
            whole(input_kernel.shape),
            rows(tile, width),
            whole(pre_gain.shape),
            whole(gate_weight.shape),
            whole(input_weight.shape),
            whole(step_weight.shape),
        ],
        out_specs=[
            pl.BlockSpec((pieces, tile, part), lambda b: (0, b, 0)),
            rows(tile, inner),
            pl.BlockSpec((EDGE, tile), lambda b: (0, b)),
            whole((EDGE, width)),
        ],
        out_shape=[
            jax.ShapeDtypeStruct((pieces, tokens, part), f32),
            jax.ShapeDtypeStruct((tokens, inner), bf16),
            jax.ShapeDtypeStruct((EDGE, tokens), f32),
            jax.ShapeDtypeStruct((EDGE, width), f32),
        ],
        scratch_shapes=[pltpu.VMEM((2 * EDGE, inner), bf16)],
        compiler_params=params(28),
        cost_estimate=cost(9),
    )(grad_gate, grad_value, grad_step, last_rows, ahead, input_kernel, residual, pre_gain, gate_weight, input_weight, step_weight)


def scalar_call(body, plan, operands, in_specs, out_specs, out_shape, grid=(1,), scratch=(), limit=16, micros=2):
    return pl.pallas_call(
        body,
        grid_spec=pltpu.PrefetchScalarGridSpec(
            num_scalar_prefetch=1, grid=grid, in_specs=in_specs, out_specs=out_specs, scratch_shapes=list(scratch)
        ),
        out_shape=out_shape,
        compiler_params=pltpu.CompilerParams(dimension_semantics=("arbitrary",) * len(grid), vmem_limit_bytes=limit * 1024 * 1024),
        cost_estimate=cost(micros),
    )(plan, *operands)


def all_of(a):
    return pl.BlockSpec(a.shape, lambda *_: (0,) * len(a.shape))


def pieces_kernel(count, plan_ref, rows_ref, ahead_ref, *outs):
    tokens, state2 = rows_ref.shape
    part = tokens // count
    first = ahead_ref.shape[1] - 2 * state2
    for k, out in enumerate(outs):
        at = lax.rem(plan_ref[0] + k, count)
        start = pl.multiple_of(at * part, EDGE)
        out[:part] = rows_ref[pl.ds(start, part)]
        beyond = pl.multiple_of(jnp.minimum(start + part, tokens - EDGE), EDGE)
        out[part:] = jnp.where(at == count - 1, ahead_ref[:, first : first + state2], rows_ref[pl.ds(beyond, EDGE)])


def pieces_of(place, count, grad_rows, ahead):
    tokens, state2 = grad_rows.shape
    shape = jax.ShapeDtypeStruct((tokens // count + EDGE, state2), f32)
    return scalar_call(
        functools.partial(pieces_kernel, count), place, (grad_rows, ahead), [all_of(grad_rows), all_of(ahead)],
        [all_of(shape)] * count, [shape] * count, limit=8, micros=1,
    )


def three_parts(x):
    return jnp.concatenate(split3(x), axis=0)


def three_sum(parts):
    size = parts.shape[0] // 3
    parts = parts.astype(f32)
    return parts[:size] + (parts[size : 2 * size] + parts[2 * size :])


PACK = 16


def state_kernel_body(count, plan_ref, *refs):
    grads = refs[:count]
    spre_ref, input_ref, halo_ref, ahead_ref, taps_ref, w_ref, x_ref, gain_ref, row_ref, col_ref, out_ref, inputs = refs[count:]
    tokens, state2 = spre_ref.shape
    part = tokens // count
    at = plan_ref[0]
    start = pl.multiple_of(at * part, 2 * EDGE)
    total = grads[0][...]
    for ref in grads[1:]:
        total = total + ref[...]
    beyond = pl.multiple_of(jnp.minimum(start + part, tokens - EDGE), EDGE)
    after_rows = jnp.where(at == count - 1, ahead_ref[:, ahead_ref.shape[1] - state2 :], spre_ref[pl.ds(beyond, EDGE)])
    pre = jnp.concatenate([spre_ref[pl.ds(start, part)], after_rows], axis=0)
    s = sig(pre)
    through = total * (s * (1.0 + pre * (1.0 - s)))
    taps = taps_ref[...].astype(f32)
    before = pl.multiple_of(jnp.maximum(start - 2 * EDGE, 0), 2 * EDGE)
    inputs[: 2 * EDGE] = jnp.where(at == 0, halo_ref[...].astype(f32), input_ref[pl.ds(before, 2 * EDGE)].astype(f32))
    inputs[2 * EDGE :] = input_ref[pl.ds(start, part)].astype(f32)
    grad = jnp.zeros((part, state2), f32)
    own = through[:part]
    first = 2 * EDGE - CONV + 1
    tap_rows = []
    for k in range(CONV):
        grad = grad + taps[k : k + 1] * through[CONV - 1 - k : CONV - 1 - k + part]
        tap_rows.append(jnp.sum(own * inputs[first + k : first + k + part], axis=0, keepdims=True))
    rounded = grad.astype(bf16)
    out_ref[:part] = rounded
    x = x_ref[...].astype(f32)
    width = x.shape[1]
    scaling = lax.rsqrt(jnp.mean(x * x, axis=-1, keepdims=True) + epsilon)
    row = jnp.zeros((part, LANES), f32)
    cols = []
    for span in spans(width):
        pulled = dot(rounded, w_ref[span, :], NT) * x[:, span]
        row = row + pulled * gain_ref[:, span]
        cols.append(jnp.sum(by_eights(pulled * scaling) + col_ref[:, span], axis=0, keepdims=True))
    row = exact_dot(jnp.ones((EDGE, LANES), bf16), row, NT)[:1]
    packed = [row_ref[:1, j * part : (j + 1) * part] + jnp.where(at == j, row, 0.0) for j in range(count)]
    wide = state2 // LANES
    packed += [jnp.concatenate(cols[i : i + wide], axis=1) for i in range(0, len(cols), wide)]
    packed += tap_rows
    packed.append(jnp.zeros((PACK - len(packed), state2), f32))
    out_ref[part:] = three_parts(jnp.concatenate(packed, axis=0))


def state_back(place, grads, spre, state_in, halo, ahead, taps, weight, residual, pre_gain, row_sums, col_sums):
    count = len(grads)
    tokens, state2 = spre.shape
    part = tokens // count
    shape = jax.ShapeDtypeStruct((part + 3 * PACK, state2), bf16)
    operands = (*grads, spre, state_in, halo, ahead, taps, weight, residual, pre_gain, row_sums, col_sums)
    in_specs = [all_of(a) for a in operands]
    in_specs[count + 6] = pl.BlockSpec((part, residual.shape[1]), lambda b, plan: (plan[0], 0))
    return scalar_call(
        functools.partial(state_kernel_body, count), place, operands, in_specs, all_of(shape), shape,
        scratch=[pltpu.VMEM((part + 2 * EDGE, state2), f32)], limit=16, micros=3,
    )


SMALL = 48


def narrow_kernel(count, plan_ref, *refs):
    messages = refs[:count]
    step_ref, kernel_ref, gain_ref, small_ref, out_ref, row_out = refs[count:]
    tokens, steps = step_ref.shape
    part = tokens // count
    state2 = messages[0].shape[1]
    mine = state2 // count
    me = plan_ref[0]
    pick = ((iota((state2, LANES), 0) == iota((state2, LANES), 1) + me * mine) & (iota((state2, LANES), 1) < mine)).astype(f32).astype(bf16)
    place = (iota((steps, LANES), 0) + mine == iota((steps, LANES), 1)).astype(f32).astype(bf16)
    sums = jnp.zeros((PACK, state2), f32)
    for k in range(count):
        start = pl.multiple_of(lax.rem(me - k + count, count) * part, 2 * EDGE)
        both = dot(messages[k][:part], pick) + dot(step_ref[pl.ds(start, part)], place)
        out_ref[pl.ds(start, part)] = both.astype(bf16)
        sums = sums + three_sum(messages[k][part:])
    row_out[...] = sums
    wide = state2 // LANES
    inner = kernel_ref.shape[1]
    rows_of = [kernel_ref[k : k + 1, span] for k in range(CONV) for span in spans(inner)]
    gain = jnp.sum(gain_ref[...], axis=0, keepdims=True)
    rows_of += [gain[:, span] for span in spans(inner)]
    rows_of += [small_ref[i : i + 1] for i in range(3)]
    cols = [sums[count + r : count + r + 1, i * LANES : (i + 1) * LANES] for r in range(PACK - count - CONV) for i in range(wide)]
    quarter = (PACK - count - CONV - 2) * wide // count
    for i in range(quarter):
        chosen = jnp.zeros((1, LANES), f32)
        for q in range(count):
            chosen = jnp.where(me == q, cols[q * quarter + i], chosen)
        rows_of.append(chosen)
    first = count + (PACK - count - CONV - 2)
    rows_of += [sums[first + k : first + k + 1, i * LANES : (i + 1) * LANES] for k in range(CONV) for i in range(wide)]
    rows_of.append(jnp.zeros((SMALL - len(rows_of), LANES), f32))
    out_ref[tokens:] = three_parts(jnp.concatenate(rows_of, axis=0))


def narrow_of(place, messages, grad_step, kernel_grad, gain_grad, small):
    count = len(messages)
    tokens = grad_step.shape[0]
    shapes = [jax.ShapeDtypeStruct((tokens + 3 * SMALL, LANES), bf16), jax.ShapeDtypeStruct((PACK, messages[0].shape[1]), f32)]
    operands = (*messages, grad_step, kernel_grad, gain_grad, small)
    return scalar_call(
        functools.partial(narrow_kernel, count), place, operands, [all_of(a) for a in operands],
        [all_of(a) for a in shapes], shapes, limit=8, micros=2,
    )


def wide_weights_kernel(plan_ref, normed_a, normed_b, gate_a, gate_b, out_a, out_b, cot_a, cot_b, *outs):
    k = pl.program_id(0)
    tile = normed_a.shape[1]
    gate = dot(normed_a[...], gate_a[...], TN) + dot(normed_b[...], gate_b[...], TN)
    out = dot(out_a[...], cot_a[...], TN) + dot(out_b[...], cot_b[...], TN)
    for i, ref in enumerate(outs):

        @pl.when(k == i)
        def _(ref=ref):
            ref[:tile] = gate
            ref[tile:] = out


def wide_weights(plan, count, normed, grad_gate, normed_out, cotangent):
    tokens, width = normed[0].shape
    tile = width // count
    moving = pl.BlockSpec((tokens, tile), lambda k, plan: (0, jnp.bitwise_xor(plan[1], k)))
    still = pl.BlockSpec((tokens, tile), lambda k, plan: (0, plan[0]))
    shape = jax.ShapeDtypeStruct((2 * tile, tile), f32)
    return scalar_call(
        wide_weights_kernel, plan, (*normed, *grad_gate, *normed_out, *cotangent),
        [moving, moving, still, still, still, still, moving, moving],
        [all_of(shape)] * count, [shape] * count, grid=(count,), limit=28, micros=8,
    )


def value_weights_kernel(plan_ref, normed_a, normed_b, value_a, value_b, *outs):
    k = pl.program_id(0)
    total = dot(normed_a[...], value_a[...], TN) + dot(normed_b[...], value_b[...], TN)
    for i, ref in enumerate(outs):

        @pl.when(k == i)
        def _(ref=ref):
            ref[...] = total


def value_weights(plan, count, normed, grad_value):
    tokens, width = normed[0].shape
    tile = width // count
    half = grad_value[0].shape[1] // 2
    moving = pl.BlockSpec((tokens, tile), lambda k, plan: (0, jnp.bitwise_xor(plan[1], k)))
    still = pl.BlockSpec((tokens, half), lambda k, plan: (0, plan[0]))
    shape = jax.ShapeDtypeStruct((tile, half), f32)
    return scalar_call(
        value_weights_kernel, plan, (*normed, *grad_value), [moving, moving, still, still],
        [all_of(shape)] * count, [shape] * count, grid=(count,), limit=20, micros=5,
    )


def narrow_weights_kernel(plan_ref, normed_a, normed_b, narrow_a, narrow_b, *outs):
    k = pl.program_id(0)
    tokens, tile = normed_a.shape
    total = dot(narrow_a[:tokens], normed_a[...], TN) + dot(narrow_b[:tokens], normed_b[...], TN)
    small = three_sum(narrow_a[tokens:]) + three_sum(narrow_b[tokens:])
    per_row = tile // LANES
    for i, ref in enumerate(outs):

        @pl.when(k == i)
        def _(ref=ref):
            ref[:LANES] = total
            for j in range(per_row):
                ref[LANES:, j * LANES : (j + 1) * LANES] = small[j * SMALL // per_row : (j + 1) * SMALL // per_row]


def narrow_weights(plan, count, normed, narrow):
    tokens, width = normed[0].shape
    tile = width // count
    moving = pl.BlockSpec((tokens, tile), lambda k, plan: (0, jnp.bitwise_xor(plan[1], k)))
    shape = jax.ShapeDtypeStruct((LANES + SMALL * LANES // tile, tile), f32)
    return scalar_call(
        narrow_weights_kernel, plan, (*normed, *narrow), [moving, moving, all_of(narrow[0]), all_of(narrow[1])],
        [all_of(shape)] * count, [shape] * count, grid=(count,), limit=16, micros=4,
    )


def sum_kernel(count, *refs):
    total = refs[0][...]
    for ref in refs[1:count]:
        total = total + ref[...]
    refs[count][...] = total.astype(refs[count].dtype)


def sum_of(arrays, dtype):
    shape = jax.ShapeDtypeStruct(arrays[0].shape, dtype)
    return pl.pallas_call(
        functools.partial(sum_kernel, len(arrays)),
        out_shape=shape,
        compiler_params=pltpu.CompilerParams(vmem_limit_bytes=16 * 1024 * 1024),
        cost_estimate=cost(2),
    )(*arrays)


def over_ctx(arrays, wait=()):
    arrived = [swapped(a, "ctx", k) for k, a in enumerate(arrays) if k]
    total = sum_of([arrays[0], *after(wait, arrived)], f32)
    step = 2
    while step < lax.axis_size("dp"):
        total = total + swapped(total, "dp", step)
        step *= 2
    return total


def gather_chunks(chunk):
    return jnp.concatenate([chunk, *[swapped(chunk, "ctx", k) for k in range(1, lax.axis_size("ctx"))]], axis=0)


def ordered(first, here, there):
    here, there = here.astype(f32), there.astype(f32)
    return jnp.where(first, here, there), jnp.where(first, there, here)


def wide_together_kernel(plan_ref, here, there, gate_out, out_out):
    tile = gate_out.shape[0]
    k = jnp.bitwise_xor(pl.program_id(0), plan_ref[1])
    first = plan_ref[0] == 0
    half = gate_out.shape[1] // 2
    span = pl.ds(pl.multiple_of(k * 2 * tile, 2 * EDGE), tile)
    gate_out[:, :half], gate_out[:, half:] = ordered(first, here[span], there[span])
    span = pl.ds(pl.multiple_of(k * 2 * tile + tile, 2 * EDGE), tile)
    out_out[:tile], out_out[tile:] = ordered(first, here[span], there[span])


def wide_together(plan, count, here, there):
    tile = here.shape[0] // (2 * count)
    width, inner = tile * count, 2 * here.shape[1]
    return scalar_call(
        wide_together_kernel, plan, (here, there), [all_of(here), all_of(there)],
        [pl.BlockSpec((tile, inner), lambda q, plan: (q, 0)), pl.BlockSpec((inner, tile), lambda q, plan: (0, q))],
        [jax.ShapeDtypeStruct((width, inner), f32), jax.ShapeDtypeStruct((inner, width), f32)],
        grid=(count,), limit=24, micros=6,
    )


def narrow_together_kernel(plan_ref, here, there, input_out, state_out, step_out):
    tile = input_out.shape[0]
    k = jnp.bitwise_xor(pl.program_id(0), plan_ref[1])
    half = input_out.shape[1] // 2
    start = pl.multiple_of(k * (tile + LANES), 2 * EDGE)
    span = pl.ds(start, tile)
    input_out[:, :half], input_out[:, half:] = ordered(plan_ref[0] == 0, here[span], there[span])
    rest = here[pl.ds(pl.multiple_of(start + tile, 2 * EDGE), LANES)].astype(f32)
    states = state_out.shape[0]
    state_out[...] = rest[:states]
    step_out[...] = rest[states : states + step_out.shape[0]]


def narrow_together(plan, count, here, there, state_part, steps):
    tile = here.shape[0] // count - LANES
    width, inner = tile * count, 2 * here.shape[1]
    by_lane = lambda size: pl.BlockSpec((size, tile), lambda q, plan: (0, q))
    return scalar_call(
        narrow_together_kernel, plan, (here, there), [all_of(here), all_of(there)],
        [pl.BlockSpec((tile, inner), lambda q, plan: (q, 0)), by_lane(state_part), by_lane(steps)],
        [
            jax.ShapeDtypeStruct((width, inner), f32),
            jax.ShapeDtypeStruct((state_part, width), f32),
            jax.ShapeDtypeStruct((steps, width), f32),
        ],
        grid=(count,), limit=20, micros=4,
    )


def final_kernel(count, plan_ref, part_ref, up_ref, down_ref, x_ref, mine_ref, cot_ref, gain_ref, w_ref, sums_ref, *refs):
    messages, out_ref = refs[:count], refs[count]
    b = pl.program_id(0)
    size, part = up_ref.shape
    k = lax.rem(plan_ref[0] - b + count, count)
    state = messages[0][:size]
    for i in range(1, count):
        state = jnp.where(k == i, messages[i][:size], state)
    normed_grad = part_ref[0] + up_ref[...].astype(f32) + down_ref[...].astype(f32) + dot(state, w_ref[...], NT)
    x = x_ref[...].astype(f32)
    width = x.shape[1]
    scaling = lax.rsqrt(jnp.mean(x * x, axis=-1, keepdims=True) + epsilon)
    row = jnp.zeros((1, size), f32)
    for q in range(count):
        row = jnp.where(b == q, sums_ref[q : q + 1], row)
    pull = column(row) * ((scaling * scaling * scaling) / width)
    for span in spans(part):
        out_ref[:, span] = (
            cot_ref[:, span].astype(f32) + scaling * gain_ref[:, span] * normed_grad[:, span] - mine_ref[:, span].astype(f32) * pull
        )


def final(place, parts, arrived, residual, cotangent, pre_gain, state_weight, sums, messages):
    count, tokens, part = parts.shape
    size = tokens // count
    state2 = state_weight.shape[1]
    mine = pl.BlockSpec((size, part), lambda b, plan: (b, plan[0]))
    return scalar_call(
        functools.partial(final_kernel, count), place,
        (parts, *arrived, residual, residual, cotangent, pre_gain, state_weight, sums, *messages),
        [
            pl.BlockSpec((1, size, part), lambda b, plan: (plan[0], b, 0)),
            pl.BlockSpec((size, part), lambda b, plan: (b, 0)),
            pl.BlockSpec((size, part), lambda b, plan: (b, 0)),
            pl.BlockSpec((size, residual.shape[1]), lambda b, plan: (b, 0)),
            mine,
            mine,
            pl.BlockSpec((1, part), lambda b, plan: (0, plan[0])),
            pl.BlockSpec((part, state2), lambda b, plan: (plan[0], 0)),
            all_of(sums),
            *[all_of(m) for m in messages],
        ],
        pl.BlockSpec((size, part), lambda b, plan: (b, 0)),
        jax.ShapeDtypeStruct((tokens, part), f32),
        grid=(count,), limit=16, micros=4,
    )


def per_device(residual, pre_gain, gate_weight, input_weight, state_weight, step_weight, input_kernel, state_kernel,
               step_bias, decay_log, skip_gain, norm_gain, out_weight, cotangent):
    residual, cotangent = residual[0], cotangent[0]
    tokens, width = residual.shape
    tensor_size = lax.axis_size("tensor")
    ctx_size = lax.axis_size("ctx")
    inner = gate_weight.shape[1]
    inner_total = inner * tensor_size
    head_count = step_weight.shape[1]
    state2 = state_weight.shape[1]
    state_part = state2 // tensor_size
    row = lambda v: v.reshape(1, -1)
    plan = jnp.stack([lax.axis_index("dp") % 2, lax.axis_index("ctx")]).astype(jnp.int32)
    place = lax.axis_index("tensor").astype(jnp.int32).reshape(1)

    halo = from_before(residual[-2 * EDGE :], "ctx")
    other_cotangent = swapped(cotangent, "dp", 1)
    step_weight = step_weight.T
    normed, value_in, state_in, step_raw = project(residual, row(pre_gain), input_weight, state_weight, step_weight)
    other_normed = swapped(normed, "dp", 1)
    conv, pre, state_rows, spre, dt, cum, cumt, held, message, vhalo, shalo = local_states(
        value_in, state_in, step_raw, halo, row(pre_gain), input_weight, state_weight, input_kernel, state_kernel,
        row(step_bias), row(decay_log)
    )
    messages = [from_before(message, "ctx", by) for by in range(1, ctx_size)]
    gate_in, grad_normed = beside(after(message, normed), gate_weight, cotangent, out_weight)
    intra = inner_forward(head_count, conv, dt, state_rows, cum, cumt, row(skip_gain))
    messages = after((gate_in, intra), messages)
    mixed, sums, held, end_state = combine(
        intra, state_rows, cum, held, message, messages, gate_in, grad_normed, row(norm_gain)
    )
    all_sums = [sums, *from_all(sums, "tensor")]
    normed_out, grad_gate, grad_mixed, later, message, gain_grad = gate_back(
        mixed, gate_in, grad_normed, state_rows, cum, row(norm_gain), all_sums, inner_total
    )
    messages = [from_after(message, "ctx", by) for by in range(1, ctx_size)]
    other_gate = swapped(grad_gate, "dp", 1)
    other_out = swapped(normed_out, "dp", 1)

    resid_part = own_part(residual, "tensor", 1).astype(f32)
    partial_out = dot(after(message, normed_out), out_weight)
    branch = lax.psum_scatter(partial_out, "tensor", scatter_dimension=1, tiled=True)
    output = (resid_part + branch).astype(bf16)

    wide = wide_weights(
        after(partial_out, plan), ctx_size, (normed, other_normed), (grad_gate, other_gate), (normed_out, other_out),
        (cotangent, other_cotangent)
    )
    grad_driven, grad_rows = inner_back(head_count, conv, dt, state_rows, cum, cumt, after(wide, grad_mixed))
    messages = after(grad_driven, messages)
    grad_value, grad_rows, grad_step, last_rows, first_rows, kernel_grad, small = finish(
        grad_driven, grad_rows, grad_mixed, mixed, pre, value_in, dt, cum, step_raw, state_rows, held, end_state, later,
        messages, spre, vhalo, input_kernel, row(skip_gain), row(step_bias), row(decay_log)
    )
    ahead = from_after(first_rows, "ctx")
    wide_chunk = over_ctx(wide, first_rows).astype(bf16)
    ahead = after(wide_chunk, ahead)

    pieces = pieces_of(place, tensor_size, grad_rows, ahead)
    arrived = [
        lax.ppermute(pieces[k], "tensor", [(i, (i + k) % tensor_size) for i in range(tensor_size)]) for k in range(1, tensor_size)
    ]
    parts, grad_value, row_sums, col_sums = input_partials(
        tensor_size, grad_gate, grad_value, grad_step, last_rows, ahead, input_kernel,
        residual, row(pre_gain), gate_weight, input_weight, step_weight
    )
    other_value = swapped(grad_value, "dp", 1)
    sent, moving = line_step(parts, 1, [], "tensor")
    wide_here = gather_chunks(wide_chunk)
    weights = value_weights(after(sent, plan), ctx_size, (normed, other_normed), (grad_value, other_value))
    arrived = after(weights, arrived)
    state_message = state_back(
        place, [pieces[0], *arrived], spre, state_in, shalo, ahead, state_kernel, state_weight, residual, row(pre_gain),
        row_sums, col_sums
    )
    arrived = from_all(state_message, "tensor")
    wide_there = swapped(wide_here, "dp", 1)
    sent, moving = line_step(parts, 2, moving, "tensor")
    state_messages = [state_message, *after(sent, arrived)]
    narrow, sums = narrow_of(place, state_messages, grad_step, kernel_grad, gain_grad, small)
    other_narrow = swapped(narrow, "dp", 1)
    value_chunk = over_ctx(weights, narrow)
    weights = narrow_weights(plan, ctx_size, (normed, other_normed), (narrow, other_narrow))
    gate_weight_grad, out_weight_grad = wide_together(plan, ctx_size, wide_here, wide_there)
    narrow_total = over_ctx(weights, (gate_weight_grad, output))
    sent, moving = line_step(parts, 3, moving, "tensor")
    chunk = after(sent, jnp.concatenate([value_chunk, narrow_total[:LANES]], axis=0).astype(bf16))
    arrived = [swapped(chunk, "ctx", k) for k in range(1, ctx_size)]
    input_grad = final(place, parts, moving, residual, cotangent, row(pre_gain), state_weight, sums, state_messages)
    narrow_here = jnp.concatenate([chunk, *after(input_grad, arrived)], axis=0)
    narrow_there = swapped(narrow_here, "dp", 1)
    input_weight_grad, state_weight_grad, step_weight_grad = narrow_together(
        plan, ctx_size, narrow_here, narrow_there, state_part, head_count
    )
    small_total = narrow_total[LANES:]
    small_total = jnp.concatenate([small_total[:, i : i + LANES] for i in range(0, small_total.shape[1], LANES)], axis=0)
    wide_rows = inner // LANES
    at = CONV * wide_rows
    kernel_grad = small_total[:at].reshape(CONV, inner)
    gain_grad = small_total[at : at + wide_rows].reshape(inner)
    at += wide_rows
    small = small_total[at : at + 3, :head_count]
    at += 3
    gain_rows = width // tensor_size // LANES
    pre_gain_grad = small_total[at : at + gain_rows].reshape(width // tensor_size)
    at += gain_rows
    taps_grad = small_total[at : at + CONV * state2 // LANES].reshape(CONV, state2)
    return (
        output[None],
        input_grad[None],
        pre_gain_grad,
        gate_weight_grad,
        input_weight_grad,
        state_weight_grad.T,
        step_weight_grad.T,
        kernel_grad,
        taps_grad,
        small[1],
        small[2],
        small[0],
        gain_grad,
        out_weight_grad,
    )


def solution(mesh):
    in_specs = (
        P("dp", "ctx", None),
        P(),
        P(None, "tensor"),
        P(None, "tensor"),
        P(),
        P(None, "tensor"),
        P(None, "tensor"),
        P(),
        P("tensor"),
        P("tensor"),
        P("tensor"),
        P("tensor"),
        P("tensor", None),
        P("dp", "ctx", None),
    )
    out_specs = (
        P("dp", "ctx", "tensor"),
        P("dp", "ctx", "tensor"),
        P("tensor"),
        P(None, "tensor"),
        P(None, "tensor"),
        P(None, "tensor"),
        P(None, "tensor"),
        P(None, "tensor"),
        P(),
        P("tensor"),
        P("tensor"),
        P("tensor"),
        P("tensor"),
        P("tensor", None),
    )
    return jax.shard_map(per_device, mesh=mesh, in_specs=in_specs, out_specs=out_specs, check_vma=False)
```

```python
import functools

import jax
import jax.numpy as jnp
from jax import lax
from jax.experimental import pallas as pl
from jax.experimental.pallas import tpu as pltpu
from jax.sharding import PartitionSpec as P

HEAD_DIM = 64
CONV = 4
EDGE = 8
BLOCK = 128
LANES = 128
epsilon = 1e-05
f32 = jnp.float32
bf16 = jnp.bfloat16

NN = (((1,), (0,)), ((), ()))
NT = (((1,), (1,)), ((), ()))
TN = (((0,), (0,)), ((), ()))


def dot(a, b, dims=NN):
    return lax.dot_general(a, b, dims, preferred_element_type=f32)


def split2(x):
    high = x.astype(bf16)
    return high, (x - high.astype(f32)).astype(bf16)


def split3(x):
    high = x.astype(bf16)
    rest = x - high.astype(f32)
    middle = rest.astype(bf16)
    return high, middle, (rest - middle.astype(f32)).astype(bf16)


def dot3(a, b, dims=NN):
    ah, al = split2(a)
    bh, bl = split2(b)
    return dot(ah, bh, dims) + (dot(ah, bl, dims) + dot(al, bh, dims))


def both_parts(x):
    return jnp.concatenate(split2(x), axis=1)


def fold(product):
    half = product.shape[1] // 2
    return product[:, :half] + product[:, half:]


def wide_dot(parts, x):
    across = both_parts(x)
    return fold(dot(parts, jnp.concatenate([across, across], axis=0)))


def exact_dot(ones, x, dims):
    high, middle, low = split3(x)
    return dot(ones, high, dims) + (dot(ones, middle, dims) + dot(ones, low, dims))


def iota(shape, axis):
    return lax.broadcasted_iota(jnp.int32, shape, axis)


REPEAT = 16


def head_map(width):
    lane = iota((LANES, width), 0)
    mine = (lane % REPEAT == iota((LANES, width), 1) // HEAD_DIM) & (lane < 3 * REPEAT)
    return mine.astype(f32).astype(bf16)


def spread(per_head, heads):
    high = per_head.astype(bf16).astype(f32)
    rest = per_head - high
    middle = rest.astype(bf16).astype(f32)
    group = iota(per_head.shape, 1) // REPEAT
    parts = jnp.where(group == 0, high, jnp.where(group == 1, middle, rest - middle))
    return dot(parts.astype(bf16), heads)


def repeated(row):
    group = jnp.concatenate([row, jnp.zeros((1, REPEAT - row.shape[1]), f32)], axis=1)
    return jnp.concatenate([group] * (LANES // REPEAT), axis=1)


def sig(v):
    return jax.nn.sigmoid(v)


def cost(micros):
    return pl.CostEstimate(flops=micros * 900_000_000, bytes_accessed=micros * 3_000_000, transcendentals=0)


def params(limit=20):
    return pltpu.CompilerParams(
        dimension_semantics=("arbitrary",), vmem_limit_bytes=limit * 1024 * 1024
    )


def whole(shape):
    return pl.BlockSpec(shape, lambda b: (0,) * len(shape))


def rows(size, width, count=0):
    if count:
        return pl.BlockSpec((size, width), lambda b: (count - 1 - b, 0))
    return pl.BlockSpec((size, width), lambda b: (b, 0))


def spans(width):
    return [slice(i * LANES, (i + 1) * LANES) for i in range(width // LANES)]


def by_eights(x):
    return jnp.sum(x.reshape(x.shape[0] // EDGE, EDGE, x.shape[1]), axis=0)


def norm_rows(x, gain):
    scaling = lax.rsqrt(jnp.mean(x * x, axis=-1, keepdims=True) + epsilon)
    return (x * scaling * gain).astype(bf16)


def project_kernel(x_ref, gain_ref, value_ref, state_ref, step_ref, normed_out, value_out, state_out, step_out, step_w):
    @pl.when(pl.program_id(0) == 0)
    def _():
        count = step_ref.shape[0]
        copies = (iota((LANES, count), 0) % REPEAT == iota((LANES, count), 1)).astype(f32).astype(bf16)
        step_w[...] = dot(copies, step_ref[...]).astype(bf16)

    normed = norm_rows(x_ref[...].astype(f32), gain_ref[...])
    normed_out[...] = normed
    value_out[...] = dot(normed, value_ref[...]).astype(bf16)
    state_out[...] = dot(normed, state_ref[...]).astype(bf16)
    step_out[...] = dot(normed, step_w[...], NT)


def project(residual, pre_gain, input_weight, state_weight, step_weight):
    tokens, width = residual.shape
    inner, state2 = input_weight.shape[1], state_weight.shape[1]
    tile = min(tokens, 256)
    return pl.pallas_call(
        project_kernel,
        grid=(tokens // tile,),
        in_specs=[
            rows(tile, width),
            whole((1, width)),
            whole(input_weight.shape),
            whole(state_weight.shape),
            whole(step_weight.shape),
        ],
        out_specs=[rows(tile, width), rows(tile, inner), rows(tile, state2), rows(tile, LANES)],
        out_shape=[
            jax.ShapeDtypeStruct((tokens, width), bf16),
            jax.ShapeDtypeStruct((tokens, inner), bf16),
            jax.ShapeDtypeStruct((tokens, state2), bf16),
            jax.ShapeDtypeStruct((tokens, LANES), f32),
        ],
        scratch_shapes=[pltpu.VMEM((LANES, width), bf16)],
        compiler_params=params(56),
        cost_estimate=cost(6),
    )(residual, pre_gain, input_weight, state_weight, step_weight)


def beside_kernel(normed_ref, gate_w, cot_ref, out_w, gate_out, grad_out):
    gate_out[...] = dot(normed_ref[...], gate_w[...])
    grad_out[...] = dot(cot_ref[...], out_w[...], NT)


def beside(normed, gate_weight, cotangent, out_weight):
    tokens, width = normed.shape
    inner = gate_weight.shape[1]
    tile = min(tokens, 256)
    return pl.pallas_call(
        beside_kernel,
        grid=(tokens // tile,),
        in_specs=[rows(tile, width), whole(gate_weight.shape), rows(tile, width), whole(out_weight.shape)],
        out_specs=[rows(tile, inner), rows(tile, inner)],
        out_shape=[jax.ShapeDtypeStruct((tokens, inner), f32), jax.ShapeDtypeStruct((tokens, inner), f32)],
        compiler_params=params(20),
        cost_estimate=cost(6),
    )(normed, gate_weight, cotangent, out_weight)


def convolve(before, here, kernel):
    extended = jnp.concatenate([before, here], axis=0)
    count = here.shape[0]
    first = EDGE - CONV + 1
    summed = kernel[0:1] * extended[first : first + count]
    for k in range(1, CONV):
        summed = summed + kernel[k : k + 1] * extended[first + k : first + k + count]
    return summed


def local_kernel(
    value_ref, state_ref, step_ref, halo_ref, gain_ref, value_w, state_w, value_k, state_k, bias_ref, log_ref,
    conv_out, pre_out, rows_out, spre_out, dt_out, cum_out, cumt_out, held_out, message_out, vhalo_out, shalo_out,
    value_before, state_before, held, total, heads,
):
    b = pl.program_id(0)
    width = value_ref.shape[1]

    @pl.when(b == 0)
    def _():
        normed = norm_rows(halo_ref[...].astype(f32), gain_ref[...])
        value_halo = dot(normed, value_w[...]).astype(bf16)
        state_halo = dot(normed, state_w[...]).astype(bf16)
        vhalo_out[...] = value_halo
        shalo_out[...] = state_halo
        value_before[...] = value_halo.astype(f32)[-EDGE:]
        state_before[...] = state_halo.astype(f32)[-EDGE:]
        held[...] = jnp.zeros(held.shape, f32)
        total[...] = jnp.zeros(total.shape, f32)
        heads[...] = head_map(width)

    dt = jax.nn.softplus(step_ref[...] + repeated(bias_ref[...]))
    decay = -dt * jnp.exp(repeated(log_ref[...]))
    size = value_ref.shape[0]
    lower = (iota((size, size), 0) >= iota((size, size), 1)).astype(f32).astype(bf16)
    cum = exact_dot(lower, decay, NN)
    dt_out[...] = dt
    cum_out[...] = cum
    cumt_out[...] = cum.T[: cumt_out.shape[0]]
    last = cum[size - 1 : size]
    wide = spread(jnp.concatenate([dt, cum], axis=0), heads[...])

    state = state_ref[...].astype(f32)
    spre = convolve(state_before[...], state, state_k[...].astype(f32))
    state_before[...] = state[-EDGE:]
    mixed_rows = spre * sig(spre)
    spre_out[...] = spre
    rows_out[...] = mixed_rows
    b_parts = both_parts(mixed_rows[:, :LANES].T)

    taps = value_k[...].astype(f32)
    held_out[0] = held[...]
    for span in spans(width):
        value = value_ref[:, span].astype(f32)
        pre = convolve(value_before[:, span], value, taps[:, span])
        value_before[:, span] = value[-EDGE:]
        conv = pre * sig(pre)
        pre_out[:, span] = pre
        conv_out[:, span] = conv
        cum_wide = wide[size:, span]
        end = cum_wide[size - 1 : size]
        weighted = conv * wide[:size, span] * jnp.exp(end - cum_wide)
        held[:, span] = jnp.exp(end) * held[:, span] + wide_dot(b_parts, weighted)
        total[:, span] = total[:, span] + end

    @pl.when(b == pl.num_programs(0) - 1)
    def _():
        message_out[:LANES] = held[...]
        message_out[LANES:] = total[...]


def local_states(value_in, state_in, step_raw, halo, pre_gain, input_weight, state_weight, input_kernel, state_kernel, step_bias, decay_log):
    tokens, inner = value_in.shape
    state2 = state_in.shape[1]
    state = state2 // 2
    blocks = tokens // BLOCK
    headrows = 16
    return pl.pallas_call(
        local_kernel,
        grid=(blocks,),
        in_specs=[
            rows(BLOCK, inner),
            rows(BLOCK, state2),
            rows(BLOCK, LANES),
            whole(halo.shape),
            whole(pre_gain.shape),
            whole(input_weight.shape),
            whole(state_weight.shape),
            whole(input_kernel.shape),
            whole(state_kernel.shape),
            whole(step_bias.shape),
            whole(decay_log.shape),
        ],
        out_specs=[
            rows(BLOCK, inner),
            rows(BLOCK, inner),
            rows(BLOCK, state2),
            rows(BLOCK, state2),
            rows(BLOCK, LANES),
            rows(BLOCK, LANES),
            pl.BlockSpec((headrows, BLOCK), lambda b: (0, b)),
            pl.BlockSpec((1, state, inner), lambda b: (b, 0, 0)),
            whole((state + EDGE, inner)),
            whole((halo.shape[0], inner)),
            whole((halo.shape[0], state2)),
        ],
        out_shape=[
            jax.ShapeDtypeStruct((tokens, inner), f32),
            jax.ShapeDtypeStruct((tokens, inner), f32),
            jax.ShapeDtypeStruct((tokens, state2), f32),
            jax.ShapeDtypeStruct((tokens, state2), f32),
            jax.ShapeDtypeStruct((tokens, LANES), f32),
            jax.ShapeDtypeStruct((tokens, LANES), f32),
            jax.ShapeDtypeStruct((headrows, tokens), f32),
            jax.ShapeDtypeStruct((blocks, state, inner), f32),
            jax.ShapeDtypeStruct((state + EDGE, inner), f32),
            jax.ShapeDtypeStruct((halo.shape[0], inner), bf16),
            jax.ShapeDtypeStruct((halo.shape[0], state2), bf16),
        ],
        scratch_shapes=[
            pltpu.VMEM((EDGE, inner), f32),
            pltpu.VMEM((EDGE, state2), f32),
            pltpu.VMEM((state, inner), f32),
            pltpu.VMEM((EDGE, inner), f32),
            pltpu.VMEM((LANES, inner), bf16),
        ],
        compiler_params=params(),
        cost_estimate=cost(10),
    )(value_in, state_in, step_raw, halo, pre_gain, input_weight, state_weight, input_kernel, state_kernel, step_bias, decay_log)


def inner_kernel(heads_count, conv_ref, dt_ref, rows_ref, cum_ref, cumt_ref, skip_ref, out_ref, heads):
    size, width = conv_ref.shape

    @pl.when(pl.program_id(0) == 0)
    def _():
        heads[...] = head_map(width)

    skip = jnp.broadcast_to(repeated(skip_ref[...]), (EDGE, LANES))
    wide = spread(jnp.concatenate([dt_ref[...], skip], axis=0), heads[...])
    scores = dot3(rows_ref[:, LANES:], rows_ref[:, :LANES], NT)
    causal = iota((size, size), 0) >= iota((size, size), 1)
    left = iota((size, LANES), 1) < HEAD_DIM
    cum = cum_ref[...]
    cumt = cumt_ref[...]
    for pair, span in enumerate(spans(width)):
        conv = conv_ref[:, span]
        mixes = []
        for h in (2 * pair, 2 * pair + 1):
            gap = cum[:, h : h + 1] - cumt[h : h + 1, :]
            mixes.append(both_parts(jnp.exp(jnp.where(causal, gap, -1e30)) * scores))
        both = wide_dot(jnp.concatenate(mixes, axis=0), conv * wide[:size, span])
        out_ref[:, span] = jnp.where(left, both[:size], both[size:]) + wide[size : size + 1, span] * conv


def inner_forward(heads_count, conv, dt, state_rows, cum, cumt, skip_gain):
    tokens, inner = conv.shape
    return pl.pallas_call(
        functools.partial(inner_kernel, heads_count),
        grid=(tokens // BLOCK,),
        in_specs=[
            rows(BLOCK, inner),
            rows(BLOCK, LANES),
            rows(BLOCK, state_rows.shape[1]),
            rows(BLOCK, LANES),
            pl.BlockSpec((cumt.shape[0], BLOCK), lambda b: (0, b)),
            whole(skip_gain.shape),
        ],
        out_specs=rows(BLOCK, inner),
        out_shape=jax.ShapeDtypeStruct((tokens, inner), f32),
        scratch_shapes=[pltpu.VMEM((LANES, inner), bf16)],
        compiler_params=params(12),
        cost_estimate=cost(6),
    )(conv, dt, state_rows, cum, cumt, skip_gain)


def combine_kernel(count, intra_ref, rows_ref, cum_ref, held_ref, own_ref, *refs):
    message_refs, (gate_ref, grad_ref, gain_ref, mixed_out, sums_out, held_out, end_out, start, total, heads) = refs[:count], refs[count:]
    b = pl.program_id(0)
    size, width = intra_ref.shape
    state = held_ref.shape[1]

    @pl.when(b == 0)
    def _():
        heads[...] = head_map(width)
        total[...] = jnp.zeros(total.shape, f32)
        for span in spans(width):
            entering = jnp.zeros((state, LANES), f32)
            passed = jnp.zeros((EDGE, LANES), f32)
            for ref in message_refs:
                entering = entering + jnp.exp(passed[0:1]) * ref[:state, span]
                passed = passed + ref[state:, span]
            start[:, span] = entering
            end_out[:, span] = own_ref[:state, span] + jnp.exp(own_ref[state : state + 1, span]) * entering

    cum_wide = spread(cum_ref[...], heads[...])
    c_parts = both_parts(rows_ref[:, LANES:])
    square = jnp.zeros((size, LANES), f32)
    inner = jnp.zeros((size, LANES), f32)
    for span in spans(width):
        held = held_ref[0, :, span] + jnp.exp(total[0:1, span]) * start[:, span]
        held_out[0, :, span] = held
        cum_part = cum_wide[:, span]
        total[:, span] = total[:, span] + cum_part[size - 1 : size]
        mixed = intra_ref[:, span] + jnp.exp(cum_part) * wide_dot(c_parts, held)
        mixed_out[:, span] = mixed
        gate = gate_ref[:, span]
        gated = mixed * (gate * sig(gate))
        square = square + gated * gated
        inner = inner + grad_ref[:, span] * gain_ref[:, span] * gated
    ones = jnp.ones((EDGE, LANES), bf16)
    square = exact_dot(ones, square, NT)
    inner = exact_dot(ones, inner, NT)
    sums_out[...] = jnp.where(iota(square.shape, 0) == 0, square, inner)


def combine(intra, state_rows, cum, held, own, messages, gate_in, grad_normed, norm_gain):
    tokens, inner = intra.shape
    blocks, state, _ = held.shape
    state_block = pl.BlockSpec((1, state, inner), lambda b: (b, 0, 0))
    return pl.pallas_call(
        functools.partial(combine_kernel, len(messages)),
        grid=(blocks,),
        in_specs=[
            rows(BLOCK, inner),
            rows(BLOCK, state_rows.shape[1]),
            rows(BLOCK, LANES),
            state_block,
            whole(own.shape),
            *[whole(own.shape) for _ in messages],
            rows(BLOCK, inner),
            rows(BLOCK, inner),
            whole(norm_gain.shape),
        ],
        out_specs=[
            rows(BLOCK, inner),
            pl.BlockSpec((EDGE, BLOCK), lambda b: (0, b)),
            state_block,
            whole((state, inner)),
        ],
        out_shape=[
            jax.ShapeDtypeStruct((tokens, inner), f32),
            jax.ShapeDtypeStruct((EDGE, tokens), f32),
            jax.ShapeDtypeStruct(held.shape, f32),
            jax.ShapeDtypeStruct((state, inner), f32),
        ],
        scratch_shapes=[pltpu.VMEM((state, inner), f32), pltpu.VMEM((EDGE, inner), f32), pltpu.VMEM((LANES, inner), bf16)],
        compiler_params=params(),
        cost_estimate=cost(5),
    )(intra, state_rows, cum, held, own, *messages, gate_in, grad_normed, norm_gain)


def column(row):
    return jnp.broadcast_to(row, (LANES, row.shape[1])).T


def gate_back_kernel(count, inner_total, mixed_ref, gate_ref, grad_ref, rows_ref, cum_ref, gain_ref, *refs):
    sums_refs, (normed_out, gate_out, dmix_out, later_out, message_out, gain_out, later, total, heads) = refs[:count], refs[count:]
    b = pl.program_id(0)
    size, width = mixed_ref.shape

    @pl.when(b == 0)
    def _():
        later[...] = jnp.zeros(later.shape, f32)
        total[...] = jnp.zeros(total.shape, f32)
        gain_out[...] = jnp.zeros(gain_out.shape, f32)
        heads[...] = head_map(width)

    sums = sums_refs[0][...]
    for ref in sums_refs[1:]:
        sums = sums + ref[...]
    rms_row = lax.rsqrt(sums[0:1] / inner_total + epsilon)
    pull_row = rms_row * rms_row * rms_row * sums[1:2] / inner_total
    rms = column(rms_row)
    pull = column(pull_row)
    cum_wide = spread(cum_ref[...], heads[...])
    c_parts = both_parts(rows_ref[:, LANES:].T)
    later_out[0] = later[...]
    for span in spans(width):
        gain = gain_ref[:, span]
        gate = gate_ref[:, span]
        mixed = mixed_ref[:, span]
        grad = grad_ref[:, span]
        gate_sig = sig(gate)
        gate_silu = gate * gate_sig
        gated = mixed * gate_silu
        normed_out[:, span] = (gated * rms * gain).astype(bf16)
        gain_out[:, span] = gain_out[:, span] + by_eights(grad * gated * rms)
        grad_gated = rms * gain * grad - gated * pull
        gate_out[:, span] = (grad_gated * mixed * gate_sig * (1.0 + gate * (1.0 - gate_sig))).astype(bf16)
        grad_mixed = grad_gated * gate_silu
        dmix_out[:, span] = grad_mixed
        cum_part = cum_wide[:, span]
        end = cum_part[size - 1 : size]
        later[:, span] = jnp.exp(end) * later[:, span] + wide_dot(c_parts, jnp.exp(cum_part) * grad_mixed)
        total[:, span] = total[:, span] + end

    @pl.when(b == pl.num_programs(0) - 1)
    def _():
        message_out[:LANES] = later[...]
        message_out[LANES:] = total[...]


def gate_back(mixed, gate_in, grad_normed, state_rows, cum, norm_gain, sums, inner_total):
    tokens, inner = mixed.shape
    blocks = tokens // BLOCK
    state = state_rows.shape[1] // 2
    return pl.pallas_call(
        functools.partial(gate_back_kernel, len(sums), inner_total),
        grid=(blocks,),
        in_specs=[
            rows(BLOCK, inner, blocks),
            rows(BLOCK, inner, blocks),
            rows(BLOCK, inner, blocks),
            rows(BLOCK, 2 * state, blocks),
            rows(BLOCK, LANES, blocks),
            whole(norm_gain.shape),
            *[pl.BlockSpec((EDGE, BLOCK), lambda b: (0, blocks - 1 - b)) for _ in sums],
        ],
        out_specs=[
            rows(BLOCK, inner, blocks),
            rows(BLOCK, inner, blocks),
            rows(BLOCK, inner, blocks),
            pl.BlockSpec((1, state, inner), lambda b: (blocks - 1 - b, 0, 0)),
            whole((state + EDGE, inner)),
            whole((EDGE, inner)),
        ],
        out_shape=[
            jax.ShapeDtypeStruct((tokens, inner), bf16),
            jax.ShapeDtypeStruct((tokens, inner), bf16),
            jax.ShapeDtypeStruct((tokens, inner), f32),
            jax.ShapeDtypeStruct((blocks, state, inner), f32),
            jax.ShapeDtypeStruct((state + EDGE, inner), f32),
            jax.ShapeDtypeStruct((EDGE, inner), f32),
        ],
        scratch_shapes=[pltpu.VMEM((state, inner), f32), pltpu.VMEM((EDGE, inner), f32), pltpu.VMEM((LANES, inner), bf16)],
        compiler_params=params(),
        cost_estimate=cost(7),
    )(mixed, gate_in, grad_normed, state_rows, cum, norm_gain, *sums)


def inner_back_kernel(heads_count, conv_ref, dt_ref, rows_ref, cum_ref, cumt_ref, dmix_ref, driven_out, rows_out, heads):
    size, width = conv_ref.shape

    @pl.when(pl.program_id(0) == 0)
    def _():
        heads[...] = head_map(width)

    dt_wide = spread(dt_ref[...], heads[...])
    b_rows = rows_ref[:, :LANES]
    c_rows = rows_ref[:, LANES:]
    scores = dot3(b_rows, c_rows, NT)
    causal = iota((size, size), 1) >= iota((size, size), 0)
    left = iota((size, LANES), 1) < HEAD_DIM
    cum = cum_ref[...]
    cumt = cumt_ref[...]
    score_grad = jnp.zeros((size, size), f32)
    for pair, span in enumerate(spans(width)):
        dmix_high, dmix_low = split2(dmix_ref[:, span])
        across = jnp.concatenate([dmix_high, dmix_low], axis=1)
        right_side = jnp.concatenate([across, across], axis=0)
        taking = jnp.concatenate([dmix_high, dmix_high, dmix_low], axis=1)
        driven = conv_ref[:, span] * dt_wide[:, span]
        owns = []
        for mine in (left, jnp.logical_not(left)):
            own_high, own_low = split2(jnp.where(mine, driven, 0.0))
            owns.append(jnp.concatenate([own_high, own_low, own_high], axis=1))
        mix_grads = dot(jnp.concatenate(owns, axis=0), taking, NT)
        mixes = []
        for side in range(2):
            h = 2 * pair + side
            gap = cumt[h : h + 1, :] - cum[:, h : h + 1]
            kept = jnp.exp(jnp.where(causal, gap, -1e30))
            score_grad = score_grad + mix_grads[side * size : (side + 1) * size] * kept
            mixes.append(both_parts(kept * scores))
        both = fold(dot(jnp.concatenate(mixes, axis=0), right_side))
        driven_out[:, span] = jnp.where(left, both[:size], both[size:])
    rows_out[:, :LANES] = dot3(score_grad, c_rows, NN)
    rows_out[:, LANES:] = dot3(score_grad, b_rows, TN)


def inner_back(heads_count, conv, dt, state_rows, cum, cumt, grad_mixed):
    tokens, inner = conv.shape
    return pl.pallas_call(
        functools.partial(inner_back_kernel, heads_count),
        grid=(tokens // BLOCK,),
        in_specs=[
            rows(BLOCK, inner),
            rows(BLOCK, LANES),
            rows(BLOCK, state_rows.shape[1]),
            rows(BLOCK, LANES),
            pl.BlockSpec((cumt.shape[0], BLOCK), lambda b: (0, b)),
            rows(BLOCK, inner),
        ],
        out_specs=[rows(BLOCK, inner), rows(BLOCK, state_rows.shape[1])],
        out_shape=[
            jax.ShapeDtypeStruct((tokens, inner), f32),
            jax.ShapeDtypeStruct(state_rows.shape, f32),
        ],
        scratch_shapes=[pltpu.VMEM((LANES, inner), bf16)],
        compiler_params=params(16),
        cost_estimate=cost(0),
    )(conv, dt, state_rows, cum, cumt, grad_mixed)


def stacked(high, low):
    return jnp.concatenate([jnp.concatenate([high, high], axis=1), jnp.concatenate([low, low], axis=1)], axis=0)


def rows_back_kernel(
    count, drows_ref, dmix_ref, conv_ref, dt_ref, cum_ref, rows_ref, held_ref, later_ref, *refs
):
    message_refs = refs[:count]
    spre_ref, grad_rows_out, later_out, first_out, entering, total, heads = refs[count:]
    b = pl.program_id(0)
    size, width = conv_ref.shape
    state = held_ref.shape[1]

    @pl.when(b == 0)
    def _():
        heads[...] = head_map(width)
        for span in spans(width):
            coming = jnp.zeros((state, LANES), f32)
            passed = jnp.zeros((EDGE, LANES), f32)
            for ref in message_refs:
                coming = coming + jnp.exp(passed[0:1]) * ref[:state, span]
                passed = passed + ref[state:, span]
            entering[:, span] = coming
        total[...] = jnp.zeros(total.shape, f32)

    wide = spread(jnp.concatenate([cum_ref[...], dt_ref[...]], axis=0), heads[...])
    toward_b, toward_c, laters, helds = [], [], [], []
    for span in spans(width):
        cum_part = wide[:size, span]
        end = cum_part[size - 1 : size]
        later = later_ref[0, :, span] + jnp.exp(total[0:1, span]) * entering[:, span]
        later_out[0, :, span] = later
        total[:, span] = total[:, span] + end
        driven = conv_ref[:, span] * wide[size:, span]
        toward_b.append(both_parts(jnp.exp(end - cum_part) * driven))
        laters.append(stacked(*split2(later)))
        toward_c.append(both_parts(jnp.exp(cum_part) * dmix_ref[:, span]))
        helds.append(stacked(*split2(held_ref[0, :, span])))
    side = lambda parts: jnp.concatenate(parts, axis=1)
    grad_rows_out[:, :LANES] = drows_ref[:, :LANES] + fold(dot(side(toward_b), side(laters), NT))
    grad_rows_out[:, LANES:] = drows_ref[:, LANES:] + fold(dot(side(toward_c), side(helds), NT))

    @pl.when(b == pl.num_programs(0) - 1)
    def _():
        first_out[:, : 2 * LANES] = grad_rows_out[:EDGE]
        first_out[:, 2 * LANES :] = spre_ref[...]


def rows_back(grad_rows, grad_mixed, conv, dt, cum, state_rows, held, later, messages, spre):
    tokens, inner = conv.shape
    blocks, state, _ = held.shape
    state_block = pl.BlockSpec((1, state, inner), lambda b: (blocks - 1 - b, 0, 0))
    wide = rows(BLOCK, inner, blocks)
    narrow = rows(BLOCK, LANES, blocks)
    both = rows(BLOCK, 2 * state, blocks)
    return pl.pallas_call(
        functools.partial(rows_back_kernel, len(messages)),
        grid=(blocks,),
        in_specs=[
            both, wide, wide, narrow, narrow, both, state_block, state_block,
            *[whole(m.shape) for m in messages],
            pl.BlockSpec((EDGE, 2 * state), lambda b: (0, 0)),
        ],
        out_specs=[both, state_block, whole((EDGE, 4 * state))],
        out_shape=[
            jax.ShapeDtypeStruct((tokens, 2 * state), f32),
            jax.ShapeDtypeStruct(held.shape, f32),
            jax.ShapeDtypeStruct((EDGE, 4 * state), f32),
        ],
        scratch_shapes=[pltpu.VMEM((state, inner), f32), pltpu.VMEM((EDGE, inner), f32), pltpu.VMEM((LANES, inner), bf16)],
        compiler_params=params(24),
        cost_estimate=cost(0),
    )(grad_rows, grad_mixed, conv, dt, cum, state_rows, held, later, *messages, spre)


def finish_kernel(
    blocks, driven_ref, dmix_ref, mixed_ref, pre_ref, value_ref, dt_ref, cum_ref, step_ref, rows_ref, held_ref, end_ref, later_ref,
    vhalo_ref, kernel_ref, skip_ref, bias_ref, log_ref,
    grad_value_out, grad_step_out, last_out, first_out, kernel_out, small_out,
    held_next, pre_next, skip_sum, heads, kernel_sum, heads_t, edge_rows,
):
    b = pl.program_id(0)
    size, width = mixed_ref.shape
    state = held_ref.shape[1]
    final = b == blocks - 1

    @pl.when(b == 0)
    def _():
        heads[...] = head_map(width)
        heads_t[...] = (iota((width, LANES), 1) == iota((width, LANES), 0) // HEAD_DIM).astype(f32).astype(bf16)
        held_next[...] = end_ref[...]
        pre_next[...] = jnp.zeros(pre_next.shape, f32)
        kernel_sum[...] = jnp.zeros(kernel_sum.shape, f32)
        small_out[...] = jnp.zeros(small_out.shape, f32)
        skip_sum[...] = jnp.zeros(skip_sum.shape, f32)

    dt = dt_ref[...]
    cum = cum_ref[...]
    skip_row = jnp.broadcast_to(repeated(skip_ref[...]), (EDGE, LANES))
    wide = spread(jnp.concatenate([cum, dt, skip_row], axis=0), heads[...])
    b_parts = both_parts(rows_ref[:, :LANES])
    taps = kernel_ref[...].astype(f32)
    levels, throughs, boundaries = [], [], []
    for span in spans(width):
        cum_part = wide[:size, span]
        dt_wide = wide[size : 2 * size, span]
        skip = wide[2 * size : 2 * size + 1, span]
        end = cum_part[size - 1 : size]
        later = later_ref[0, :, span]
        held = held_ref[0, :, span]
        tail = jnp.exp(end - cum_part)
        dmix = dmix_ref[:, span]
        pre = pre_ref[:, span]
        pre_sig = sig(pre)
        conv = pre * pre_sig
        driven = conv * dt_wide
        later_high, later_low = split2(later)
        across = jnp.concatenate([later_high, later_low], axis=1)
        ddriven = driven_ref[:, span] + tail * fold(dot(b_parts, jnp.concatenate([across, across], axis=0)))
        skip_sum[:, span] = skip_sum[:, span] + by_eights(dmix * conv)
        levels.append(both_parts(dmix * (mixed_ref[:, span] - skip * conv) - driven * ddriven))
        throughs.append(both_parts(ddriven * conv))
        boundaries.append(both_parts(by_eights(later * held_next[:, span])))
        held_next[:, span] = held

        dpre = (ddriven * dt_wide + skip * dmix) * (pre_sig * (1.0 + pre * (1.0 - pre_sig)))
        extended = jnp.concatenate([dpre, pre_next[:, span]], axis=0)
        pre_next[:, span] = dpre[:EDGE]
        value = value_ref[:, span].astype(f32)
        dvalue = jnp.zeros((size, LANES), f32)
        for k in range(CONV):
            shifted = extended[CONV - 1 - k : CONV - 1 - k + size]
            dvalue = dvalue + taps[k : k + 1, span] * shifted
            kernel_sum[k, :, span] = kernel_sum[k, :, span] + by_eights(value * shifted)
        grad_value_out[:, span] = dvalue.astype(bf16)
        edge_rows[:, span] = dvalue[-2 * EDGE :]

    side = lambda parts: jnp.concatenate(parts, axis=1)
    picks = jnp.concatenate([heads_t[span] for span in spans(width) for _ in range(2)], axis=0)
    reduced = dot(jnp.concatenate([side(levels), side(throughs), side(boundaries)], axis=0), picks)
    level, through, boundary = reduced[:size], reduced[size : 2 * size], reduced[2 * size :]
    boundary = jnp.sum(boundary, axis=0, keepdims=True)
    upper = (iota((size, size), 1) >= iota((size, size), 0)).astype(f32).astype(bf16)
    ddecay = exact_dot(upper, level, NN) + boundary
    rate = jnp.exp(repeated(log_ref[...]))
    dstep = (through - ddecay * rate) * sig(step_ref[...] + repeated(bias_ref[...]))
    grad_step_out[...] = dstep[:, : grad_step_out.shape[1]].astype(bf16)
    small_out[1:2] = small_out[1:2] + jnp.sum(dstep, axis=0, keepdims=True)
    small_out[2:3] = small_out[2:3] + jnp.sum(-ddecay * dt * rate, axis=0, keepdims=True)

    @pl.when(b == 0)
    def _():
        last_out[...] = edge_rows[...]

    @pl.when(final)
    def _():
        first = pre_next[...]
        first_out[...] = first
        ahead = jnp.concatenate([jnp.zeros((EDGE, width), f32), first], axis=0)
        halo = vhalo_ref[...].astype(f32)[-EDGE:]
        kernel_out[...] = jnp.zeros(kernel_out.shape, f32)
        for k in range(CONV):
            shifted = ahead[CONV - 1 - k : CONV - 1 - k + EDGE]
            kernel_out[k : k + 1] = jnp.sum(kernel_sum[k] + halo * shifted, axis=0, keepdims=True)
        high, middle, low = split3(skip_sum[...])
        summed = dot(high, heads[...], NT) + (dot(middle, heads[...], NT) + dot(low, heads[...], NT))
        small_out[0:1] = jnp.sum(summed, axis=0, keepdims=True)


def finish(plan, count, wide_operands, grad_driven, grad_mixed, mixed, pre, value_in, dt, cum, step_raw, state_rows, held, end_state, later,
           vhalo, input_kernel, skip_gain, step_bias, decay_log):
    tokens, inner = mixed.shape
    blocks, state, _ = held.shape
    head_count = skip_gain.shape[1]
    width = wide_operands[0].shape[1]
    tile = width // count
    at = lambda b: jnp.maximum(blocks - 1 - b, 0)
    by_rows = lambda cols: pl.BlockSpec((BLOCK, cols), lambda b, plan: (at(b), 0))
    state_block = pl.BlockSpec((1, state, inner), lambda b, plan: (at(b), 0, 0))
    moving = pl.BlockSpec((tokens, tile), lambda b, plan: (0, jnp.bitwise_xor(plan[1], jnp.maximum(b - blocks, 0))))
    still = pl.BlockSpec((tokens, tile), lambda b, plan: (0, plan[0]))
    wide, narrow = by_rows(inner), by_rows(LANES)
    operands = (grad_driven, grad_mixed, mixed, pre, value_in, dt, cum, step_raw, state_rows, held, end_state, later,
                vhalo, input_kernel, skip_gain, step_bias, decay_log)
    outs = [
        (wide, jax.ShapeDtypeStruct((tokens, inner), bf16)),
        (by_rows(head_count), jax.ShapeDtypeStruct((tokens, head_count), bf16)),
    ]
    for shape in ((2 * EDGE, inner), (EDGE, inner), (EDGE, inner), (EDGE, LANES), *[(2 * tile, tile)] * 4):
        outs.append((pl.BlockSpec(shape, lambda b, plan: (0, 0)), jax.ShapeDtypeStruct(shape, f32)))

    def body(plan_ref, *refs):
        b = pl.program_id(0)
        ins, wide_ins, rest = refs[:17], refs[17:25], refs[25:]

        @pl.when(b < blocks)
        def _():
            finish_kernel(blocks, *ins, *rest[:6], *rest[10:])

        @pl.when(b >= blocks)
        def _():
            wide_weights_kernel(b - blocks, *wide_ins, *rest[6:10])

    return scalar_call(
        body, plan, (*operands, *wide_operands),
        [wide, wide, wide, wide, wide, narrow, narrow, narrow, by_rows(2 * state), state_block, all_of(end_state), state_block,
         *[all_of(a) for a in operands[12:]], moving, moving, still, still, still, still, moving, moving],
        [o[0] for o in outs], [o[1] for o in outs], grid=(blocks + count,),
        scratch=[
            pltpu.VMEM((state, inner), f32),
            pltpu.VMEM((EDGE, inner), f32),
            pltpu.VMEM((EDGE, inner), f32),
            pltpu.VMEM((LANES, inner), bf16),
            pltpu.VMEM((CONV, EDGE, inner), f32),
            pltpu.VMEM((inner, LANES), bf16),
            pltpu.VMEM((2 * EDGE, inner), f32),
        ],
        limit=56, micros=0,
    )


def from_before(value, axis, by=1):
    count = lax.axis_size(axis)
    return lax.ppermute(value, axis, [(i, i + by) for i in range(count - by)])


def from_after(value, axis, by=1):
    count = lax.axis_size(axis)
    return lax.ppermute(value, axis, [(i + by, i) for i in range(count - by)])


def from_all(value, axis):
    count = lax.axis_size(axis)
    return [lax.ppermute(value, axis, [(i, (i + by) % count) for i in range(count)]) for by in range(1, count)]


def after(first, then):
    return lax.optimization_barrier((first, then))[1]


def swapped(value, axis, flip):
    return lax.ppermute(value, axis, [(i, i ^ flip) for i in range(lax.axis_size(axis))])


def own_part(array, axis_name, dim):
    size = array.shape[dim] // lax.axis_size(axis_name)
    return lax.dynamic_slice_in_dim(array, lax.axis_index(axis_name) * size, size, dim)


def first_kernel(plan_ref, part_ref, out_ref):
    out_ref[...] = part_ref[0].astype(bf16)


def line_first(parts, axis):
    count, tokens, width = parts.shape
    plan = jnp.where(lax.axis_index(axis) == 0, count - 1, 0).astype(jnp.int32).reshape(1)
    tile = min(tokens, 512)
    sent = pl.pallas_call(
        first_kernel,
        grid_spec=pltpu.PrefetchScalarGridSpec(
            num_scalar_prefetch=1,
            grid=(tokens // tile,),
            in_specs=[pl.BlockSpec((1, tile, width), lambda b, plan: (plan[0], b, 0))],
            out_specs=pl.BlockSpec((tile, width), lambda b, plan: (b, 0)),
        ),
        out_shape=jax.ShapeDtypeStruct((tokens, width), bf16),
        compiler_params=params(56),
        cost_estimate=cost(0),
    )(plan, parts)
    return sent


def line_step(parts, step, arrived, axis):
    count, tokens, width = parts.shape
    place = lax.axis_index(axis)
    plan = jnp.clip(jnp.stack([count - step + place, step - count + place]), 0, count - 1).astype(jnp.int32)
    if step == 2:
        arrived = [arrived, arrived]

    def body(plan_ref, up_ref, down_ref, up_in, down_in, up_out, down_out):
        up, down = up_in[...].astype(f32), down_in[...].astype(f32)
        if step == 2:
            up = jnp.where(plan_ref[2] == 1, up, 0.0)
            down = jnp.where(plan_ref[2] == count - 2, down, 0.0)
        up_out[...] = (up_ref[0] + up).astype(bf16)
        down_out[...] = (down_ref[0] + down).astype(bf16)

    tile = min(tokens, 512)
    block = pl.BlockSpec((tile, width), lambda b, plan: (b, 0))
    up, down = pl.pallas_call(
        body,
        grid_spec=pltpu.PrefetchScalarGridSpec(
            num_scalar_prefetch=1,
            grid=(tokens // tile,),
            in_specs=[
                pl.BlockSpec((1, tile, width), lambda b, plan: (plan[0], b, 0)),
                pl.BlockSpec((1, tile, width), lambda b, plan: (plan[1], b, 0)),
                block,
                block,
            ],
            out_specs=[block, block],
        ),
        out_shape=[jax.ShapeDtypeStruct((tokens, width), bf16)] * 2,
        compiler_params=params(56),
        cost_estimate=cost(0),
    )(jnp.concatenate([plan, place.astype(jnp.int32).reshape(1)]), parts, parts, *arrived)
    return (up, down), [
        lax.ppermute(up, axis, [(k, k + 1) for k in range(step)]),
        lax.ppermute(down, axis, [(count - 1 - k, count - 2 - k) for k in range(step)]),
    ]


def input_kernel_body(
    pieces, plan_ref, gate_ref, value_ref, narrow_ref, x_ref, gain_ref, gate_w, value_w, state_w, step_w, part_out, row_out, col_out, narrow_w
):
    b = pl.program_id(0)
    size = value_ref.shape[0]

    @pl.when(b == 0)
    def _():
        col_out[...] = jnp.zeros(col_out.shape, f32)
        state2, steps = state_w.shape[1], step_w.shape[0]
        mine = take_columns(plan_ref[0], pieces, state2)
        beside = (iota((steps, LANES), 0) + state2 // pieces == iota((steps, LANES), 1)).astype(f32).astype(bf16)
        narrow_w[...] = (dot(state_w[...], mine) + dot(step_w[...], beside, TN)).astype(bf16)

    gate = gate_ref[...]
    value = value_ref[...]
    narrow = narrow_ref[...]
    x = x_ref[...].astype(f32)
    scaling = lax.rsqrt(jnp.mean(x * x, axis=-1, keepdims=True) + epsilon)
    part = x.shape[1] // pieces
    row = jnp.zeros((size, LANES), f32)
    for j in range(pieces):
        span = slice(j * part, (j + 1) * part)
        partial = dot(gate, gate_w[span, :], NT) + dot(value, value_w[span, :], NT) + dot(narrow, narrow_w[span, :], NT)
        part_out[j] = partial
        pulled = partial * x[:, span]
        gained = pulled * gain_ref[:, span]
        for inside in spans(part):
            row = row + gained[:, inside]
        col_out[:, span] = col_out[:, span] + by_eights(pulled * scaling)
    row_out[...] = exact_dot(jnp.ones((EDGE, LANES), bf16), row, NT)


def scalar_call(body, plan, operands, in_specs, out_specs, out_shape, grid=(1,), scratch=(), limit=16, micros=2):
    return pl.pallas_call(
        body,
        grid_spec=pltpu.PrefetchScalarGridSpec(
            num_scalar_prefetch=1, grid=grid, in_specs=in_specs, out_specs=out_specs, scratch_shapes=list(scratch)
        ),
        out_shape=out_shape,
        compiler_params=pltpu.CompilerParams(dimension_semantics=("arbitrary",) * len(grid), vmem_limit_bytes=limit * 1024 * 1024),
        cost_estimate=cost(micros),
    )(plan, *operands)


def all_of(a):
    return pl.BlockSpec(a.shape, lambda *_: (0,) * len(a.shape))


def take_columns(at, count, width):
    part = width // count
    lane = iota((width, LANES), 1)
    return ((iota((width, LANES), 0) == lane + at * part) & (lane < part)).astype(f32).astype(bf16)


def extended_rows(x, beyond):
    return jnp.concatenate([x, beyond, jnp.zeros((EDGE, x.shape[1]), f32)], axis=0)


def pieces_kernel(count, plan_ref, rows_ref, ahead_ref, *outs):
    tokens, state2 = rows_ref.shape
    extended = extended_rows(rows_ref[...], ahead_ref[:, :state2])
    size = extended.shape[0] // 2
    picks = [take_columns(lax.rem(plan_ref[0] + k, count), count, state2) for k in range(count)]
    none = jnp.zeros((state2, LANES // 2), bf16)
    half = LANES // 2
    upper = jnp.concatenate([jnp.concatenate([p[:, :half], none], axis=1) for p in picks], axis=1)
    lower = jnp.concatenate([jnp.concatenate([none, p[:, :half]], axis=1) for p in picks], axis=1)
    both = dot_exact(extended[:size], upper) + dot_exact(extended[size:], lower)
    for k, out in enumerate(outs):
        out[...] = both[:, k * LANES : (k + 1) * LANES]


def dot_exact(x, ones):
    high, middle, low = split3(x)
    return dot(high, ones) + (dot(middle, ones) + dot(low, ones))


def pieces_of(place, count, grad_rows, ahead):
    tokens, state2 = grad_rows.shape
    shape = jax.ShapeDtypeStruct((tokens // 2 + EDGE, LANES), f32)
    return scalar_call(
        functools.partial(pieces_kernel, count), place, (grad_rows, ahead), [all_of(grad_rows), all_of(ahead)],
        [all_of(shape)] * count, [shape] * count, limit=12, micros=0,
    )


def complete_kernel(ahead_ref, last_ref, taps_ref, value_ref, out_ref):
    fixed = last_ref[...]
    taps = taps_ref[...].astype(f32)
    extended = jnp.concatenate([jnp.zeros(last_ref.shape, f32), ahead_ref[...]], axis=0)
    for k in range(CONV):
        fixed = fixed + taps[k : k + 1] * extended[CONV - 1 - k : CONV - 1 - k + last_ref.shape[0]]
    out_ref[...] = fixed.astype(bf16)


def complete(ahead, last_rows, taps, grad_value):
    tokens, inner = grad_value.shape
    size = last_rows.shape[0]
    final_rows = pl.BlockSpec((size, inner), lambda b: (tokens // size - 1, 0))
    return pl.pallas_call(
        complete_kernel,
        grid=(1,),
        in_specs=[whole(ahead.shape), whole(last_rows.shape), whole(taps.shape), final_rows],
        out_specs=final_rows,
        out_shape=jax.ShapeDtypeStruct(grad_value.shape, bf16),
        input_output_aliases={3: 0},
        compiler_params=params(4),
        cost_estimate=cost(0),
    )(ahead, last_rows, taps, grad_value)


def three_parts(x):
    return jnp.concatenate(split3(x), axis=0)


def three_sum(parts):
    size = parts.shape[0] // 3
    parts = parts.astype(f32)
    return parts[:size] + (parts[size : 2 * size] + parts[2 * size :])


PACK = 16
SMALL = 48


def state_kernel_body(count, plan_ref, *refs):
    grads = refs[:count]
    spre_ref, input_ref, halo_ref, ahead_ref, taps_ref, step_ref, out_ref, taps_out = refs[count:]
    tokens, state2 = spre_ref.shape
    part = state2 // count
    pick = take_columns(plan_ref[0], count, state2)
    total = grads[0][...]
    for ref in grads[1:]:
        total = total + ref[...]
    total = jnp.concatenate([total, pltpu.roll(total, LANES // 2, 1)], axis=0)
    total = jnp.where(iota(total.shape, 1) < part, total, 0.0)
    pre = dot_exact(extended_rows(spre_ref[...], ahead_ref[:, state2:]), pick)
    s = sig(pre)
    through = total * (s * (1.0 + pre * (1.0 - s)))
    taps = dot(taps_ref[...], pick)
    inputs = dot(jnp.concatenate([halo_ref[...], input_ref[...]], axis=0), pick)
    steps = step_ref.shape[1]
    place = (iota((steps, LANES), 0) + part == iota((steps, LANES), 1)).astype(f32).astype(bf16)
    grad = dot(step_ref[...], place)
    own = through[:tokens]
    first = halo_ref.shape[0] - CONV + 1
    taps_out[...] = jnp.zeros(taps_out.shape, f32)
    for k in range(CONV):
        grad = grad + taps[k : k + 1] * through[CONV - 1 - k : CONV - 1 - k + tokens]
        taps_out[k : k + 1] = jnp.sum(own * inputs[first + k : first + k + tokens], axis=0, keepdims=True)
    out_ref[...] = grad.astype(bf16)


def state_back(place, grads, spre, state_in, halo, ahead, taps, grad_step):
    count = len(grads)
    tokens = spre.shape[0]
    shapes = [jax.ShapeDtypeStruct((tokens, LANES), bf16), jax.ShapeDtypeStruct((EDGE, LANES), f32)]
    operands = (*grads, spre, state_in, halo, ahead, taps, grad_step)
    return scalar_call(
        functools.partial(state_kernel_body, count), place, operands, [all_of(a) for a in operands],
        [all_of(a) for a in shapes], shapes, limit=16, micros=0,
    )


def sums_kernel(count, plan_ref, row_ref, col_ref, taps_ref, out_ref):
    state2 = out_ref.shape[1]
    tokens, width = row_ref.shape[1], col_ref.shape[1]
    packed = [row_ref[:1, i : i + state2] for i in range(0, tokens, state2)]
    col = jnp.sum(col_ref[...], axis=0, keepdims=True)
    packed += [col[:, i : i + state2] for i in range(0, width, state2)]
    high, middle, low = split3(taps_ref[:CONV])
    pick = take_columns(plan_ref[0], count, state2)
    packed.append(dot(high, pick, NT) + (dot(middle, pick, NT) + dot(low, pick, NT)))
    packed = jnp.concatenate(packed, axis=0)
    out_ref[...] = jnp.concatenate([packed, jnp.zeros((PACK - packed.shape[0], state2), f32)], axis=0)


def sums_of(place, count, row_sums, col_sums, taps_grad, state2):
    shape = jax.ShapeDtypeStruct((PACK, state2), f32)
    operands = (row_sums, col_sums, taps_grad)
    return scalar_call(
        functools.partial(sums_kernel, count), place, operands, [all_of(a) for a in operands], all_of(shape), shape,
        limit=8, micros=0,
    )


def small_kernel(count, tokens, plan_ref, *refs):
    parts, (kernel_ref, gain_ref, small_ref, sums_out, out_ref) = refs[:count], refs[count:]
    sums = parts[0][...]
    for ref in parts[1:]:
        sums = sums + ref[...]
    sums_out[...] = sums
    state2 = sums.shape[1]
    wide = state2 // LANES
    inner = kernel_ref.shape[1]
    rows_of = [kernel_ref[k : k + 1, span] for k in range(CONV) for span in spans(inner)]
    gain = jnp.sum(gain_ref[...], axis=0, keepdims=True)
    rows_of += [gain[:, span] for span in spans(inner)]
    rows_of += [small_ref[i : i + 1] for i in range(3)]
    first = tokens // state2
    last = PACK - 2 - CONV
    cols = [sums[r : r + 1, i * LANES : (i + 1) * LANES] for r in range(first, last) for i in range(wide)]
    quarter = len(cols) // count
    for i in range(quarter):
        chosen = jnp.zeros((1, LANES), f32)
        for q in range(count):
            chosen = jnp.where(plan_ref[0] == q, cols[q * quarter + i], chosen)
        rows_of.append(chosen)
    rows_of += [sums[last + k : last + k + 1, i * LANES : (i + 1) * LANES] for k in range(CONV) for i in range(wide)]
    rows_of.append(jnp.zeros((SMALL - len(rows_of), LANES), f32))
    out_ref[...] = jnp.concatenate(rows_of, axis=0)


def small_sums(place, tokens, parts, kernel_grad, gain_grad, small):
    shapes = [jax.ShapeDtypeStruct(parts[0].shape, f32), jax.ShapeDtypeStruct((SMALL, LANES), f32)]
    operands = (*parts, kernel_grad, gain_grad, small)
    return scalar_call(
        functools.partial(small_kernel, len(parts), tokens), place, operands, [all_of(a) for a in operands],
        [all_of(a) for a in shapes], shapes, limit=8, micros=0,
    )


def wide_weights_kernel(k, normed_a, normed_b, gate_a, gate_b, out_a, out_b, cot_a, cot_b, *outs):
    tile = normed_a.shape[1]
    gate_keep, gate_send, out_keep, out_send = outs
    gate = dot(normed_a[...], gate_a[...], TN) + dot(normed_b[...], gate_b[...], TN)
    out = dot(out_a[...], cot_a[...], TN) + dot(out_b[...], cot_b[...], TN)
    targets = ((gate_keep, 0, out_keep, 0), (gate_send, 0, out_keep, 1), (gate_keep, 1, out_send, 0), (gate_send, 1, out_send, 1))
    for i, (gate_ref, gate_at, out_ref, out_at) in enumerate(targets):

        @pl.when(k == i)
        def _(gate_ref=gate_ref, gate_at=gate_at, out_ref=out_ref, out_at=out_at):
            gate_ref[gate_at * tile : (gate_at + 1) * tile] = gate
            out_ref[out_at * tile : (out_at + 1) * tile] = out


def value_weights_kernel(k, normed_a, normed_b, value_a, value_b, first_keep, first_send, second_keep, second_send):
    total = dot(normed_a[...], value_a[...], TN) + dot(normed_b[...], value_b[...], TN)
    half = total.shape[0] // 2
    targets = ((first_keep, 0, second_keep, 0), (first_send, 0, second_keep, 1), (first_keep, 1, second_send, 0), (first_send, 1, second_send, 1))
    for i, (first_ref, first_at, second_ref, second_at) in enumerate(targets):

        @pl.when(k == i)
        def _(first_ref=first_ref, first_at=first_at, second_ref=second_ref, second_at=second_at):
            first_ref[first_at * half : (first_at + 1) * half] = total[:half]
            second_ref[second_at * half : (second_at + 1) * half] = total[half:]


def input_partials(place, pieces, grad_gate, grad_value, narrow, residual, pre_gain, gate_weight, input_weight, state_weight, step_weight):
    tokens, width = residual.shape
    inner = grad_gate.shape[1]
    tile = min(tokens, 256)
    by_rows = lambda cols: pl.BlockSpec((tile, cols), lambda b, plan: (b, 0))
    return scalar_call(
        functools.partial(input_kernel_body, pieces), place,
        (grad_gate, grad_value, narrow, residual, pre_gain, gate_weight, input_weight, state_weight, step_weight),
        [
            by_rows(inner), by_rows(inner), by_rows(narrow.shape[1]), by_rows(width),
            *[all_of(a) for a in (pre_gain, gate_weight, input_weight, state_weight, step_weight)],
        ],
        [
            pl.BlockSpec((pieces, tile, width // pieces), lambda b, plan: (0, b, 0)),
            pl.BlockSpec((EDGE, tile), lambda b, plan: (0, b)),
            pl.BlockSpec((EDGE, width), lambda b, plan: (0, 0)),
        ],
        [
            jax.ShapeDtypeStruct((pieces, tokens, width // pieces), f32),
            jax.ShapeDtypeStruct((EDGE, tokens), f32),
            jax.ShapeDtypeStruct((EDGE, width), f32),
        ],
        grid=(tokens // tile,), scratch=[pltpu.VMEM((width, LANES), bf16)], limit=56, micros=0,
    )


def value_weights(plan, count, normed, grad_value):
    tokens, width = normed[0].shape
    tile = width // count
    half = grad_value[0].shape[1] // 2
    moving = pl.BlockSpec((tokens, tile), lambda k, plan: (0, jnp.bitwise_xor(plan[1], k)))
    still = pl.BlockSpec((tokens, half), lambda k, plan: (0, plan[0]))
    shape = jax.ShapeDtypeStruct((tile, half), f32)

    def body(plan_ref, *refs):
        value_weights_kernel(pl.program_id(0), *refs)

    return scalar_call(
        body, plan, (*normed, *grad_value), [moving, moving, still, still],
        [all_of(shape)] * 4, [shape] * 4, grid=(count,), limit=56, micros=0,
    )


def narrow_weights_kernel(plan_ref, normed_a, normed_b, narrow_a, narrow_b, small_a, small_b, *outs):
    k = pl.program_id(0)
    tokens, tile = normed_a.shape
    total = dot(narrow_a[...], normed_a[...], TN) + dot(narrow_b[...], normed_b[...], TN)
    small = small_a[...] + small_b[...]
    per_row = tile // LANES
    for i, ref in enumerate(outs):

        @pl.when(k == i)
        def _(ref=ref):
            ref[:LANES] = total
            for j in range(per_row):
                ref[LANES:, j * LANES : (j + 1) * LANES] = small[j * SMALL // per_row : (j + 1) * SMALL // per_row]


def narrow_weights(plan, count, normed, narrow, small):
    tokens, width = normed[0].shape
    tile = width // count
    moving = pl.BlockSpec((tokens, tile), lambda k, plan: (0, jnp.bitwise_xor(plan[1], k)))
    shape = jax.ShapeDtypeStruct((LANES + SMALL * LANES // tile, tile), f32)
    return scalar_call(
        narrow_weights_kernel, plan, (*normed, *narrow, *small), [moving, moving, *[all_of(a) for a in (*narrow, *small)]],
        [all_of(shape)] * count, [shape] * count, grid=(count,), limit=16, micros=0,
    )


def sum_kernel(count, *refs):
    total = refs[0][...]
    for ref in refs[1:count]:
        total = total + ref[...]
    refs[count][...] = total.astype(refs[count].dtype)


def sum_of(arrays, dtype):
    shape = jax.ShapeDtypeStruct(arrays[0].shape, dtype)
    return pl.pallas_call(
        functools.partial(sum_kernel, len(arrays)),
        out_shape=shape,
        compiler_params=pltpu.CompilerParams(vmem_limit_bytes=16 * 1024 * 1024),
        cost_estimate=cost(0),
    )(*arrays)


def over_ctx(arrays, wait=()):
    arrived = [swapped(a, "ctx", k) for k, a in enumerate(arrays) if k]
    return over_dp(sum_of([arrays[0], *after(wait, arrived)], f32))


def over_dp(total):
    step = 2
    while step < lax.axis_size("dp"):
        total = total + swapped(total, "dp", step)
        step *= 2
    return total


def halves_kernel(own_a, own_b, got_a, got_b, stay_out, away_a, away_b):
    half = away_a.shape[0]
    stay_out[:half] = own_a[:half] + got_a[:half]
    stay_out[half:] = own_b[:half] + got_b[:half]
    away_a[...] = own_a[half:] + got_a[half:]
    away_b[...] = own_b[half:] + got_b[half:]


def halves(own_a, own_b, got_a, got_b):
    size, cols = own_a.shape
    half = jax.ShapeDtypeStruct((size // 2, cols), f32)
    return pl.pallas_call(
        halves_kernel,
        out_shape=[jax.ShapeDtypeStruct((size, cols), f32), half, half],
        compiler_params=pltpu.CompilerParams(vmem_limit_bytes=16 * 1024 * 1024),
        cost_estimate=cost(0),
    )(own_a, own_b, got_a, got_b)


def add_kernel(stay, got_a, got_b, out):
    half = got_a.shape[0]
    out[:half] = (stay[:half] + got_a[...]).astype(out.dtype)
    out[half:] = (stay[half:] + got_b[...]).astype(out.dtype)


def add_halves(stay, got_a, got_b, dtype):
    return pl.pallas_call(
        add_kernel,
        out_shape=jax.ShapeDtypeStruct(stay.shape, dtype),
        compiler_params=pltpu.CompilerParams(vmem_limit_bytes=16 * 1024 * 1024),
        cost_estimate=cost(0),
    )(stay, got_a, got_b)


def summed(stay, got_a, got_b):
    if lax.axis_size("dp") == 2:
        return add_halves(stay, got_a, got_b, bf16)
    return over_dp(add_halves(stay, got_a, got_b, f32)).astype(bf16)


def ordered(first, here, there):
    here, there = here.astype(f32), there.astype(f32)
    return jnp.where(first, here, there), jnp.where(first, there, here)


def wide_together_kernel(plan_ref, here, there, gate_out, out_out):
    tile = gate_out.shape[0]
    k = pl.program_id(0)
    first = plan_ref[0] == 0
    half = gate_out.shape[1] // 2
    span = pl.ds(pl.multiple_of(k * 2 * tile, 2 * EDGE), tile)
    gate_out[:, :half], gate_out[:, half:] = ordered(first, here[span], there[span])
    span = pl.ds(pl.multiple_of(k * 2 * tile + tile, 2 * EDGE), tile)
    out_out[:tile], out_out[tile:] = ordered(first, here[span], there[span])


def wide_together(plan, count, here, there):
    tile = here.shape[0] // (2 * count)
    width, inner = tile * count, 2 * here.shape[1]
    return scalar_call(
        wide_together_kernel, plan, (here, there), [all_of(here), all_of(there)],
        [pl.BlockSpec((tile, inner), lambda q, plan: (q, 0)), pl.BlockSpec((inner, tile), lambda q, plan: (0, q))],
        [jax.ShapeDtypeStruct((width, inner), f32), jax.ShapeDtypeStruct((inner, width), f32)],
        grid=(count,), limit=24, micros=0,
    )


def narrow_together_kernel(plan_ref, here, there, input_out, state_out, step_out):
    tile = input_out.shape[0]
    k = jnp.bitwise_xor(pl.program_id(0), plan_ref[1])
    half = input_out.shape[1] // 2
    start = pl.multiple_of(k * (tile + LANES), 2 * EDGE)
    span = pl.ds(start, tile)
    input_out[:, :half], input_out[:, half:] = ordered(plan_ref[0] == 0, here[span], there[span])
    rest = here[pl.ds(pl.multiple_of(start + tile, 2 * EDGE), LANES)].astype(f32)
    states = state_out.shape[0]
    state_out[...] = rest[:states]
    step_out[...] = rest[states : states + step_out.shape[0]]


def narrow_together(plan, count, here, there, state_part, steps):
    tile = here.shape[0] // count - LANES
    width, inner = tile * count, 2 * here.shape[1]
    by_lane = lambda size: pl.BlockSpec((size, tile), lambda q, plan: (0, q))
    return scalar_call(
        narrow_together_kernel, plan, (here, there), [all_of(here), all_of(there)],
        [pl.BlockSpec((tile, inner), lambda q, plan: (q, 0)), by_lane(state_part), by_lane(steps)],
        [
            jax.ShapeDtypeStruct((width, inner), f32),
            jax.ShapeDtypeStruct((state_part, width), f32),
            jax.ShapeDtypeStruct((steps, width), f32),
        ],
        grid=(count,), limit=20, micros=0,
    )


def final_kernel(count, plan_ref, part_ref, up_ref, down_ref, x_ref, mine_ref, cot_ref, gain_ref, sums_ref, out_ref):
    b = pl.program_id(0)
    size, part = up_ref.shape
    x = x_ref[...].astype(f32)
    width = x.shape[1]
    scaling = lax.rsqrt(jnp.mean(x * x, axis=-1, keepdims=True) + epsilon)
    row = jnp.zeros((1, size), f32)
    for q in range(count):
        row = jnp.where(b == q, sums_ref[q : q + 1], row)
    pull = column(row) * ((scaling * scaling * scaling) / width)
    for span in spans(part):
        normed_grad = part_ref[0, :, span] + up_ref[:, span].astype(f32) + down_ref[:, span].astype(f32)
        out_ref[:, span] = (
            cot_ref[:, span].astype(f32) + scaling * gain_ref[:, span] * normed_grad - mine_ref[:, span].astype(f32) * pull
        )


def final(place, parts, arrived, residual, cotangent, pre_gain, sums):
    count, tokens, part = parts.shape
    size = sums.shape[1]
    mine = pl.BlockSpec((size, part), lambda b, plan: (b, plan[0]))
    own = pl.BlockSpec((size, part), lambda b, plan: (b, 0))
    return scalar_call(
        functools.partial(final_kernel, tokens // size), place,
        (parts, *arrived, residual, residual, cotangent, pre_gain, sums),
        [
            pl.BlockSpec((1, size, part), lambda b, plan: (plan[0], b, 0)),
            own,
            own,
            pl.BlockSpec((size, residual.shape[1]), lambda b, plan: (b, 0)),
            mine,
            mine,
            pl.BlockSpec((1, part), lambda b, plan: (0, plan[0])),
            all_of(sums),
        ],
        own,
        jax.ShapeDtypeStruct((tokens, part), f32),
        grid=(tokens // size,), limit=16, micros=0,
    )


def per_device(residual, pre_gain, gate_weight, input_weight, state_weight, step_weight, input_kernel, state_kernel,
               step_bias, decay_log, skip_gain, norm_gain, out_weight, cotangent):
    residual, cotangent = residual[0], cotangent[0]
    tokens, width = residual.shape
    tensor_size = lax.axis_size("tensor")
    ctx_size = lax.axis_size("ctx")
    inner = gate_weight.shape[1]
    inner_total = inner * tensor_size
    head_count = step_weight.shape[1]
    state2 = state_weight.shape[1]
    state_part = state2 // tensor_size
    row = lambda v: v.reshape(1, -1)
    plan = jnp.stack([lax.axis_index("dp") % 2, lax.axis_index("ctx"), lax.axis_index("tensor")]).astype(jnp.int32)
    place = lax.axis_index("tensor").astype(jnp.int32).reshape(1)

    halo = from_before(residual[-2 * EDGE :], "ctx")
    other_cotangent = swapped(cotangent, "dp", 1)
    step_weight = step_weight.T
    normed, value_in, state_in, step_raw = project(residual, row(pre_gain), input_weight, state_weight, step_weight)
    other_normed = swapped(normed, "dp", 1)
    conv, pre, state_rows, spre, dt, cum, cumt, held, message, vhalo, shalo = local_states(
        value_in, state_in, step_raw, halo, row(pre_gain), input_weight, state_weight, input_kernel, state_kernel,
        row(step_bias), row(decay_log)
    )
    messages = [from_before(message, "ctx", by) for by in range(1, ctx_size)]
    gate_in, grad_normed = beside(after(message, normed), gate_weight, cotangent, out_weight)
    intra = inner_forward(head_count, conv, dt, state_rows, cum, cumt, row(skip_gain))
    messages = after((gate_in, intra, other_cotangent), messages)
    mixed, sums, held, end_state = combine(
        intra, state_rows, cum, held, message, messages, gate_in, grad_normed, row(norm_gain)
    )
    all_sums = [sums, *after(other_normed, from_all(sums, "tensor"))]
    normed_out, grad_gate, grad_mixed, later, message, gain_grad = gate_back(
        mixed, gate_in, grad_normed, state_rows, cum, row(norm_gain), all_sums, inner_total
    )
    messages = [from_after(message, "ctx", by) for by in range(1, ctx_size)]
    other_gate = swapped(grad_gate, "dp", 1)
    other_out = swapped(normed_out, "dp", 1)

    resid_part = own_part(residual, "tensor", 1).astype(f32)
    partial_out = dot(after(message, normed_out), out_weight)
    branch = lax.psum_scatter(partial_out, "tensor", scatter_dimension=1, tiled=True)
    output = (resid_part + branch).astype(bf16)

    grad_driven, grad_rows = inner_back(head_count, conv, dt, state_rows, cum, cumt, after(partial_out, grad_mixed))
    messages = after(grad_driven, messages)
    grad_rows, later, first_rows = rows_back(grad_rows, grad_mixed, conv, dt, cum, state_rows, held, later, messages, spre)
    ahead = from_after(first_rows, "ctx")
    pieces = list(pieces_of(place, tensor_size, grad_rows, ahead))
    arrived = [
        lax.ppermute(pieces[k], "tensor", [(i, (i + k) % tensor_size) for i in range(tensor_size)]) for k in range(1, tensor_size)
    ]
    (grad_value, grad_step, last_rows, first_rows, kernel_grad, small, gate_keep, gate_send, out_keep, out_send) = finish(
        plan, ctx_size, (normed, other_normed, grad_gate, other_gate, normed_out, other_out, cotangent, other_cotangent),
        grad_driven, after(pieces[0], grad_mixed), mixed, pre, value_in, dt, cum, step_raw, state_rows, held, end_state, later,
        vhalo, input_kernel, row(skip_gain), row(step_bias), row(decay_log)
    )
    ahead_value = from_after(first_rows, "ctx")
    arrived = after(first_rows, arrived)
    narrow, taps_grad = state_back(place, [pieces[0], *arrived], spre, state_in, shalo, ahead, state_kernel, grad_step)
    grad_value = complete(after(narrow, ahead_value), last_rows, input_kernel, grad_value)
    other_value = swapped(grad_value, "dp", 1)
    other_narrow = swapped(narrow, "dp", 1)
    gate_send, out_send = after(grad_value, (gate_send, out_send))
    gate_got, out_got = swapped(gate_send, "ctx", 1), swapped(out_send, "ctx", 2)
    parts, row_sums, col_sums = input_partials(
        place, tensor_size, grad_gate, grad_value, narrow, residual, row(pre_gain), gate_weight, input_weight, state_weight,
        step_weight
    )
    packed = sums_of(place, tensor_size, row_sums, col_sums, taps_grad, state2)
    packed = [packed, *from_all(packed, "tensor")]
    sent = line_first(parts, "tensor")
    packed, sent = after(sent, packed), after(packed, sent)
    moving = lax.ppermute(sent, "tensor", [(0, 1), (tensor_size - 1, tensor_size - 2)])
    first_keep, first_send, second_keep, second_send = value_weights(
        after(sent, plan), ctx_size, (normed, other_normed), (grad_value, other_value)
    )
    sums, small = small_sums(place, tokens, after(first_keep, packed), kernel_grad, gain_grad, small)
    other_small = swapped(small, "dp", 1)
    stay, gate_away, out_away = halves(gate_keep, out_keep, *after(small, (gate_got, out_got)))
    gate_got, out_got = swapped(gate_away, "ctx", 2), swapped(out_away, "ctx", 1)
    sent, moving = line_step(parts, 2, after(stay, moving), "tensor")
    wide_chunk = summed(stay, *after(sent, (gate_got, out_got)))
    first_send, second_send = after(wide_chunk, (first_send, second_send))
    first_got, second_got = swapped(first_send, "ctx", 1), swapped(second_send, "ctx", 2)
    wide_here = lax.all_gather(wide_chunk, "ctx", tiled=True)
    weights = narrow_weights(after(small, plan), ctx_size, (normed, other_normed), (narrow, other_narrow), (small, other_small))
    sent, moving = line_step(parts, 3, after(weights, moving), "tensor")
    stay, first_away, second_away = halves(first_keep, second_keep, *after(sent, (first_got, second_got)))
    first_got, second_got = swapped(first_away, "ctx", 2), swapped(second_away, "ctx", 1)
    narrow_total = over_ctx(weights, stay)
    value_chunk = summed(stay, *after((narrow_total, output), (first_got, second_got)))
    chunk = jnp.concatenate([value_chunk, narrow_total[:LANES].astype(bf16)], axis=0)
    chunks = [swapped(chunk, "ctx", k) for k in range(1, ctx_size)]
    input_grad = final(place, parts, after(chunk, moving), residual, cotangent, row(pre_gain), sums)
    narrow_here = jnp.concatenate([chunk, *after(input_grad, chunks)], axis=0)
    narrow_there = swapped(narrow_here, "dp", 1)
    wide_there = swapped(after(narrow_here, wide_here), "dp", 1)
    input_weight_grad, state_weight_grad, step_weight_grad = narrow_together(
        plan, ctx_size, narrow_here, narrow_there, state_part, head_count
    )
    gate_weight_grad, out_weight_grad = wide_together(after(input_weight_grad, plan), ctx_size, wide_here, wide_there)
    small_total = narrow_total[LANES:]
    small_total = jnp.concatenate([small_total[:, i : i + LANES] for i in range(0, small_total.shape[1], LANES)], axis=0)
    wide_rows = inner // LANES
    at = CONV * wide_rows
    kernel_grad = small_total[:at].reshape(CONV, inner)
    gain_grad = small_total[at : at + wide_rows].reshape(inner)
    at += wide_rows
    small = small_total[at : at + 3, :head_count]
    at += 3
    gain_rows = width // tensor_size // LANES
    pre_gain_grad = small_total[at : at + gain_rows].reshape(width // tensor_size)
    at += gain_rows
    taps_grad = small_total[at : at + CONV * state2 // LANES].reshape(CONV, state2)
    return (
        output[None],
        input_grad[None],
        pre_gain_grad,
        gate_weight_grad,
        input_weight_grad,
        state_weight_grad.T,
        step_weight_grad.T,
        kernel_grad,
        taps_grad,
        small[1],
        small[2],
        small[0],
        gain_grad,
        out_weight_grad,
    )


def solution(mesh):
    in_specs = (
        P("dp", "ctx", None),
        P(),
        P(None, "tensor"),
        P(None, "tensor"),
        P(),
        P(None, "tensor"),
        P(None, "tensor"),
        P(),
        P("tensor"),
        P("tensor"),
        P("tensor"),
        P("tensor"),
        P("tensor", None),
        P("dp", "ctx", None),
    )
    out_specs = (
        P("dp", "ctx", "tensor"),
        P("dp", "ctx", "tensor"),
        P("tensor"),
        P(None, "tensor"),
        P(None, "tensor"),
        P(None, "tensor"),
        P(None, "tensor"),
        P(None, "tensor"),
        P(),
        P("tensor"),
        P("tensor"),
        P("tensor"),
        P("tensor"),
        P("tensor", None),
    )
    return jax.shard_map(per_device, mesh=mesh, in_specs=in_specs, out_specs=out_specs, check_vma=False)
```

```python
import functools

import jax
import jax.numpy as jnp
from jax import lax
from jax.experimental import pallas as pl
from jax.experimental.pallas import tpu as pltpu
from jax.sharding import PartitionSpec as P

HEAD_DIM = 64
CONV = 4
EDGE = 8
BLOCK = 128
LANES = 128
epsilon = 1e-05
f32 = jnp.float32
bf16 = jnp.bfloat16

NN = (((1,), (0,)), ((), ()))
NT = (((1,), (1,)), ((), ()))
TN = (((0,), (0,)), ((), ()))


def dot(a, b, dims=NN):
    return lax.dot_general(a, b, dims, preferred_element_type=f32)


def split2(x):
    high = x.astype(bf16)
    return high, (x - high.astype(f32)).astype(bf16)


def split3(x):
    high = x.astype(bf16)
    rest = x - high.astype(f32)
    middle = rest.astype(bf16)
    return high, middle, (rest - middle.astype(f32)).astype(bf16)


def dot3(a, b, dims=NN):
    ah, al = split2(a)
    bh, bl = split2(b)
    return dot(ah, bh, dims) + (dot(ah, bl, dims) + dot(al, bh, dims))


def both_parts(x):
    return jnp.concatenate(split2(x), axis=1)


def fold(product):
    half = product.shape[1] // 2
    return product[:, :half] + product[:, half:]


def wide_dot(parts, x):
    across = both_parts(x)
    return fold(dot(parts, jnp.concatenate([across, across], axis=0)))


def exact_dot(ones, x, dims):
    high, middle, low = split3(x)
    return dot(ones, high, dims) + (dot(ones, middle, dims) + dot(ones, low, dims))


def iota(shape, axis):
    return lax.broadcasted_iota(jnp.int32, shape, axis)


REPEAT = 16


def head_map(width):
    lane = iota((LANES, width), 0)
    mine = (lane % REPEAT == iota((LANES, width), 1) // HEAD_DIM) & (lane < 3 * REPEAT)
    return mine.astype(f32).astype(bf16)


def spread(per_head, heads):
    high = per_head.astype(bf16).astype(f32)
    rest = per_head - high
    middle = rest.astype(bf16).astype(f32)
    group = iota(per_head.shape, 1) // REPEAT
    parts = jnp.where(group == 0, high, jnp.where(group == 1, middle, rest - middle))
    return dot(parts.astype(bf16), heads)


def repeated(row):
    group = jnp.concatenate([row, jnp.zeros((1, REPEAT - row.shape[1]), f32)], axis=1)
    return jnp.concatenate([group] * (LANES // REPEAT), axis=1)


def sig(v):
    return jax.nn.sigmoid(v)


def cost(micros):
    return pl.CostEstimate(flops=micros * 900_000_000, bytes_accessed=micros * 3_000_000, transcendentals=0)


def params(limit=20):
    return pltpu.CompilerParams(
        dimension_semantics=("arbitrary",), vmem_limit_bytes=limit * 1024 * 1024
    )


def in_hbm(x):
    return pltpu.with_memory_space_constraint(x, pltpu.HBM)


def whole(shape):
    return pl.BlockSpec(shape, lambda b: (0,) * len(shape))


def rows(size, width, count=0):
    if count:
        return pl.BlockSpec((size, width), lambda b: (count - 1 - b, 0))
    return pl.BlockSpec((size, width), lambda b: (b, 0))


def spans(width):
    return [slice(i * LANES, (i + 1) * LANES) for i in range(width // LANES)]


def by_eights(x):
    return jnp.sum(x.reshape(x.shape[0] // EDGE, EDGE, x.shape[1]), axis=0)


def norm_rows(x, gain):
    scaling = lax.rsqrt(jnp.mean(x * x, axis=-1, keepdims=True) + epsilon)
    return (x * scaling * gain).astype(bf16)


def project_kernel(x_ref, gain_ref, value_ref, state_ref, step_ref, normed_out, value_out, state_out, step_out, step_w):
    @pl.when(pl.program_id(0) == 0)
    def _():
        count = step_ref.shape[0]
        copies = (iota((LANES, count), 0) % REPEAT == iota((LANES, count), 1)).astype(f32).astype(bf16)
        step_w[...] = dot(copies, step_ref[...]).astype(bf16)

    normed = norm_rows(x_ref[...].astype(f32), gain_ref[...])
    normed_out[...] = normed
    value_out[...] = dot(normed, value_ref[...]).astype(bf16)
    state_out[...] = dot(normed, state_ref[...]).astype(bf16)
    step_out[...] = dot(normed, step_w[...], NT)


def project(residual, pre_gain, input_weight, state_weight, step_weight):
    tokens, width = residual.shape
    inner, state2 = input_weight.shape[1], state_weight.shape[1]
    tile = min(tokens, 256)
    return pl.pallas_call(
        project_kernel,
        grid=(tokens // tile,),
        in_specs=[
            rows(tile, width),
            whole((1, width)),
            whole(input_weight.shape),
            whole(state_weight.shape),
            whole(step_weight.shape),
        ],
        out_specs=[rows(tile, width), rows(tile, inner), rows(tile, state2), rows(tile, LANES)],
        out_shape=[
            pltpu.HBM((tokens, width), bf16),
            jax.ShapeDtypeStruct((tokens, inner), bf16),
            jax.ShapeDtypeStruct((tokens, state2), bf16),
            jax.ShapeDtypeStruct((tokens, LANES), f32),
        ],
        scratch_shapes=[pltpu.VMEM((LANES, width), bf16)],
        compiler_params=params(24),
        cost_estimate=cost(6),
    )(residual, pre_gain, input_weight, state_weight, step_weight)


def beside_kernel(normed_ref, gate_w, cot_ref, out_w, gate_out, grad_out):
    gate_out[...] = dot(normed_ref[...], gate_w[...])
    grad_out[...] = dot(cot_ref[...], out_w[...], NT)


def beside(normed, gate_weight, cotangent, out_weight):
    tokens, width = normed.shape
    inner = gate_weight.shape[1]
    tile = min(tokens, 256)
    return pl.pallas_call(
        beside_kernel,
        grid=(tokens // tile,),
        in_specs=[rows(tile, width), whole(gate_weight.shape), rows(tile, width), whole(out_weight.shape)],
        out_specs=[rows(tile, inner), rows(tile, inner)],
        out_shape=[jax.ShapeDtypeStruct((tokens, inner), f32), jax.ShapeDtypeStruct((tokens, inner), f32)],
        compiler_params=params(20),
        cost_estimate=cost(6),
    )(normed, gate_weight, cotangent, out_weight)


def convolve(before, here, kernel):
    extended = jnp.concatenate([before, here], axis=0)
    count = here.shape[0]
    first = EDGE - CONV + 1
    summed = kernel[0:1] * extended[first : first + count]
    for k in range(1, CONV):
        summed = summed + kernel[k : k + 1] * extended[first + k : first + k + count]
    return summed


def local_kernel(
    value_ref, state_ref, step_ref, halo_ref, gain_ref, value_w, state_w, value_k, state_k, bias_ref, log_ref,
    conv_out, pre_out, rows_out, spre_out, dt_out, cum_out, cumt_out, held_out, message_out, vhalo_out, shalo_out,
    value_before, state_before, held, total, heads,
):
    b = pl.program_id(0)
    width = value_ref.shape[1]

    @pl.when(b == 0)
    def _():
        normed = norm_rows(halo_ref[...].astype(f32), gain_ref[...])
        value_halo = dot(normed, value_w[...]).astype(bf16)
        state_halo = dot(normed, state_w[...]).astype(bf16)
        vhalo_out[...] = value_halo
        shalo_out[...] = state_halo
        value_before[...] = value_halo.astype(f32)[-EDGE:]
        state_before[...] = state_halo.astype(f32)[-EDGE:]
        held[...] = jnp.zeros(held.shape, f32)
        total[...] = jnp.zeros(total.shape, f32)
        heads[...] = head_map(width)

    dt = jax.nn.softplus(step_ref[...] + repeated(bias_ref[...]))
    decay = -dt * jnp.exp(repeated(log_ref[...]))
    size = value_ref.shape[0]
    lower = (iota((size, size), 0) >= iota((size, size), 1)).astype(f32).astype(bf16)
    cum = exact_dot(lower, decay, NN)
    dt_out[...] = dt
    cum_out[...] = cum
    cumt_out[...] = cum.T[: cumt_out.shape[0]]
    last = cum[size - 1 : size]
    wide = spread(jnp.concatenate([dt, cum], axis=0), heads[...])

    state = state_ref[...].astype(f32)
    spre = convolve(state_before[...], state, state_k[...].astype(f32))
    state_before[...] = state[-EDGE:]
    mixed_rows = spre * sig(spre)
    spre_out[...] = spre
    rows_out[...] = mixed_rows
    b_parts = both_parts(mixed_rows[:, :LANES].T)

    taps = value_k[...].astype(f32)
    held_out[0] = held[...]
    for span in spans(width):
        value = value_ref[:, span].astype(f32)
        pre = convolve(value_before[:, span], value, taps[:, span])
        value_before[:, span] = value[-EDGE:]
        conv = pre * sig(pre)
        pre_out[:, span] = pre
        conv_out[:, span] = conv
        cum_wide = wide[size:, span]
        end = cum_wide[size - 1 : size]
        weighted = conv * wide[:size, span] * jnp.exp(end - cum_wide)
        held[:, span] = jnp.exp(end) * held[:, span] + wide_dot(b_parts, weighted)
        total[:, span] = total[:, span] + end

    @pl.when(b == pl.num_programs(0) - 1)
    def _():
        message_out[:LANES] = held[...]
        message_out[LANES:] = total[...]


def local_states(value_in, state_in, step_raw, halo, pre_gain, input_weight, state_weight, input_kernel, state_kernel, step_bias, decay_log):
    tokens, inner = value_in.shape
    state2 = state_in.shape[1]
    state = state2 // 2
    blocks = tokens // BLOCK
    headrows = 16
    return pl.pallas_call(
        local_kernel,
        grid=(blocks,),
        in_specs=[
            rows(BLOCK, inner),
            rows(BLOCK, state2),
            rows(BLOCK, LANES),
            whole(halo.shape),
            whole(pre_gain.shape),
            whole(input_weight.shape),
            whole(state_weight.shape),
            whole(input_kernel.shape),
            whole(state_kernel.shape),
            whole(step_bias.shape),
            whole(decay_log.shape),
        ],
        out_specs=[
            rows(BLOCK, inner),
            rows(BLOCK, inner),
            rows(BLOCK, state2),
            rows(BLOCK, state2),
            rows(BLOCK, LANES),
            rows(BLOCK, LANES),
            pl.BlockSpec((headrows, BLOCK), lambda b: (0, b)),
            pl.BlockSpec((1, state, inner), lambda b: (b, 0, 0)),
            whole((state + EDGE, inner)),
            whole((halo.shape[0], inner)),
            whole((halo.shape[0], state2)),
        ],
        out_shape=[
            jax.ShapeDtypeStruct((tokens, inner), f32),
            pltpu.HBM((tokens, inner), f32),
            jax.ShapeDtypeStruct((tokens, state2), f32),
            jax.ShapeDtypeStruct((tokens, state2), f32),
            jax.ShapeDtypeStruct((tokens, LANES), f32),
            jax.ShapeDtypeStruct((tokens, LANES), f32),
            jax.ShapeDtypeStruct((headrows, tokens), f32),
            jax.ShapeDtypeStruct((blocks, state, inner), f32),
            jax.ShapeDtypeStruct((state + EDGE, inner), f32),
            jax.ShapeDtypeStruct((halo.shape[0], inner), bf16),
            jax.ShapeDtypeStruct((halo.shape[0], state2), bf16),
        ],
        scratch_shapes=[
            pltpu.VMEM((EDGE, inner), f32),
            pltpu.VMEM((EDGE, state2), f32),
            pltpu.VMEM((state, inner), f32),
            pltpu.VMEM((EDGE, inner), f32),
            pltpu.VMEM((LANES, inner), bf16),
        ],
        compiler_params=params(),
        cost_estimate=cost(10),
    )(value_in, state_in, step_raw, halo, pre_gain, input_weight, state_weight, input_kernel, state_kernel, step_bias, decay_log)


def inner_kernel(heads_count, conv_ref, dt_ref, rows_ref, cum_ref, cumt_ref, skip_ref, out_ref, heads):
    size, width = conv_ref.shape

    @pl.when(pl.program_id(0) == 0)
    def _():
        heads[...] = head_map(width)

    skip = jnp.broadcast_to(repeated(skip_ref[...]), (EDGE, LANES))
    wide = spread(jnp.concatenate([dt_ref[...], skip], axis=0), heads[...])
    scores = dot3(rows_ref[:, LANES:], rows_ref[:, :LANES], NT)
    causal = iota((size, size), 0) >= iota((size, size), 1)
    left = iota((size, LANES), 1) < HEAD_DIM
    cum = cum_ref[...]
    cumt = cumt_ref[...]
    for pair, span in enumerate(spans(width)):
        conv = conv_ref[:, span]
        mixes = []
        for h in (2 * pair, 2 * pair + 1):
            gap = cum[:, h : h + 1] - cumt[h : h + 1, :]
            mixes.append(both_parts(jnp.exp(jnp.where(causal, gap, -1e30)) * scores))
        both = wide_dot(jnp.concatenate(mixes, axis=0), conv * wide[:size, span])
        out_ref[:, span] = jnp.where(left, both[:size], both[size:]) + wide[size : size + 1, span] * conv


def inner_forward(heads_count, conv, dt, state_rows, cum, cumt, skip_gain):
    tokens, inner = conv.shape
    return pl.pallas_call(
        functools.partial(inner_kernel, heads_count),
        grid=(tokens // BLOCK,),
        in_specs=[
            rows(BLOCK, inner),
            rows(BLOCK, LANES),
            rows(BLOCK, state_rows.shape[1]),
            rows(BLOCK, LANES),
            pl.BlockSpec((cumt.shape[0], BLOCK), lambda b: (0, b)),
            whole(skip_gain.shape),
        ],
        out_specs=rows(BLOCK, inner),
        out_shape=jax.ShapeDtypeStruct((tokens, inner), f32),
        scratch_shapes=[pltpu.VMEM((LANES, inner), bf16)],
        compiler_params=params(12),
        cost_estimate=cost(6),
    )(conv, dt, state_rows, cum, cumt, skip_gain)


def combine_kernel(count, intra_ref, rows_ref, cum_ref, held_ref, own_ref, *refs):
    message_refs, (gate_ref, grad_ref, gain_ref, mixed_out, sums_out, held_out, end_out, start, total, heads) = refs[:count], refs[count:]
    b = pl.program_id(0)
    size, width = intra_ref.shape
    state = held_ref.shape[1]

    @pl.when(b == 0)
    def _():
        heads[...] = head_map(width)
        total[...] = jnp.zeros(total.shape, f32)
        for span in spans(width):
            entering = jnp.zeros((state, LANES), f32)
            passed = jnp.zeros((EDGE, LANES), f32)
            for ref in message_refs:
                entering = entering + jnp.exp(passed[0:1]) * ref[:state, span]
                passed = passed + ref[state:, span]
            start[:, span] = entering
            end_out[:, span] = own_ref[:state, span] + jnp.exp(own_ref[state : state + 1, span]) * entering

    cum_wide = spread(cum_ref[...], heads[...])
    c_parts = both_parts(rows_ref[:, LANES:])
    square = jnp.zeros((size, LANES), f32)
    inner = jnp.zeros((size, LANES), f32)
    for span in spans(width):
        held = held_ref[0, :, span] + jnp.exp(total[0:1, span]) * start[:, span]
        held_out[0, :, span] = held
        cum_part = cum_wide[:, span]
        total[:, span] = total[:, span] + cum_part[size - 1 : size]
        mixed = intra_ref[:, span] + jnp.exp(cum_part) * wide_dot(c_parts, held)
        mixed_out[:, span] = mixed
        gate = gate_ref[:, span]
        gated = mixed * (gate * sig(gate))
        square = square + gated * gated
        inner = inner + grad_ref[:, span] * gain_ref[:, span] * gated
    ones = jnp.ones((EDGE, LANES), bf16)
    square = exact_dot(ones, square, NT)
    inner = exact_dot(ones, inner, NT)
    sums_out[...] = jnp.where(iota(square.shape, 0) == 0, square, inner)


def combine(intra, state_rows, cum, held, own, messages, gate_in, grad_normed, norm_gain):
    tokens, inner = intra.shape
    blocks, state, _ = held.shape
    state_block = pl.BlockSpec((1, state, inner), lambda b: (b, 0, 0))
    return pl.pallas_call(
        functools.partial(combine_kernel, len(messages)),
        grid=(blocks,),
        in_specs=[
            rows(BLOCK, inner),
            rows(BLOCK, state_rows.shape[1]),
            rows(BLOCK, LANES),
            state_block,
            whole(own.shape),
            *[whole(own.shape) for _ in messages],
            rows(BLOCK, inner),
            rows(BLOCK, inner),
            whole(norm_gain.shape),
        ],
        out_specs=[
            rows(BLOCK, inner),
            pl.BlockSpec((EDGE, BLOCK), lambda b: (0, b)),
            state_block,
            whole((state, inner)),
        ],
        out_shape=[
            jax.ShapeDtypeStruct((tokens, inner), f32),
            jax.ShapeDtypeStruct((EDGE, tokens), f32),
            pltpu.HBM(held.shape, f32),
            jax.ShapeDtypeStruct((state, inner), f32),
        ],
        scratch_shapes=[pltpu.VMEM((state, inner), f32), pltpu.VMEM((EDGE, inner), f32), pltpu.VMEM((LANES, inner), bf16)],
        compiler_params=params(),
        cost_estimate=cost(5),
    )(intra, state_rows, cum, held, own, *messages, gate_in, grad_normed, norm_gain)


def column(row):
    return jnp.broadcast_to(row, (LANES, row.shape[1])).T


def gate_back_kernel(count, inner_total, mixed_ref, gate_ref, grad_ref, rows_ref, cum_ref, gain_ref, *refs):
    sums_refs, (normed_out, gate_out, dmix_out, later_out, message_out, gain_out, later, total, heads) = refs[:count], refs[count:]
    b = pl.program_id(0)
    size, width = mixed_ref.shape

    @pl.when(b == 0)
    def _():
        later[...] = jnp.zeros(later.shape, f32)
        total[...] = jnp.zeros(total.shape, f32)
        gain_out[...] = jnp.zeros(gain_out.shape, f32)
        heads[...] = head_map(width)

    sums = sums_refs[0][...]
    for ref in sums_refs[1:]:
        sums = sums + ref[...]
    rms_row = lax.rsqrt(sums[0:1] / inner_total + epsilon)
    pull_row = rms_row * rms_row * rms_row * sums[1:2] / inner_total
    rms = column(rms_row)
    pull = column(pull_row)
    cum_wide = spread(cum_ref[...], heads[...])
    c_parts = both_parts(rows_ref[:, LANES:].T)
    later_out[0] = later[...]
    for span in spans(width):
        gain = gain_ref[:, span]
        gate = gate_ref[:, span]
        mixed = mixed_ref[:, span]
        grad = grad_ref[:, span]
        gate_sig = sig(gate)
        gate_silu = gate * gate_sig
        gated = mixed * gate_silu
        normed_out[:, span] = (gated * rms * gain).astype(bf16)
        gain_out[:, span] = gain_out[:, span] + by_eights(grad * gated * rms)
        grad_gated = rms * gain * grad - gated * pull
        gate_out[:, span] = (grad_gated * mixed * gate_sig * (1.0 + gate * (1.0 - gate_sig))).astype(bf16)
        grad_mixed = grad_gated * gate_silu
        dmix_out[:, span] = grad_mixed
        cum_part = cum_wide[:, span]
        end = cum_part[size - 1 : size]
        later[:, span] = jnp.exp(end) * later[:, span] + wide_dot(c_parts, jnp.exp(cum_part) * grad_mixed)
        total[:, span] = total[:, span] + end

    @pl.when(b == pl.num_programs(0) - 1)
    def _():
        message_out[:LANES] = later[...]
        message_out[LANES:] = total[...]


def gate_back(mixed, gate_in, grad_normed, state_rows, cum, norm_gain, sums, inner_total):
    tokens, inner = mixed.shape
    blocks = tokens // BLOCK
    state = state_rows.shape[1] // 2
    return pl.pallas_call(
        functools.partial(gate_back_kernel, len(sums), inner_total),
        grid=(blocks,),
        in_specs=[
            rows(BLOCK, inner, blocks),
            rows(BLOCK, inner, blocks),
            rows(BLOCK, inner, blocks),
            rows(BLOCK, 2 * state, blocks),
            rows(BLOCK, LANES, blocks),
            whole(norm_gain.shape),
            *[pl.BlockSpec((EDGE, BLOCK), lambda b: (0, blocks - 1 - b)) for _ in sums],
        ],
        out_specs=[
            rows(BLOCK, inner, blocks),
            rows(BLOCK, inner, blocks),
            rows(BLOCK, inner, blocks),
            pl.BlockSpec((1, state, inner), lambda b: (blocks - 1 - b, 0, 0)),
            whole((state + EDGE, inner)),
            whole((EDGE, inner)),
        ],
        out_shape=[
            pltpu.HBM((tokens, inner), bf16),
            pltpu.HBM((tokens, inner), bf16),
            pltpu.HBM((tokens, inner), f32),
            pltpu.HBM((blocks, state, inner), f32),
            jax.ShapeDtypeStruct((state + EDGE, inner), f32),
            jax.ShapeDtypeStruct((EDGE, inner), f32),
        ],
        scratch_shapes=[pltpu.VMEM((state, inner), f32), pltpu.VMEM((EDGE, inner), f32), pltpu.VMEM((LANES, inner), bf16)],
        compiler_params=params(),
        cost_estimate=cost(7),
    )(mixed, gate_in, grad_normed, state_rows, cum, norm_gain, *sums)


def inner_back_kernel(b, conv_ref, dt_ref, rows_ref, cum_ref, cumt_ref, dmix_ref, driven_out, rows_out, heads):
    size, width = conv_ref.shape

    @pl.when(b == 0)
    def _():
        heads[...] = head_map(width)

    dt_wide = spread(dt_ref[...], heads[...])
    b_rows = rows_ref[:, :LANES]
    c_rows = rows_ref[:, LANES:]
    scores = dot3(b_rows, c_rows, NT)
    causal = iota((size, size), 1) >= iota((size, size), 0)
    left = iota((size, LANES), 1) < HEAD_DIM
    cum = cum_ref[...]
    cumt = cumt_ref[...]
    score_grad = jnp.zeros((size, size), f32)
    for pair, span in enumerate(spans(width)):
        dmix_high, dmix_low = split2(dmix_ref[:, span])
        across = jnp.concatenate([dmix_high, dmix_low], axis=1)
        right_side = jnp.concatenate([across, across], axis=0)
        taking = jnp.concatenate([dmix_high, dmix_high, dmix_low], axis=1)
        driven = conv_ref[:, span] * dt_wide[:, span]
        owns = []
        for mine in (left, jnp.logical_not(left)):
            own_high, own_low = split2(jnp.where(mine, driven, 0.0))
            owns.append(jnp.concatenate([own_high, own_low, own_high], axis=1))
        mix_grads = dot(jnp.concatenate(owns, axis=0), taking, NT)
        mixes = []
        for side in range(2):
            h = 2 * pair + side
            gap = cumt[h : h + 1, :] - cum[:, h : h + 1]
            kept = jnp.exp(jnp.where(causal, gap, -1e30))
            score_grad = score_grad + mix_grads[side * size : (side + 1) * size] * kept
            mixes.append(both_parts(kept * scores))
        both = fold(dot(jnp.concatenate(mixes, axis=0), right_side))
        driven_out[:, span] = jnp.where(left, both[:size], both[size:])
    rows_out[:, :LANES] = dot3(score_grad, c_rows, NN)
    rows_out[:, LANES:] = dot3(score_grad, b_rows, TN)


def inner_back(normed_out, out_weight, conv, dt, state_rows, cum, cumt, grad_mixed):
    tokens, inner = conv.shape
    width = out_weight.shape[1]
    tile = min(tokens, 256)
    first = tokens // tile
    at = lambda b: jnp.maximum(b - first, 0)
    by_rows = lambda cols: pl.BlockSpec((BLOCK, cols), lambda b: (at(b), 0))
    early = lambda cols: pl.BlockSpec((tile, cols), lambda b: (jnp.minimum(b, first - 1), 0))

    def body(normed_ref, weight_ref, *refs):
        ins, partial_out, rest = refs[:6], refs[6], refs[7:]
        b = pl.program_id(0)

        @pl.when(b < first)
        def _():
            partial_out[...] = dot(normed_ref[...], weight_ref[...])

        @pl.when(b >= first)
        def _():
            inner_back_kernel(b - first, *ins, *rest)

    return pl.pallas_call(
        body,
        grid=(first + tokens // BLOCK,),
        in_specs=[
            early(inner),
            whole(out_weight.shape),
            by_rows(inner),
            by_rows(LANES),
            by_rows(state_rows.shape[1]),
            by_rows(LANES),
            pl.BlockSpec((cumt.shape[0], BLOCK), lambda b: (0, at(b))),
            by_rows(inner),
        ],
        out_specs=[early(width), by_rows(inner), by_rows(state_rows.shape[1])],
        out_shape=[
            pltpu.HBM((tokens, width), f32),
            pltpu.HBM((tokens, inner), f32),
            pltpu.HBM(state_rows.shape, f32),
        ],
        scratch_shapes=[pltpu.VMEM((LANES, inner), bf16)],
        compiler_params=params(28),
        cost_estimate=cost(1),
    )(in_hbm(normed_out), in_hbm(out_weight), conv, *map(in_hbm, (dt, state_rows, cum, cumt, grad_mixed)))


def stacked(high, low):
    return jnp.concatenate([jnp.concatenate([high, high], axis=1), jnp.concatenate([low, low], axis=1)], axis=0)


def rows_back_kernel(
    count, drows_ref, dmix_ref, conv_ref, dt_ref, cum_ref, rows_ref, held_ref, later_ref, *refs
):
    message_refs = refs[:count]
    spre_ref, grad_rows_out, later_out, first_out, entering, total, heads = refs[count:]
    b = pl.program_id(0)
    size, width = conv_ref.shape
    state = held_ref.shape[1]

    @pl.when(b == 0)
    def _():
        heads[...] = head_map(width)
        for span in spans(width):
            coming = jnp.zeros((state, LANES), f32)
            passed = jnp.zeros((EDGE, LANES), f32)
            for ref in message_refs:
                coming = coming + jnp.exp(passed[0:1]) * ref[:state, span]
                passed = passed + ref[state:, span]
            entering[:, span] = coming
        total[...] = jnp.zeros(total.shape, f32)

    wide = spread(jnp.concatenate([cum_ref[...], dt_ref[...]], axis=0), heads[...])
    toward_b, toward_c, laters, helds = [], [], [], []
    for span in spans(width):
        cum_part = wide[:size, span]
        end = cum_part[size - 1 : size]
        later = later_ref[0, :, span] + jnp.exp(total[0:1, span]) * entering[:, span]
        later_out[0, :, span] = later
        total[:, span] = total[:, span] + end
        driven = conv_ref[:, span] * wide[size:, span]
        toward_b.append(both_parts(jnp.exp(end - cum_part) * driven))
        laters.append(stacked(*split2(later)))
        toward_c.append(both_parts(jnp.exp(cum_part) * dmix_ref[:, span]))
        helds.append(stacked(*split2(held_ref[0, :, span])))
    side = lambda parts: jnp.concatenate(parts, axis=1)
    grad_rows_out[:, :LANES] = drows_ref[:, :LANES] + fold(dot(side(toward_b), side(laters), NT))
    grad_rows_out[:, LANES:] = drows_ref[:, LANES:] + fold(dot(side(toward_c), side(helds), NT))

    @pl.when(b == pl.num_programs(0) - 1)
    def _():
        first_out[:, : 2 * LANES] = grad_rows_out[:EDGE]
        first_out[:, 2 * LANES :] = spre_ref[...]


def rows_back(grad_rows, grad_mixed, conv, dt, cum, state_rows, held, later, messages, spre):
    tokens, inner = conv.shape
    blocks, state, _ = held.shape
    state_block = pl.BlockSpec((1, state, inner), lambda b: (blocks - 1 - b, 0, 0))
    deep = rows(BLOCK, inner, blocks)
    deep_state = pl.BlockSpec((1, state, inner), lambda b: (blocks - 1 - b, 0, 0))
    narrow = rows(BLOCK, LANES, blocks)
    both = rows(BLOCK, 2 * state, blocks)
    return pl.pallas_call(
        functools.partial(rows_back_kernel, len(messages)),
        grid=(blocks,),
        in_specs=[
            both, deep, deep, narrow, narrow, both, deep_state, deep_state,
            *[whole(m.shape) for m in messages],
            pl.BlockSpec((EDGE, 2 * state), lambda b: (0, 0)),
        ],
        out_specs=[both, state_block, whole((EDGE, 4 * state))],
        out_shape=[
            jax.ShapeDtypeStruct((tokens, 2 * state), f32),
            pltpu.HBM(held.shape, f32),
            jax.ShapeDtypeStruct((EDGE, 4 * state), f32),
        ],
        scratch_shapes=[pltpu.VMEM((state, inner), f32), pltpu.VMEM((EDGE, inner), f32), pltpu.VMEM((LANES, inner), bf16)],
        compiler_params=params(24),
        cost_estimate=cost(0),
    )(*map(in_hbm, (grad_rows, grad_mixed, conv, dt, cum, state_rows, held, later, *messages, spre)))


def finish_kernel(
    blocks, driven_ref, dmix_ref, mixed_ref, pre_ref, value_ref, dt_ref, cum_ref, step_ref, rows_ref, held_ref, end_ref, later_ref,
    vhalo_ref, kernel_ref, skip_ref, bias_ref, log_ref,
    grad_value_out, grad_step_out, last_out, first_out, kernel_out, small_out,
    held_next, pre_next, skip_sum, heads, kernel_sum, heads_t, edge_rows,
):
    b = pl.program_id(0)
    size, width = mixed_ref.shape
    state = held_ref.shape[1]
    final = b == blocks - 1

    @pl.when(b == 0)
    def _():
        heads[...] = head_map(width)
        heads_t[...] = (iota((width, LANES), 1) == iota((width, LANES), 0) // HEAD_DIM).astype(f32).astype(bf16)
        held_next[...] = end_ref[...]
        pre_next[...] = jnp.zeros(pre_next.shape, f32)
        kernel_sum[...] = jnp.zeros(kernel_sum.shape, f32)
        small_out[...] = jnp.zeros(small_out.shape, f32)
        skip_sum[...] = jnp.zeros(skip_sum.shape, f32)

    dt = dt_ref[...]
    cum = cum_ref[...]
    skip_row = jnp.broadcast_to(repeated(skip_ref[...]), (EDGE, LANES))
    wide = spread(jnp.concatenate([cum, dt, skip_row], axis=0), heads[...])
    b_parts = both_parts(rows_ref[:, :LANES])
    taps = kernel_ref[...].astype(f32)
    levels, throughs, boundaries = [], [], []
    for span in spans(width):
        cum_part = wide[:size, span]
        dt_wide = wide[size : 2 * size, span]
        skip = wide[2 * size : 2 * size + 1, span]
        end = cum_part[size - 1 : size]
        later = later_ref[0, :, span]
        held = held_ref[0, :, span]
        tail = jnp.exp(end - cum_part)
        dmix = dmix_ref[:, span]
        pre = pre_ref[:, span]
        pre_sig = sig(pre)
        conv = pre * pre_sig
        driven = conv * dt_wide
        later_high, later_low = split2(later)
        across = jnp.concatenate([later_high, later_low], axis=1)
        ddriven = driven_ref[:, span] + tail * fold(dot(b_parts, jnp.concatenate([across, across], axis=0)))
        skip_sum[:, span] = skip_sum[:, span] + by_eights(dmix * conv)
        levels.append(both_parts(dmix * (mixed_ref[:, span] - skip * conv) - driven * ddriven))
        throughs.append(both_parts(ddriven * conv))
        boundaries.append(both_parts(by_eights(later * held_next[:, span])))
        held_next[:, span] = held

        dpre = (ddriven * dt_wide + skip * dmix) * (pre_sig * (1.0 + pre * (1.0 - pre_sig)))
        extended = jnp.concatenate([dpre, pre_next[:, span]], axis=0)
        pre_next[:, span] = dpre[:EDGE]
        value = value_ref[:, span].astype(f32)
        dvalue = jnp.zeros((size, LANES), f32)
        for k in range(CONV):
            shifted = extended[CONV - 1 - k : CONV - 1 - k + size]
            dvalue = dvalue + taps[k : k + 1, span] * shifted
            kernel_sum[k, :, span] = kernel_sum[k, :, span] + by_eights(value * shifted)
        grad_value_out[:, span] = dvalue.astype(bf16)
        edge_rows[:, span] = dvalue[-2 * EDGE :]

    side = lambda parts: jnp.concatenate(parts, axis=1)
    picks = jnp.concatenate([heads_t[span] for span in spans(width) for _ in range(2)], axis=0)
    reduced = dot(jnp.concatenate([side(levels), side(throughs), side(boundaries)], axis=0), picks)
    level, through, boundary = reduced[:size], reduced[size : 2 * size], reduced[2 * size :]
    boundary = jnp.sum(boundary, axis=0, keepdims=True)
    upper = (iota((size, size), 1) >= iota((size, size), 0)).astype(f32).astype(bf16)
    ddecay = exact_dot(upper, level, NN) + boundary
    rate = jnp.exp(repeated(log_ref[...]))
    dstep = (through - ddecay * rate) * sig(step_ref[...] + repeated(bias_ref[...]))
    grad_step_out[...] = dstep[:, : grad_step_out.shape[1]].astype(bf16)
    small_out[1:2] = small_out[1:2] + jnp.sum(dstep, axis=0, keepdims=True)
    small_out[2:3] = small_out[2:3] + jnp.sum(-ddecay * dt * rate, axis=0, keepdims=True)

    @pl.when(b == 0)
    def _():
        last_out[...] = edge_rows[...]

    @pl.when(final)
    def _():
        first = pre_next[...]
        first_out[...] = first
        ahead = jnp.concatenate([jnp.zeros((EDGE, width), f32), first], axis=0)
        halo = vhalo_ref[...].astype(f32)[-EDGE:]
        kernel_out[...] = jnp.zeros(kernel_out.shape, f32)
        for k in range(CONV):
            shifted = ahead[CONV - 1 - k : CONV - 1 - k + EDGE]
            kernel_out[k : k + 1] = jnp.sum(kernel_sum[k] + halo * shifted, axis=0, keepdims=True)
        high, middle, low = split3(skip_sum[...])
        summed = dot(high, heads[...], NT) + (dot(middle, heads[...], NT) + dot(low, heads[...], NT))
        small_out[0:1] = jnp.sum(summed, axis=0, keepdims=True)


def finish(plan, count, wide_operands, grad_driven, grad_mixed, mixed, pre, value_in, dt, cum, step_raw, state_rows, held, end_state, later,
           vhalo, input_kernel, skip_gain, step_bias, decay_log):
    tokens, inner = mixed.shape
    blocks, state, _ = held.shape
    head_count = skip_gain.shape[1]
    width = wide_operands[0].shape[1]
    tile = width // count
    at = lambda b: jnp.maximum(blocks - 1 - b, 0)
    by_rows = lambda cols: pl.BlockSpec((BLOCK, cols), lambda b, plan: (at(b), 0))
    state_block = pl.BlockSpec((1, state, inner), lambda b, plan: (at(b), 0, 0))
    moving = pl.BlockSpec((tokens, tile), lambda b, plan: (0, jnp.bitwise_xor(plan[1], jnp.maximum(b - blocks, 0))))
    still = pl.BlockSpec((tokens, tile), lambda b, plan: (0, plan[0]))
    wide, narrow = by_rows(inner), by_rows(LANES)
    operands = (grad_driven, grad_mixed, mixed, pre, value_in, dt, cum, step_raw, state_rows, held, end_state, later,
                vhalo, input_kernel, skip_gain, step_bias, decay_log)
    outs = [
        (wide, jax.ShapeDtypeStruct((tokens, inner), bf16)),
        (by_rows(head_count), jax.ShapeDtypeStruct((tokens, head_count), bf16)),
    ]
    for shape in ((2 * EDGE, inner), (EDGE, inner), (EDGE, inner), (EDGE, LANES), *[(2 * tile, tile)] * 4):
        outs.append((pl.BlockSpec(shape, lambda b, plan: (0, 0)), jax.ShapeDtypeStruct(shape, f32)))

    def body(plan_ref, *refs):
        b = pl.program_id(0)
        ins, wide_ins, rest = refs[:17], refs[17:25], refs[25:]

        @pl.when(b < blocks)
        def _():
            finish_kernel(blocks, *ins, *rest[:6], *rest[10:])

        @pl.when(b >= blocks)
        def _():
            wide_weights_kernel(b - blocks, *wide_ins, *rest[6:10])

    return scalar_call(
        body, plan, tuple(map(in_hbm, (*operands, *wide_operands))),
        [wide, wide, wide, wide, wide, narrow, narrow, narrow, by_rows(2 * state), state_block, all_of(end_state), state_block,
         *[all_of(a) for a in operands[12:]], moving, moving, still, still, still, still, moving, moving],
        [o[0] for o in outs], [o[1] for o in outs], grid=(blocks + count,),
        scratch=[
            pltpu.VMEM((state, inner), f32),
            pltpu.VMEM((EDGE, inner), f32),
            pltpu.VMEM((EDGE, inner), f32),
            pltpu.VMEM((LANES, inner), bf16),
            pltpu.VMEM((CONV, EDGE, inner), f32),
            pltpu.VMEM((inner, LANES), bf16),
            pltpu.VMEM((2 * EDGE, inner), f32),
        ],
        limit=44, micros=0,
    )


def from_before(value, axis, by=1):
    count = lax.axis_size(axis)
    return lax.ppermute(value, axis, [(i, i + by) for i in range(count - by)])


def from_after(value, axis, by=1):
    count = lax.axis_size(axis)
    return lax.ppermute(value, axis, [(i + by, i) for i in range(count - by)])


def from_all(value, axis):
    count = lax.axis_size(axis)
    return [lax.ppermute(value, axis, [(i, (i + by) % count) for i in range(count)]) for by in range(1, count)]


def after(first, then):
    return lax.optimization_barrier((first, then))[1]


def swapped(value, axis, flip):
    return lax.ppermute(value, axis, [(i, i ^ flip) for i in range(lax.axis_size(axis))])


def own_part(array, axis_name, dim):
    size = array.shape[dim] // lax.axis_size(axis_name)
    return lax.dynamic_slice_in_dim(array, lax.axis_index(axis_name) * size, size, dim)


def first_kernel(plan_ref, part_ref, out_ref):
    out_ref[...] = part_ref[0].astype(bf16)


def line_first(parts, axis):
    count, tokens, width = parts.shape
    plan = jnp.where(lax.axis_index(axis) == 0, count - 1, 0).astype(jnp.int32).reshape(1)
    tile = min(tokens, 512)
    sent = pl.pallas_call(
        first_kernel,
        grid_spec=pltpu.PrefetchScalarGridSpec(
            num_scalar_prefetch=1,
            grid=(tokens // tile,),
            in_specs=[pl.BlockSpec((1, tile, width), lambda b, plan: (plan[0], b, 0))],
            out_specs=pl.BlockSpec((tile, width), lambda b, plan: (b, 0)),
        ),
        out_shape=jax.ShapeDtypeStruct((tokens, width), bf16),
        compiler_params=params(8),
        cost_estimate=cost(0),
    )(plan, in_hbm(parts))
    return sent


def line_step(parts, step, arrived, axis):
    count, tokens, width = parts.shape
    place = lax.axis_index(axis)
    plan = jnp.clip(jnp.stack([count - step + place, step - count + place]), 0, count - 1).astype(jnp.int32)
    if step == 2:
        arrived = [arrived, arrived]

    def body(plan_ref, up_ref, down_ref, up_in, down_in, up_out, down_out):
        up, down = up_in[...].astype(f32), down_in[...].astype(f32)
        if step == 2:
            up = jnp.where(plan_ref[2] == 1, up, 0.0)
            down = jnp.where(plan_ref[2] == count - 2, down, 0.0)
        up_out[...] = (up_ref[0] + up).astype(bf16)
        down_out[...] = (down_ref[0] + down).astype(bf16)

    tile = min(tokens, 512)
    block = pl.BlockSpec((tile, width), lambda b, plan: (b, 0))
    up, down = pl.pallas_call(
        body,
        grid_spec=pltpu.PrefetchScalarGridSpec(
            num_scalar_prefetch=1,
            grid=(tokens // tile,),
            in_specs=[
                pl.BlockSpec((1, tile, width), lambda b, plan: (plan[0], b, 0)),
                pl.BlockSpec((1, tile, width), lambda b, plan: (plan[1], b, 0)),
                block,
                block,
            ],
            out_specs=[block, block],
        ),
        out_shape=[jax.ShapeDtypeStruct((tokens, width), bf16)] * 2,
        compiler_params=params(12),
        cost_estimate=cost(0),
    )(jnp.concatenate([plan, place.astype(jnp.int32).reshape(1)]), in_hbm(parts), in_hbm(parts), *arrived)
    return (up, down), [
        lax.ppermute(up, axis, [(k, k + 1) for k in range(step)]),
        lax.ppermute(down, axis, [(count - 1 - k, count - 2 - k) for k in range(step)]),
    ]


def input_kernel_body(
    pieces, plan_ref, gate_ref, value_ref, narrow_ref, x_ref, gain_ref, gate_w, value_w, state_w, step_w, part_out, row_out, col_out, narrow_w
):
    b = pl.program_id(0)
    size = value_ref.shape[0]

    @pl.when(b == 0)
    def _():
        col_out[...] = jnp.zeros(col_out.shape, f32)
        state2, steps = state_w.shape[1], step_w.shape[0]
        mine = take_columns(plan_ref[0], pieces, state2)
        beside = (iota((steps, LANES), 0) + state2 // pieces == iota((steps, LANES), 1)).astype(f32).astype(bf16)
        narrow_w[...] = (dot(state_w[...], mine) + dot(step_w[...], beside, TN)).astype(bf16)

    gate = gate_ref[...]
    value = value_ref[...]
    narrow = narrow_ref[...]
    x = x_ref[...].astype(f32)
    scaling = lax.rsqrt(jnp.mean(x * x, axis=-1, keepdims=True) + epsilon)
    part = x.shape[1] // pieces
    row = jnp.zeros((size, LANES), f32)
    for j in range(pieces):
        span = slice(j * part, (j + 1) * part)
        partial = dot(gate, gate_w[span, :], NT) + dot(value, value_w[span, :], NT) + dot(narrow, narrow_w[span, :], NT)
        part_out[j] = partial
        pulled = partial * x[:, span]
        gained = pulled * gain_ref[:, span]
        for inside in spans(part):
            row = row + gained[:, inside]
        col_out[:, span] = col_out[:, span] + by_eights(pulled * scaling)
    row_out[...] = exact_dot(jnp.ones((EDGE, LANES), bf16), row, NT)


def scalar_call(body, plan, operands, in_specs, out_specs, out_shape, grid=(1,), scratch=(), limit=16, micros=2):
    return pl.pallas_call(
        body,
        grid_spec=pltpu.PrefetchScalarGridSpec(
            num_scalar_prefetch=1, grid=grid, in_specs=in_specs, out_specs=out_specs, scratch_shapes=list(scratch)
        ),
        out_shape=out_shape,
        compiler_params=pltpu.CompilerParams(dimension_semantics=("arbitrary",) * len(grid), vmem_limit_bytes=limit * 1024 * 1024),
        cost_estimate=cost(micros),
    )(plan, *operands)


def all_of(a):
    return pl.BlockSpec(a.shape, lambda *_: (0,) * len(a.shape))


def take_columns(at, count, width):
    part = width // count
    lane = iota((width, LANES), 1)
    return ((iota((width, LANES), 0) == lane + at * part) & (lane < part)).astype(f32).astype(bf16)


def extended_rows(x, beyond):
    return jnp.concatenate([x, beyond, jnp.zeros((EDGE, x.shape[1]), f32)], axis=0)


def pieces_kernel(count, plan_ref, rows_ref, ahead_ref, *outs):
    tokens, state2 = rows_ref.shape
    extended = extended_rows(rows_ref[...], ahead_ref[:, :state2])
    size = extended.shape[0] // 2
    picks = [take_columns(lax.rem(plan_ref[0] + k, count), count, state2) for k in range(count)]
    none = jnp.zeros((state2, LANES // 2), bf16)
    half = LANES // 2
    upper = jnp.concatenate([jnp.concatenate([p[:, :half], none], axis=1) for p in picks], axis=1)
    lower = jnp.concatenate([jnp.concatenate([none, p[:, :half]], axis=1) for p in picks], axis=1)
    both = dot_exact(extended[:size], upper) + dot_exact(extended[size:], lower)
    for k, out in enumerate(outs):
        out[...] = both[:, k * LANES : (k + 1) * LANES]


def dot_exact(x, ones):
    high, middle, low = split3(x)
    return dot(high, ones) + (dot(middle, ones) + dot(low, ones))


def pieces_of(place, count, grad_rows, ahead):
    tokens, state2 = grad_rows.shape
    shape = jax.ShapeDtypeStruct((tokens // 2 + EDGE, LANES), f32)
    return scalar_call(
        functools.partial(pieces_kernel, count), place, (grad_rows, ahead), [all_of(grad_rows), all_of(ahead)],
        [all_of(shape)] * count, [shape] * count, limit=12, micros=0,
    )


def complete_kernel(ahead_ref, last_ref, taps_ref, value_ref, out_ref):
    fixed = last_ref[...]
    taps = taps_ref[...].astype(f32)
    extended = jnp.concatenate([jnp.zeros(last_ref.shape, f32), ahead_ref[...]], axis=0)
    for k in range(CONV):
        fixed = fixed + taps[k : k + 1] * extended[CONV - 1 - k : CONV - 1 - k + last_ref.shape[0]]
    out_ref[...] = fixed.astype(bf16)


def complete(ahead, last_rows, taps, grad_value):
    tokens, inner = grad_value.shape
    size = last_rows.shape[0]
    final_rows = pl.BlockSpec((size, inner), lambda b: (tokens // size - 1, 0))
    return pl.pallas_call(
        complete_kernel,
        grid=(1,),
        in_specs=[whole(ahead.shape), whole(last_rows.shape), whole(taps.shape), final_rows],
        out_specs=final_rows,
        out_shape=jax.ShapeDtypeStruct(grad_value.shape, bf16),
        input_output_aliases={3: 0},
        compiler_params=params(4),
        cost_estimate=cost(0),
    )(ahead, last_rows, taps, grad_value)


def three_parts(x):
    return jnp.concatenate(split3(x), axis=0)


def three_sum(parts):
    size = parts.shape[0] // 3
    parts = parts.astype(f32)
    return parts[:size] + (parts[size : 2 * size] + parts[2 * size :])


PACK = 16
SMALL = 48


def state_kernel_body(count, plan_ref, *refs):
    grads = refs[:count]
    spre_ref, input_ref, halo_ref, ahead_ref, taps_ref, step_ref, out_ref, taps_out = refs[count:]
    tokens, state2 = spre_ref.shape
    part = state2 // count
    pick = take_columns(plan_ref[0], count, state2)
    total = grads[0][...]
    for ref in grads[1:]:
        total = total + ref[...]
    total = jnp.concatenate([total, pltpu.roll(total, LANES // 2, 1)], axis=0)
    total = jnp.where(iota(total.shape, 1) < part, total, 0.0)
    pre = dot_exact(extended_rows(spre_ref[...], ahead_ref[:, state2:]), pick)
    s = sig(pre)
    through = total * (s * (1.0 + pre * (1.0 - s)))
    taps = dot(taps_ref[...], pick)
    inputs = dot(jnp.concatenate([halo_ref[...], input_ref[...]], axis=0), pick)
    steps = step_ref.shape[1]
    place = (iota((steps, LANES), 0) + part == iota((steps, LANES), 1)).astype(f32).astype(bf16)
    grad = dot(step_ref[...], place)
    own = through[:tokens]
    first = halo_ref.shape[0] - CONV + 1
    taps_out[...] = jnp.zeros(taps_out.shape, f32)
    for k in range(CONV):
        grad = grad + taps[k : k + 1] * through[CONV - 1 - k : CONV - 1 - k + tokens]
        taps_out[k : k + 1] = jnp.sum(own * inputs[first + k : first + k + tokens], axis=0, keepdims=True)
    out_ref[...] = grad.astype(bf16)


def state_back(place, grads, spre, state_in, halo, ahead, taps, grad_step):
    count = len(grads)
    tokens = spre.shape[0]
    shapes = [jax.ShapeDtypeStruct((tokens, LANES), bf16), jax.ShapeDtypeStruct((EDGE, LANES), f32)]
    operands = (*grads, spre, state_in, halo, ahead, taps, grad_step)
    return scalar_call(
        functools.partial(state_kernel_body, count), place, operands, [all_of(a) for a in operands],
        [all_of(a) for a in shapes], shapes, limit=16, micros=0,
    )


def sums_kernel(count, plan_ref, row_ref, col_ref, taps_ref, out_ref):
    state2 = out_ref.shape[1]
    tokens, width = row_ref.shape[1], col_ref.shape[1]
    packed = [row_ref[:1, i : i + state2] for i in range(0, tokens, state2)]
    col = jnp.sum(col_ref[...], axis=0, keepdims=True)
    packed += [col[:, i : i + state2] for i in range(0, width, state2)]
    high, middle, low = split3(taps_ref[:CONV])
    pick = take_columns(plan_ref[0], count, state2)
    packed.append(dot(high, pick, NT) + (dot(middle, pick, NT) + dot(low, pick, NT)))
    packed = jnp.concatenate(packed, axis=0)
    out_ref[...] = jnp.concatenate([packed, jnp.zeros((PACK - packed.shape[0], state2), f32)], axis=0)


def sums_of(place, count, row_sums, col_sums, taps_grad, state2):
    shape = jax.ShapeDtypeStruct((PACK, state2), f32)
    operands = (row_sums, col_sums, taps_grad)
    return scalar_call(
        functools.partial(sums_kernel, count), place, operands, [all_of(a) for a in operands], all_of(shape), shape,
        limit=8, micros=0,
    )


def small_kernel(count, given, tokens, plan_ref, *refs):
    parts, (kernel_ref, gain_ref, small_ref, sums_out, out_ref) = refs[:given], refs[given:]
    sums = parts[0][...]
    for ref in parts[1:]:
        sums = sums + ref[...]
    sums_out[...] = sums
    state2 = sums.shape[1]
    wide = state2 // LANES
    inner = kernel_ref.shape[1]
    rows_of = [kernel_ref[k : k + 1, span] for k in range(CONV) for span in spans(inner)]
    gain = jnp.sum(gain_ref[...], axis=0, keepdims=True)
    rows_of += [gain[:, span] for span in spans(inner)]
    rows_of += [small_ref[i : i + 1] for i in range(3)]
    first = tokens // state2
    last = PACK - 2 - CONV
    cols = [sums[r : r + 1, i * LANES : (i + 1) * LANES] for r in range(first, last) for i in range(wide)]
    quarter = len(cols) // count
    for i in range(quarter):
        chosen = jnp.zeros((1, LANES), f32)
        for q in range(count):
            chosen = jnp.where(plan_ref[0] == q, cols[q * quarter + i], chosen)
        rows_of.append(chosen)
    rows_of += [sums[last + k : last + k + 1, i * LANES : (i + 1) * LANES] for k in range(CONV) for i in range(wide)]
    rows_of.append(jnp.zeros((SMALL - len(rows_of), LANES), f32))
    out_ref[...] = jnp.concatenate(rows_of, axis=0)


def small_sums(place, count, tokens, parts, kernel_grad, gain_grad, small):
    shapes = [jax.ShapeDtypeStruct(parts[0].shape, f32), jax.ShapeDtypeStruct((SMALL, LANES), f32)]
    operands = tuple(map(in_hbm, (*parts, kernel_grad, gain_grad, small)))
    return scalar_call(
        functools.partial(small_kernel, count, len(parts), tokens), place, operands, [all_of(a) for a in operands],
        [all_of(a) for a in shapes], shapes, limit=8, micros=0,
    )


def wide_weights_kernel(k, normed_a, normed_b, gate_a, gate_b, out_a, out_b, cot_a, cot_b, *outs):
    tile = normed_a.shape[1]
    gate_keep, gate_send, out_keep, out_send = outs
    gate = dot(normed_a[...], gate_a[...], TN) + dot(normed_b[...], gate_b[...], TN)
    out = dot(out_a[...], cot_a[...], TN) + dot(out_b[...], cot_b[...], TN)
    targets = ((gate_keep, 0, out_keep, 0), (gate_send, 0, out_keep, 1), (gate_keep, 1, out_send, 0), (gate_send, 1, out_send, 1))
    for i, (gate_ref, gate_at, out_ref, out_at) in enumerate(targets):

        @pl.when(k == i)
        def _(gate_ref=gate_ref, gate_at=gate_at, out_ref=out_ref, out_at=out_at):
            gate_ref[gate_at * tile : (gate_at + 1) * tile] = gate
            out_ref[out_at * tile : (out_at + 1) * tile] = out


def value_weights_kernel(k, normed_a, normed_b, value_a, value_b, first_keep, first_send, second_keep, second_send):
    total = dot(normed_a[...], value_a[...], TN) + dot(normed_b[...], value_b[...], TN)
    half = total.shape[0] // 2
    targets = ((first_keep, 0, second_keep, 0), (first_send, 0, second_keep, 1), (first_keep, 1, second_send, 0), (first_send, 1, second_send, 1))
    for i, (first_ref, first_at, second_ref, second_at) in enumerate(targets):

        @pl.when(k == i)
        def _(first_ref=first_ref, first_at=first_at, second_ref=second_ref, second_at=second_at):
            first_ref[first_at * half : (first_at + 1) * half] = total[:half]
            second_ref[second_at * half : (second_at + 1) * half] = total[half:]


def input_partials(place, pieces, grad_gate, grad_value, narrow, residual, pre_gain, gate_weight, input_weight, state_weight, step_weight):
    tokens, width = residual.shape
    inner = grad_gate.shape[1]
    tile = min(tokens, 256)
    by_rows = lambda cols: pl.BlockSpec((tile, cols), lambda b, plan: (b, 0))
    return scalar_call(
        functools.partial(input_kernel_body, pieces), place,
        (in_hbm(grad_gate), grad_value, narrow, in_hbm(residual), pre_gain, gate_weight, input_weight, state_weight, step_weight),
        [
            by_rows(inner), by_rows(inner), by_rows(narrow.shape[1]), by_rows(width),
            *[all_of(a) for a in (pre_gain, gate_weight, input_weight, state_weight, step_weight)],
        ],
        [
            pl.BlockSpec((pieces, tile, width // pieces), lambda b, plan: (0, b, 0)),
            pl.BlockSpec((EDGE, tile), lambda b, plan: (0, b)),
            pl.BlockSpec((EDGE, width), lambda b, plan: (0, 0)),
        ],
        [
            pltpu.HBM((pieces, tokens, width // pieces), f32),
            jax.ShapeDtypeStruct((EDGE, tokens), f32),
            jax.ShapeDtypeStruct((EDGE, width), f32),
        ],
        grid=(tokens // tile,), scratch=[pltpu.VMEM((width, LANES), bf16)], limit=36, micros=0,
    )


def value_weights(plan, count, normed, grad_value):
    tokens, width = normed[0].shape
    tile = width // count
    half = grad_value[0].shape[1] // 2
    moving = pl.BlockSpec((tokens, tile), lambda k, plan: (0, jnp.bitwise_xor(plan[1], k)))
    still = pl.BlockSpec((tokens, half), lambda k, plan: (0, plan[0]))
    shape = jax.ShapeDtypeStruct((tile, half), f32)

    def body(plan_ref, *refs):
        value_weights_kernel(pl.program_id(0), *refs)

    return scalar_call(
        body, plan, (*map(in_hbm, normed), *grad_value), [moving, moving, still, still],
        [all_of(shape)] * 4, [shape] * 4, grid=(count,), limit=20, micros=0,
    )


def narrow_weights_kernel(plan_ref, normed_a, normed_b, narrow_a, narrow_b, small_a, small_b, keep_out, send_out):
    k = pl.program_id(0)
    tile = normed_a.shape[1]
    total = dot(narrow_a[...], normed_a[...], TN) + dot(narrow_b[...], normed_b[...], TN)
    small = small_a[...] + small_b[...]
    per_row = tile // LANES
    size = keep_out.shape[0] // 2
    for i, (ref, at) in enumerate(((keep_out, 0), (send_out, 0), (keep_out, size), (send_out, size))):

        @pl.when(k == i)
        def _(ref=ref, at=at):
            ref[at : at + LANES] = total
            for j in range(per_row):
                ref[at + LANES : at + size, j * LANES : (j + 1) * LANES] = small[j * SMALL // per_row : (j + 1) * SMALL // per_row]


def narrow_weights(plan, count, normed, narrow, small):
    tokens, width = normed[0].shape
    tile = width // count
    moving = pl.BlockSpec((tokens, tile), lambda k, plan: (0, jnp.bitwise_xor(plan[1], k)))
    shape = jax.ShapeDtypeStruct((2 * (LANES + SMALL * LANES // tile), tile), f32)
    return scalar_call(
        narrow_weights_kernel, plan, (*map(in_hbm, normed), *narrow, *small), [moving, moving, *[all_of(a) for a in (*narrow, *small)]],
        [all_of(shape)] * 2, [shape] * 2, grid=(count,), limit=16, micros=0,
    )


def pair_kernel(keep_ref, got_ref, stay_out, away_out):
    size = stay_out.shape[0]
    stay_out[...] = keep_ref[:size] + got_ref[:size]
    away_out[...] = keep_ref[size:] + got_ref[size:]


def pair_sums(keep, got):
    shape = jax.ShapeDtypeStruct((keep.shape[0] // 2, keep.shape[1]), f32)
    return pl.pallas_call(
        pair_kernel,
        out_shape=[shape, shape],
        compiler_params=pltpu.CompilerParams(vmem_limit_bytes=6 * 1024 * 1024),
        cost_estimate=cost(0),
    )(keep, got)


def over_dp(total):
    step = 2
    while step < lax.axis_size("dp"):
        total = total + swapped(total, "dp", step)
        step *= 2
    return total


def halves_kernel(own_a, own_b, got_a, got_b, stay_out, away_a, away_b):
    half = away_a.shape[0]
    stay_out[:half] = own_a[:half] + got_a[:half]
    stay_out[half:] = own_b[:half] + got_b[:half]
    away_a[...] = own_a[half:] + got_a[half:]
    away_b[...] = own_b[half:] + got_b[half:]


def halves(own_a, own_b, got_a, got_b):
    size, cols = own_a.shape
    half = jax.ShapeDtypeStruct((size // 2, cols), f32)
    return pl.pallas_call(
        halves_kernel,
        out_shape=[pltpu.HBM((size, cols), f32), *[pltpu.HBM(half.shape, f32)] * 2],
        compiler_params=pltpu.CompilerParams(vmem_limit_bytes=16 * 1024 * 1024),
        cost_estimate=cost(0),
    )(*map(in_hbm, (own_a, own_b, got_a, got_b)))


def add_kernel(stay, got_a, got_b, out):
    half = got_a.shape[0]
    out[:half] = (stay[:half] + got_a[...]).astype(out.dtype)
    out[half:] = (stay[half:] + got_b[...]).astype(out.dtype)


def add_halves(stay, got_a, got_b, dtype):
    return pl.pallas_call(
        add_kernel,
        out_shape=jax.ShapeDtypeStruct(stay.shape, dtype),
        compiler_params=pltpu.CompilerParams(vmem_limit_bytes=16 * 1024 * 1024),
        cost_estimate=cost(0),
    )(stay, got_a, got_b)


def summed(stay, got_a, got_b):
    if lax.axis_size("dp") == 2:
        return add_halves(stay, got_a, got_b, bf16)
    return over_dp(add_halves(stay, got_a, got_b, f32)).astype(bf16)


def ordered(first, here, there):
    here, there = here.astype(f32), there.astype(f32)
    return jnp.where(first, here, there), jnp.where(first, there, here)


def joined_kernel(*refs):
    *parts, out, done = refs
    rows = parts[0].shape[0]
    copies = [
        pltpu.make_async_copy(part, out.at[pl.ds(i * rows, rows)], done.at[i]) for i, part in enumerate(parts)
    ]
    for copy in copies:
        copy.start()
    for copy in copies:
        copy.wait()


def joined(*parts):
    rows, width = parts[0].shape
    return pl.pallas_call(
        joined_kernel,
        out_shape=pltpu.HBM((len(parts) * rows, width), parts[0].dtype),
        in_specs=[pl.BlockSpec(memory_space=pl.ANY)] * len(parts),
        out_specs=pl.BlockSpec(memory_space=pl.ANY),
        scratch_shapes=[pltpu.SemaphoreType.DMA((len(parts),))],
        compiler_params=pltpu.CompilerParams(vmem_limit_bytes=2**20),
    )(*parts)


def wide_together_kernel(plan_ref, here, there, gate_out, out_out):
    tile = gate_out.shape[0]
    k = pl.program_id(0)
    first = plan_ref[0] == 0
    half = gate_out.shape[1] // 2
    span = pl.ds(pl.multiple_of(k * 2 * tile, 2 * EDGE), tile)
    gate_out[:, :half], gate_out[:, half:] = ordered(first, here[span], there[span])
    span = pl.ds(pl.multiple_of(k * 2 * tile + tile, 2 * EDGE), tile)
    out_out[:tile], out_out[tile:] = ordered(first, here[span], there[span])


def wide_together(plan, count, here, there):
    tile = here.shape[0] // (2 * count)
    width, inner = tile * count, 2 * here.shape[1]
    return scalar_call(
        wide_together_kernel, plan, (here, there), [all_of(here), all_of(there)],
        [pl.BlockSpec((tile, inner), lambda q, plan: (q, 0)), pl.BlockSpec((inner, tile), lambda q, plan: (0, q))],
        [jax.ShapeDtypeStruct((width, inner), f32), jax.ShapeDtypeStruct((inner, width), f32)],
        grid=(count,), limit=24, micros=0,
    )


def narrow_together_kernel(plan_ref, here, there, input_out, state_out, step_out):
    tile = input_out.shape[0]
    k = jnp.bitwise_xor(pl.program_id(0), plan_ref[1])
    half = input_out.shape[1] // 2
    start = pl.multiple_of(k * (tile + LANES), 2 * EDGE)
    span = pl.ds(start, tile)
    input_out[:, :half], input_out[:, half:] = ordered(plan_ref[0] == 0, here[span], there[span])
    rest = here[pl.ds(pl.multiple_of(start + tile, 2 * EDGE), LANES)].astype(f32)
    states = state_out.shape[0]
    state_out[...] = rest[:states]
    step_out[...] = rest[states : states + step_out.shape[0]]


def narrow_together(plan, count, here, there, state_part, steps):
    tile = here.shape[0] // count - LANES
    width, inner = tile * count, 2 * here.shape[1]
    by_lane = lambda size: pl.BlockSpec((size, tile), lambda q, plan: (0, q))
    return scalar_call(
        narrow_together_kernel, plan, (here, there), [all_of(here), all_of(there)],
        [pl.BlockSpec((tile, inner), lambda q, plan: (q, 0)), by_lane(state_part), by_lane(steps)],
        [
            jax.ShapeDtypeStruct((width, inner), f32),
            jax.ShapeDtypeStruct((state_part, width), f32),
            jax.ShapeDtypeStruct((steps, width), f32),
        ],
        grid=(count,), limit=20, micros=0,
    )


def final_kernel(count, plan_ref, part_ref, up_ref, down_ref, x_ref, mine_ref, cot_ref, gain_ref, sums_ref, out_ref):
    b = pl.program_id(0)
    size, part = up_ref.shape
    x = x_ref[...].astype(f32)
    width = x.shape[1]
    scaling = lax.rsqrt(jnp.mean(x * x, axis=-1, keepdims=True) + epsilon)
    row = jnp.zeros((1, size), f32)
    for q in range(count):
        row = jnp.where(b == q, sums_ref[q : q + 1], row)
    pull = column(row) * ((scaling * scaling * scaling) / width)
    for span in spans(part):
        normed_grad = part_ref[0, :, span] + up_ref[:, span].astype(f32) + down_ref[:, span].astype(f32)
        out_ref[:, span] = (
            cot_ref[:, span].astype(f32) + scaling * gain_ref[:, span] * normed_grad - mine_ref[:, span].astype(f32) * pull
        )


def final(place, parts, arrived, residual, cotangent, pre_gain, sums):
    count, tokens, part = parts.shape
    size = sums.shape[1]
    mine = pl.BlockSpec((size, part), lambda b, plan: (b, plan[0]))
    own = pl.BlockSpec((size, part), lambda b, plan: (b, 0))
    return scalar_call(
        functools.partial(final_kernel, tokens // size), place,
        (in_hbm(parts), *arrived, in_hbm(residual), in_hbm(residual), in_hbm(cotangent), pre_gain, sums),
        [
            pl.BlockSpec((1, size, part), lambda b, plan: (plan[0], b, 0)),
            own,
            own,
            pl.BlockSpec((size, residual.shape[1]), lambda b, plan: (b, 0)),
            mine,
            mine,
            pl.BlockSpec((1, part), lambda b, plan: (0, plan[0])),
            all_of(sums),
        ],
        own,
        jax.ShapeDtypeStruct((tokens, part), f32),
        grid=(tokens // size,), limit=16, micros=0,
    )


def per_device(residual, pre_gain, gate_weight, input_weight, state_weight, step_weight, input_kernel, state_kernel,
               step_bias, decay_log, skip_gain, norm_gain, out_weight, cotangent):
    residual, cotangent = residual[0], cotangent[0]
    tokens, width = residual.shape
    tensor_size = lax.axis_size("tensor")
    ctx_size = lax.axis_size("ctx")
    inner = gate_weight.shape[1]
    inner_total = inner * tensor_size
    head_count = step_weight.shape[1]
    state2 = state_weight.shape[1]
    state_part = state2 // tensor_size
    row = lambda v: v.reshape(1, -1)
    plan = jnp.stack([lax.axis_index("dp") % 2, lax.axis_index("ctx"), lax.axis_index("tensor")]).astype(jnp.int32)
    place = lax.axis_index("tensor").astype(jnp.int32).reshape(1)

    halo = from_before(residual[-2 * EDGE :], "ctx")
    other_cotangent = swapped(cotangent, "dp", 1)
    step_weight = step_weight.T
    normed, value_in, state_in, step_raw = project(residual, row(pre_gain), input_weight, state_weight, step_weight)
    other_normed = swapped(normed, "dp", 1)
    conv, pre, state_rows, spre, dt, cum, cumt, held, message, vhalo, shalo = local_states(
        value_in, state_in, step_raw, halo, row(pre_gain), input_weight, state_weight, input_kernel, state_kernel,
        row(step_bias), row(decay_log)
    )
    messages = [from_before(message, "ctx", by) for by in range(1, ctx_size)]
    gate_in, grad_normed = beside(after(message, normed), gate_weight, cotangent, out_weight)
    intra = inner_forward(head_count, conv, dt, state_rows, cum, cumt, row(skip_gain))
    messages = after((gate_in, intra, other_cotangent), messages)
    mixed, sums, held, end_state = combine(
        intra, state_rows, cum, held, message, messages, gate_in, grad_normed, row(norm_gain)
    )
    all_sums = [sums, *after(other_normed, from_all(sums, "tensor"))]
    normed_out, grad_gate, grad_mixed, later, message, gain_grad = gate_back(
        mixed, gate_in, grad_normed, state_rows, cum, row(norm_gain), all_sums, inner_total
    )
    messages = [from_after(message, "ctx", by) for by in range(1, ctx_size)]

    partial_out, grad_driven, grad_rows = inner_back(
        normed_out, out_weight, conv, dt, state_rows, cum, cumt, after(message, grad_mixed)
    )
    messages = after(grad_driven, messages)
    partial_out, gate_there, out_there = after(messages, (partial_out, grad_gate, normed_out))
    resid_part = own_part(residual, "tensor", 1).astype(f32)
    branch = lax.psum_scatter(partial_out, "tensor", scatter_dimension=1, tiled=True)
    other_gate = swapped(gate_there, "dp", 1)
    other_out = swapped(out_there, "dp", 1)
    grad_rows, later, first_rows = rows_back(grad_rows, grad_mixed, conv, dt, cum, state_rows, held, later, messages, spre)
    ahead = from_after(first_rows, "ctx")
    pieces = list(pieces_of(place, tensor_size, grad_rows, ahead))
    arrived = [
        lax.ppermute(pieces[k], "tensor", [(i, (i + k) % tensor_size) for i in range(tensor_size)]) for k in range(1, tensor_size)
    ]
    (grad_value, grad_step, last_rows, first_rows, kernel_grad, small, gate_keep, gate_send, out_keep, out_send) = finish(
        plan, ctx_size, (normed, other_normed, grad_gate, other_gate, normed_out, other_out, cotangent, other_cotangent),
        grad_driven, after(pieces[0], grad_mixed), mixed, pre, value_in, dt, cum, step_raw, state_rows, held, end_state, later,
        vhalo, input_kernel, row(skip_gain), row(step_bias), row(decay_log)
    )
    ahead_value = from_after(first_rows, "ctx")
    arrived = after(first_rows, arrived)
    narrow, taps_grad = state_back(place, [pieces[0], *arrived], spre, state_in, shalo, ahead, state_kernel, grad_step)
    grad_value = complete(after(narrow, ahead_value), last_rows, input_kernel, grad_value)
    gate_send, out_send = after(arrived, (gate_send, out_send))
    gate_got, out_got = swapped(gate_send, "ctx", 1), swapped(out_send, "ctx", 2)
    other_value = swapped(grad_value, "dp", 1)
    other_narrow = swapped(narrow, "dp", 1)
    gate_send, out_send = after(grad_value, (gate_send, out_send))
    gate_got, out_got = swapped(gate_send, "ctx", 1), swapped(out_send, "ctx", 2)
    first_keep, first_send, second_keep, second_send = value_weights(
        plan, ctx_size, (normed, other_normed), (grad_value, other_value)
    )
    first_got, second_got = swapped(first_send, "ctx", 1), swapped(second_send, "ctx", 2)
    parts, row_sums, col_sums = input_partials(
        place, tensor_size, grad_gate, after((first_keep, other_narrow), grad_value), narrow, residual, row(pre_gain), gate_weight,
        input_weight, state_weight, step_weight
    )
    packed = sums_of(place, tensor_size, row_sums, col_sums, taps_grad, state2)
    packed = [packed, *from_all(packed, "tensor")]
    sent = line_first(after(packed[0], parts), "tensor")
    packed, sent = after(sent, packed), after(packed, sent)
    moving = lax.ppermute(sent, "tensor", [(0, 1), (tensor_size - 1, tensor_size - 2)])
    wide_stay, gate_away, out_away = halves(gate_keep, out_keep, *after(sent, (gate_got, out_got)))
    gate_got, out_got = swapped(gate_away, "ctx", 2), swapped(out_away, "ctx", 1)
    value_stay, first_away, second_away = halves(first_keep, second_keep, *after(wide_stay, (first_got, second_got)))
    first_got, second_got = swapped(first_away, "ctx", 2), swapped(second_away, "ctx", 1)
    sums, small = small_sums(place, tensor_size, tokens, after(value_stay, packed), kernel_grad, gain_grad, small)
    other_small = swapped(small, "dp", 1)
    narrow_keep, narrow_send = narrow_weights(
        after(small, plan), ctx_size, (normed, other_normed), (narrow, other_narrow), (small, other_small)
    )
    narrow_got = swapped(narrow_send, "ctx", 1)
    moving, gate_got, out_got, first_got, second_got = lax.optimization_barrier(
        after(narrow_keep, (moving, gate_got, out_got, first_got, second_got))
    )
    sent, moving = line_step(parts, 2, moving, "tensor")
    value_chunk = summed(value_stay, *after(sent, (first_got, second_got)))
    wide_chunk = summed(wide_stay, *after(value_chunk, (gate_got, out_got)))
    wide_here = lax.all_gather(wide_chunk, "ctx", tiled=True)
    moving, narrow_got = lax.optimization_barrier(after(wide_chunk, (moving, narrow_got)))
    narrow_stay, narrow_away = pair_sums(narrow_keep, narrow_got)
    narrow_got = swapped(narrow_away, "ctx", 2)
    sent, moving = line_step(parts, 3, after(narrow_stay, moving), "tensor")
    output = (resid_part + after(sent, branch)).astype(bf16)
    narrow_total = over_dp(narrow_stay + after(output, narrow_got))
    chunk = jnp.concatenate([value_chunk, narrow_total[:LANES].astype(bf16)], axis=0)
    chunks = [swapped(chunk, "ctx", k) for k in range(1, ctx_size)]
    small_total = narrow_total[LANES:]
    small_total = jnp.concatenate([small_total[:, i : i + LANES] for i in range(0, small_total.shape[1], LANES)], axis=0)
    wide_rows = inner // LANES
    at = CONV * wide_rows
    kernel_grad = small_total[:at].reshape(CONV, inner)
    gain_grad = small_total[at : at + wide_rows].reshape(inner)
    at += wide_rows
    small = small_total[at : at + 3, :head_count]
    at += 3
    gain_rows = width // tensor_size // LANES
    pre_gain_grad = small_total[at : at + gain_rows].reshape(width // tensor_size)
    at += gain_rows
    taps_grad = small_total[at : at + CONV * state2 // LANES].reshape(CONV, state2)
    smalls = (pre_gain_grad, kernel_grad, taps_grad, small[1], small[2], small[0], gain_grad)
    moving, chunks, smalls = lax.optimization_barrier((moving, chunks, smalls))
    narrow_here = joined(chunk, *chunks)
    narrow_there = swapped(narrow_here, "dp", 1)
    wide_here = after(chunks, wide_here)
    wide_there = swapped(wide_here, "dp", 1)
    input_grad = final(place, parts, after(narrow_here, moving), residual, cotangent, row(pre_gain), sums)
    gate_weight_grad, out_weight_grad = wide_together(after(input_grad, plan), ctx_size, wide_here, wide_there)
    input_weight_grad, state_weight_grad, step_weight_grad = narrow_together(
        plan, ctx_size, narrow_here, after(gate_weight_grad, narrow_there), state_part, head_count
    )
    return (
        output[None],
        input_grad[None],
        smalls[0],
        gate_weight_grad,
        input_weight_grad,
        state_weight_grad.T,
        step_weight_grad.T,
        *smalls[1:],
        out_weight_grad,
    )


def solution(mesh):
    in_specs = (
        P("dp", "ctx", None),
        P(),
        P(None, "tensor"),
        P(None, "tensor"),
        P(),
        P(None, "tensor"),
        P(None, "tensor"),
        P(),
        P("tensor"),
        P("tensor"),
        P("tensor"),
        P("tensor"),
        P("tensor", None),
        P("dp", "ctx", None),
    )
    out_specs = (
        P("dp", "ctx", "tensor"),
        P("dp", "ctx", "tensor"),
        P("tensor"),
        P(None, "tensor"),
        P(None, "tensor"),
        P(None, "tensor"),
        P(None, "tensor"),
        P(None, "tensor"),
        P(),
        P("tensor"),
        P("tensor"),
        P("tensor"),
        P("tensor"),
        P("tensor", None),
    )
    return jax.shard_map(per_device, mesh=mesh, in_specs=in_specs, out_specs=out_specs, check_vma=False)
```

```python
import functools

import jax
import jax.numpy as jnp
from jax import lax
from jax.experimental import pallas as pl
from jax.experimental.pallas import tpu as pltpu
from jax.sharding import PartitionSpec as P

HEAD_DIM = 64
CONV = 4
EDGE = 8
BLOCK = 128
LANES = 128
epsilon = 1e-05
f32 = jnp.float32
bf16 = jnp.bfloat16

NN = (((1,), (0,)), ((), ()))
NT = (((1,), (1,)), ((), ()))
TN = (((0,), (0,)), ((), ()))


def dot(a, b, dims=NN):
    return lax.dot_general(a, b, dims, preferred_element_type=f32)


def split2(x):
    high = x.astype(bf16)
    return high, (x - high.astype(f32)).astype(bf16)


def split3(x):
    high = x.astype(bf16)
    rest = x - high.astype(f32)
    middle = rest.astype(bf16)
    return high, middle, (rest - middle.astype(f32)).astype(bf16)


def dot3(a, b, dims=NN):
    ah, al = split2(a)
    bh, bl = split2(b)
    return dot(ah, bh, dims) + (dot(ah, bl, dims) + dot(al, bh, dims))


def both_parts(x):
    return jnp.concatenate(split2(x), axis=1)


def fold(product):
    half = product.shape[1] // 2
    return product[:, :half] + product[:, half:]


def wide_dot(parts, x):
    across = both_parts(x)
    return fold(dot(parts, jnp.concatenate([across, across], axis=0)))


def exact_dot(ones, x, dims):
    high, middle, low = split3(x)
    return dot(ones, high, dims) + (dot(ones, middle, dims) + dot(ones, low, dims))


def iota(shape, axis):
    return lax.broadcasted_iota(jnp.int32, shape, axis)


REPEAT = 16


def head_map(width):
    lane = iota((LANES, width), 0)
    mine = (lane % REPEAT == iota((LANES, width), 1) // HEAD_DIM) & (lane < 3 * REPEAT)
    return mine.astype(f32).astype(bf16)


def spread(per_head, heads):
    high = per_head.astype(bf16).astype(f32)
    rest = per_head - high
    middle = rest.astype(bf16).astype(f32)
    group = iota(per_head.shape, 1) // REPEAT
    parts = jnp.where(group == 0, high, jnp.where(group == 1, middle, rest - middle))
    return dot(parts.astype(bf16), heads)


def repeated(row):
    group = jnp.concatenate([row, jnp.zeros((1, REPEAT - row.shape[1]), f32)], axis=1)
    return jnp.concatenate([group] * (LANES // REPEAT), axis=1)


def sig(v):
    return jax.nn.sigmoid(v)


def cost(micros):
    return pl.CostEstimate(flops=micros * 900_000_000, bytes_accessed=micros * 3_000_000, transcendentals=0)


def params(limit=20):
    return pltpu.CompilerParams(
        dimension_semantics=("arbitrary",), vmem_limit_bytes=limit * 1024 * 1024
    )


def in_hbm(x):
    return pltpu.with_memory_space_constraint(x, pltpu.HBM)


def whole(shape):
    return pl.BlockSpec(shape, lambda b: (0,) * len(shape))


def rows(size, width, count=0):
    if count:
        return pl.BlockSpec((size, width), lambda b: (count - 1 - b, 0))
    return pl.BlockSpec((size, width), lambda b: (b, 0))


def spans(width):
    return [slice(i * LANES, (i + 1) * LANES) for i in range(width // LANES)]


def by_eights(x):
    return jnp.sum(x.reshape(x.shape[0] // EDGE, EDGE, x.shape[1]), axis=0)


def norm_rows(x, gain):
    scaling = lax.rsqrt(jnp.mean(x * x, axis=-1, keepdims=True) + epsilon)
    return (x * scaling * gain).astype(bf16)


def project_kernel(x_ref, gain_ref, value_ref, state_ref, step_ref, normed_out, value_out, state_out, step_out, step_w):
    @pl.when(pl.program_id(0) == 0)
    def _():
        count = step_ref.shape[0]
        copies = (iota((LANES, count), 0) % REPEAT == iota((LANES, count), 1)).astype(f32).astype(bf16)
        step_w[...] = dot(copies, step_ref[...]).astype(bf16)

    normed = norm_rows(x_ref[...].astype(f32), gain_ref[...])
    normed_out[...] = normed
    value_out[...] = dot(normed, value_ref[...]).astype(bf16)
    state_out[...] = dot(normed, state_ref[...]).astype(bf16)
    step_out[...] = dot(normed, step_w[...], NT)


def project(residual, pre_gain, input_weight, state_weight, step_weight):
    tokens, width = residual.shape
    inner, state2 = input_weight.shape[1], state_weight.shape[1]
    tile = min(tokens, 256)
    return pl.pallas_call(
        project_kernel,
        grid=(tokens // tile,),
        in_specs=[
            rows(tile, width),
            whole((1, width)),
            whole(input_weight.shape),
            whole(state_weight.shape),
            whole(step_weight.shape),
        ],
        out_specs=[rows(tile, width), rows(tile, inner), rows(tile, state2), rows(tile, LANES)],
        out_shape=[
            pltpu.HBM((tokens, width), bf16),
            jax.ShapeDtypeStruct((tokens, inner), bf16),
            jax.ShapeDtypeStruct((tokens, state2), bf16),
            jax.ShapeDtypeStruct((tokens, LANES), f32),
        ],
        scratch_shapes=[pltpu.VMEM((LANES, width), bf16)],
        compiler_params=params(24),
        cost_estimate=cost(6),
    )(residual, pre_gain, input_weight, state_weight, step_weight)


def beside_kernel(normed_ref, gate_w, cot_ref, out_w, gate_out, grad_out):
    gate_out[...] = dot(normed_ref[...], gate_w[...])
    grad_out[...] = dot(cot_ref[...], out_w[...], NT)


def beside(normed, gate_weight, cotangent, out_weight):
    tokens, width = normed.shape
    inner = gate_weight.shape[1]
    tile = min(tokens, 256)
    return pl.pallas_call(
        beside_kernel,
        grid=(tokens // tile,),
        in_specs=[rows(tile, width), whole(gate_weight.shape), rows(tile, width), whole(out_weight.shape)],
        out_specs=[rows(tile, inner), rows(tile, inner)],
        out_shape=[jax.ShapeDtypeStruct((tokens, inner), f32), jax.ShapeDtypeStruct((tokens, inner), f32)],
        compiler_params=params(20),
        cost_estimate=cost(6),
    )(normed, gate_weight, cotangent, out_weight)


def convolve(before, here, kernel):
    extended = jnp.concatenate([before, here], axis=0)
    count = here.shape[0]
    first = EDGE - CONV + 1
    summed = kernel[0:1] * extended[first : first + count]
    for k in range(1, CONV):
        summed = summed + kernel[k : k + 1] * extended[first + k : first + k + count]
    return summed


def local_kernel(
    value_ref, state_ref, step_ref, halo_ref, gain_ref, value_w, state_w, value_k, state_k, bias_ref, log_ref,
    conv_out, pre_out, rows_out, spre_out, dt_out, cum_out, cumt_out, held_out, message_out, vhalo_out, shalo_out,
    value_before, state_before, held, total, heads,
):
    b = pl.program_id(0)
    width = value_ref.shape[1]

    @pl.when(b == 0)
    def _():
        normed = norm_rows(halo_ref[...].astype(f32), gain_ref[...])
        value_halo = dot(normed, value_w[...]).astype(bf16)
        state_halo = dot(normed, state_w[...]).astype(bf16)
        vhalo_out[...] = value_halo
        shalo_out[...] = state_halo
        value_before[...] = value_halo.astype(f32)[-EDGE:]
        state_before[...] = state_halo.astype(f32)[-EDGE:]
        held[...] = jnp.zeros(held.shape, f32)
        total[...] = jnp.zeros(total.shape, f32)
        heads[...] = head_map(width)

    dt = jax.nn.softplus(step_ref[...] + repeated(bias_ref[...]))
    decay = -dt * jnp.exp(repeated(log_ref[...]))
    size = value_ref.shape[0]
    lower = (iota((size, size), 0) >= iota((size, size), 1)).astype(f32).astype(bf16)
    cum = exact_dot(lower, decay, NN)
    dt_out[...] = dt
    cum_out[...] = cum
    cumt_out[...] = cum.T[: cumt_out.shape[0]]
    last = cum[size - 1 : size]
    wide = spread(jnp.concatenate([dt, cum], axis=0), heads[...])

    state = state_ref[...].astype(f32)
    spre = convolve(state_before[...], state, state_k[...].astype(f32))
    state_before[...] = state[-EDGE:]
    mixed_rows = spre * sig(spre)
    spre_out[...] = spre
    rows_out[...] = mixed_rows
    b_parts = both_parts(mixed_rows[:, :LANES].T)

    taps = value_k[...].astype(f32)
    held_out[0] = held[...]
    for span in spans(width):
        value = value_ref[:, span].astype(f32)
        pre = convolve(value_before[:, span], value, taps[:, span])
        value_before[:, span] = value[-EDGE:]
        conv = pre * sig(pre)
        pre_out[:, span] = pre
        conv_out[:, span] = conv
        cum_wide = wide[size:, span]
        end = cum_wide[size - 1 : size]
        weighted = conv * wide[:size, span] * jnp.exp(end - cum_wide)
        held[:, span] = jnp.exp(end) * held[:, span] + wide_dot(b_parts, weighted)
        total[:, span] = total[:, span] + end

    @pl.when(b == pl.num_programs(0) - 1)
    def _():
        message_out[:LANES] = held[...]
        message_out[LANES:] = total[...]


def local_states(value_in, state_in, step_raw, halo, pre_gain, input_weight, state_weight, input_kernel, state_kernel, step_bias, decay_log):
    tokens, inner = value_in.shape
    state2 = state_in.shape[1]
    state = state2 // 2
    blocks = tokens // BLOCK
    headrows = 16
    return pl.pallas_call(
        local_kernel,
        grid=(blocks,),
        in_specs=[
            rows(BLOCK, inner),
            rows(BLOCK, state2),
            rows(BLOCK, LANES),
            whole(halo.shape),
            whole(pre_gain.shape),
            whole(input_weight.shape),
            whole(state_weight.shape),
            whole(input_kernel.shape),
            whole(state_kernel.shape),
            whole(step_bias.shape),
            whole(decay_log.shape),
        ],
        out_specs=[
            rows(BLOCK, inner),
            rows(BLOCK, inner),
            rows(BLOCK, state2),
            rows(BLOCK, state2),
            rows(BLOCK, LANES),
            rows(BLOCK, LANES),
            pl.BlockSpec((headrows, BLOCK), lambda b: (0, b)),
            pl.BlockSpec((1, state, inner), lambda b: (b, 0, 0)),
            whole((state + EDGE, inner)),
            whole((halo.shape[0], inner)),
            whole((halo.shape[0], state2)),
        ],
        out_shape=[
            jax.ShapeDtypeStruct((tokens, inner), f32),
            pltpu.HBM((tokens, inner), f32),
            jax.ShapeDtypeStruct((tokens, state2), f32),
            jax.ShapeDtypeStruct((tokens, state2), f32),
            jax.ShapeDtypeStruct((tokens, LANES), f32),
            jax.ShapeDtypeStruct((tokens, LANES), f32),
            jax.ShapeDtypeStruct((headrows, tokens), f32),
            jax.ShapeDtypeStruct((blocks, state, inner), f32),
            jax.ShapeDtypeStruct((state + EDGE, inner), f32),
            jax.ShapeDtypeStruct((halo.shape[0], inner), bf16),
            jax.ShapeDtypeStruct((halo.shape[0], state2), bf16),
        ],
        scratch_shapes=[
            pltpu.VMEM((EDGE, inner), f32),
            pltpu.VMEM((EDGE, state2), f32),
            pltpu.VMEM((state, inner), f32),
            pltpu.VMEM((EDGE, inner), f32),
            pltpu.VMEM((LANES, inner), bf16),
        ],
        compiler_params=params(),
        cost_estimate=cost(10),
    )(value_in, state_in, step_raw, halo, pre_gain, input_weight, state_weight, input_kernel, state_kernel, step_bias, decay_log)


def inner_kernel(heads_count, conv_ref, dt_ref, rows_ref, cum_ref, cumt_ref, skip_ref, out_ref, heads):
    size, width = conv_ref.shape

    @pl.when(pl.program_id(0) == 0)
    def _():
        heads[...] = head_map(width)

    skip = jnp.broadcast_to(repeated(skip_ref[...]), (EDGE, LANES))
    wide = spread(jnp.concatenate([dt_ref[...], skip], axis=0), heads[...])
    scores = dot3(rows_ref[:, LANES:], rows_ref[:, :LANES], NT)
    causal = iota((size, size), 0) >= iota((size, size), 1)
    left = iota((size, LANES), 1) < HEAD_DIM
    cum = cum_ref[...]
    cumt = cumt_ref[...]
    for pair, span in enumerate(spans(width)):
        conv = conv_ref[:, span]
        mixes = []
        for h in (2 * pair, 2 * pair + 1):
            gap = cum[:, h : h + 1] - cumt[h : h + 1, :]
            mixes.append(both_parts(jnp.exp(jnp.where(causal, gap, -1e30)) * scores))
        both = wide_dot(jnp.concatenate(mixes, axis=0), conv * wide[:size, span])
        out_ref[:, span] = jnp.where(left, both[:size], both[size:]) + wide[size : size + 1, span] * conv


def inner_forward(heads_count, conv, dt, state_rows, cum, cumt, skip_gain):
    tokens, inner = conv.shape
    return pl.pallas_call(
        functools.partial(inner_kernel, heads_count),
        grid=(tokens // BLOCK,),
        in_specs=[
            rows(BLOCK, inner),
            rows(BLOCK, LANES),
            rows(BLOCK, state_rows.shape[1]),
            rows(BLOCK, LANES),
            pl.BlockSpec((cumt.shape[0], BLOCK), lambda b: (0, b)),
            whole(skip_gain.shape),
        ],
        out_specs=rows(BLOCK, inner),
        out_shape=jax.ShapeDtypeStruct((tokens, inner), f32),
        scratch_shapes=[pltpu.VMEM((LANES, inner), bf16)],
        compiler_params=params(12),
        cost_estimate=cost(6),
    )(conv, dt, state_rows, cum, cumt, skip_gain)


def combine_kernel(count, intra_ref, rows_ref, cum_ref, held_ref, own_ref, *refs):
    message_refs, (gate_ref, grad_ref, gain_ref, mixed_out, sums_out, held_out, end_out, start, total, heads) = refs[:count], refs[count:]
    b = pl.program_id(0)
    size, width = intra_ref.shape
    state = held_ref.shape[1]

    @pl.when(b == 0)
    def _():
        heads[...] = head_map(width)
        total[...] = jnp.zeros(total.shape, f32)
        for span in spans(width):
            entering = jnp.zeros((state, LANES), f32)
            passed = jnp.zeros((EDGE, LANES), f32)
            for ref in message_refs:
                entering = entering + jnp.exp(passed[0:1]) * ref[:state, span]
                passed = passed + ref[state:, span]
            start[:, span] = entering
            end_out[:, span] = own_ref[:state, span] + jnp.exp(own_ref[state : state + 1, span]) * entering

    cum_wide = spread(cum_ref[...], heads[...])
    c_parts = both_parts(rows_ref[:, LANES:])
    square = jnp.zeros((size, LANES), f32)
    inner = jnp.zeros((size, LANES), f32)
    for span in spans(width):
        held = held_ref[0, :, span] + jnp.exp(total[0:1, span]) * start[:, span]
        held_out[0, :, span] = held
        cum_part = cum_wide[:, span]
        total[:, span] = total[:, span] + cum_part[size - 1 : size]
        mixed = intra_ref[:, span] + jnp.exp(cum_part) * wide_dot(c_parts, held)
        mixed_out[:, span] = mixed
        gate = gate_ref[:, span]
        gated = mixed * (gate * sig(gate))
        square = square + gated * gated
        inner = inner + grad_ref[:, span] * gain_ref[:, span] * gated
    ones = jnp.ones((EDGE, LANES), bf16)
    square = exact_dot(ones, square, NT)
    inner = exact_dot(ones, inner, NT)
    sums_out[...] = jnp.where(iota(square.shape, 0) == 0, square, inner)


def combine(intra, state_rows, cum, held, own, messages, gate_in, grad_normed, norm_gain):
    tokens, inner = intra.shape
    blocks, state, _ = held.shape
    state_block = pl.BlockSpec((1, state, inner), lambda b: (b, 0, 0))
    return pl.pallas_call(
        functools.partial(combine_kernel, len(messages)),
        grid=(blocks,),
        in_specs=[
            rows(BLOCK, inner),
            rows(BLOCK, state_rows.shape[1]),
            rows(BLOCK, LANES),
            state_block,
            whole(own.shape),
            *[whole(own.shape) for _ in messages],
            rows(BLOCK, inner),
            rows(BLOCK, inner),
            whole(norm_gain.shape),
        ],
        out_specs=[
            rows(BLOCK, inner),
            pl.BlockSpec((EDGE, BLOCK), lambda b: (0, b)),
            state_block,
            whole((state, inner)),
        ],
        out_shape=[
            jax.ShapeDtypeStruct((tokens, inner), f32),
            jax.ShapeDtypeStruct((EDGE, tokens), f32),
            pltpu.HBM(held.shape, f32),
            jax.ShapeDtypeStruct((state, inner), f32),
        ],
        scratch_shapes=[pltpu.VMEM((state, inner), f32), pltpu.VMEM((EDGE, inner), f32), pltpu.VMEM((LANES, inner), bf16)],
        compiler_params=params(),
        cost_estimate=cost(5),
    )(intra, state_rows, cum, held, own, *messages, gate_in, grad_normed, norm_gain)


def column(row):
    return jnp.broadcast_to(row, (LANES, row.shape[1])).T


def gate_back_kernel(count, inner_total, mixed_ref, gate_ref, grad_ref, rows_ref, cum_ref, gain_ref, *refs):
    sums_refs, (normed_out, gate_out, dmix_out, later_out, message_out, gain_out, later, total, heads) = refs[:count], refs[count:]
    b = pl.program_id(0)
    size, width = mixed_ref.shape

    @pl.when(b == 0)
    def _():
        later[...] = jnp.zeros(later.shape, f32)
        total[...] = jnp.zeros(total.shape, f32)
        gain_out[...] = jnp.zeros(gain_out.shape, f32)
        heads[...] = head_map(width)

    sums = sums_refs[0][...]
    for ref in sums_refs[1:]:
        sums = sums + ref[...]
    rms_row = lax.rsqrt(sums[0:1] / inner_total + epsilon)
    pull_row = rms_row * rms_row * rms_row * sums[1:2] / inner_total
    rms = column(rms_row)
    pull = column(pull_row)
    cum_wide = spread(cum_ref[...], heads[...])
    c_parts = both_parts(rows_ref[:, LANES:].T)
    later_out[0] = later[...]
    for span in spans(width):
        gain = gain_ref[:, span]
        gate = gate_ref[:, span]
        mixed = mixed_ref[:, span]
        grad = grad_ref[:, span]
        gate_sig = sig(gate)
        gate_silu = gate * gate_sig
        gated = mixed * gate_silu
        normed_out[:, span] = (gated * rms * gain).astype(bf16)
        gain_out[:, span] = gain_out[:, span] + by_eights(grad * gated * rms)
        grad_gated = rms * gain * grad - gated * pull
        gate_out[:, span] = (grad_gated * mixed * gate_sig * (1.0 + gate * (1.0 - gate_sig))).astype(bf16)
        grad_mixed = grad_gated * gate_silu
        dmix_out[:, span] = grad_mixed
        cum_part = cum_wide[:, span]
        end = cum_part[size - 1 : size]
        later[:, span] = jnp.exp(end) * later[:, span] + wide_dot(c_parts, jnp.exp(cum_part) * grad_mixed)
        total[:, span] = total[:, span] + end

    @pl.when(b == pl.num_programs(0) - 1)
    def _():
        message_out[:LANES] = later[...]
        message_out[LANES:] = total[...]


def gate_back(mixed, gate_in, grad_normed, state_rows, cum, norm_gain, sums, inner_total):
    tokens, inner = mixed.shape
    blocks = tokens // BLOCK
    state = state_rows.shape[1] // 2
    return pl.pallas_call(
        functools.partial(gate_back_kernel, len(sums), inner_total),
        grid=(blocks,),
        in_specs=[
            rows(BLOCK, inner, blocks),
            rows(BLOCK, inner, blocks),
            rows(BLOCK, inner, blocks),
            rows(BLOCK, 2 * state, blocks),
            rows(BLOCK, LANES, blocks),
            whole(norm_gain.shape),
            *[pl.BlockSpec((EDGE, BLOCK), lambda b: (0, blocks - 1 - b)) for _ in sums],
        ],
        out_specs=[
            rows(BLOCK, inner, blocks),
            rows(BLOCK, inner, blocks),
            rows(BLOCK, inner, blocks),
            pl.BlockSpec((1, state, inner), lambda b: (blocks - 1 - b, 0, 0)),
            whole((state + EDGE, inner)),
            whole((EDGE, inner)),
        ],
        out_shape=[
            pltpu.HBM((tokens, inner), bf16),
            pltpu.HBM((tokens, inner), bf16),
            pltpu.HBM((tokens, inner), f32),
            pltpu.HBM((blocks, state, inner), f32),
            jax.ShapeDtypeStruct((state + EDGE, inner), f32),
            jax.ShapeDtypeStruct((EDGE, inner), f32),
        ],
        scratch_shapes=[pltpu.VMEM((state, inner), f32), pltpu.VMEM((EDGE, inner), f32), pltpu.VMEM((LANES, inner), bf16)],
        compiler_params=params(),
        cost_estimate=cost(7),
    )(mixed, gate_in, grad_normed, state_rows, cum, norm_gain, *sums)


def inner_back_kernel(b, conv_ref, dt_ref, rows_ref, cum_ref, cumt_ref, dmix_ref, driven_out, rows_out, heads):
    size, width = conv_ref.shape

    @pl.when(b == 0)
    def _():
        heads[...] = head_map(width)

    dt_wide = spread(dt_ref[...], heads[...])
    b_rows = rows_ref[:, :LANES]
    c_rows = rows_ref[:, LANES:]
    scores = dot3(b_rows, c_rows, NT)
    causal = iota((size, size), 1) >= iota((size, size), 0)
    left = iota((size, LANES), 1) < HEAD_DIM
    cum = cum_ref[...]
    cumt = cumt_ref[...]
    score_grad = jnp.zeros((size, size), f32)
    for pair, span in enumerate(spans(width)):
        dmix_high, dmix_low = split2(dmix_ref[:, span])
        across = jnp.concatenate([dmix_high, dmix_low], axis=1)
        right_side = jnp.concatenate([across, across], axis=0)
        taking = jnp.concatenate([dmix_high, dmix_high, dmix_low], axis=1)
        driven = conv_ref[:, span] * dt_wide[:, span]
        owns = []
        for mine in (left, jnp.logical_not(left)):
            own_high, own_low = split2(jnp.where(mine, driven, 0.0))
            owns.append(jnp.concatenate([own_high, own_low, own_high], axis=1))
        mix_grads = dot(jnp.concatenate(owns, axis=0), taking, NT)
        mixes = []
        for side in range(2):
            h = 2 * pair + side
            gap = cumt[h : h + 1, :] - cum[:, h : h + 1]
            kept = jnp.exp(jnp.where(causal, gap, -1e30))
            score_grad = score_grad + mix_grads[side * size : (side + 1) * size] * kept
            mixes.append(both_parts(kept * scores))
        both = fold(dot(jnp.concatenate(mixes, axis=0), right_side))
        driven_out[:, span] = jnp.where(left, both[:size], both[size:])
    rows_out[:, :LANES] = dot3(score_grad, c_rows, NN)
    rows_out[:, LANES:] = dot3(score_grad, b_rows, TN)


def inner_back(normed_out, out_weight, conv, dt, state_rows, cum, cumt, grad_mixed):
    tokens, inner = conv.shape
    width = out_weight.shape[1]
    tile = min(tokens, 256)
    first = tokens // tile
    at = lambda b: jnp.maximum(b - first, 0)
    by_rows = lambda cols: pl.BlockSpec((BLOCK, cols), lambda b: (at(b), 0))
    early = lambda cols: pl.BlockSpec((tile, cols), lambda b: (jnp.minimum(b, first - 1), 0))

    def body(normed_ref, weight_ref, *refs):
        ins, partial_out, rest = refs[:6], refs[6], refs[7:]
        b = pl.program_id(0)

        @pl.when(b < first)
        def _():
            partial_out[...] = dot(normed_ref[...], weight_ref[...])

        @pl.when(b >= first)
        def _():
            inner_back_kernel(b - first, *ins, *rest)

    return pl.pallas_call(
        body,
        grid=(first + tokens // BLOCK,),
        in_specs=[
            early(inner),
            whole(out_weight.shape),
            by_rows(inner),
            by_rows(LANES),
            by_rows(state_rows.shape[1]),
            by_rows(LANES),
            pl.BlockSpec((cumt.shape[0], BLOCK), lambda b: (0, at(b))),
            by_rows(inner),
        ],
        out_specs=[early(width), by_rows(inner), by_rows(state_rows.shape[1])],
        out_shape=[
            pltpu.HBM((tokens, width), f32),
            pltpu.HBM((tokens, inner), f32),
            pltpu.HBM(state_rows.shape, f32),
        ],
        scratch_shapes=[pltpu.VMEM((LANES, inner), bf16)],
        compiler_params=params(28),
        cost_estimate=cost(1),
    )(in_hbm(normed_out), in_hbm(out_weight), conv, *map(in_hbm, (dt, state_rows, cum, cumt, grad_mixed)))


def stacked(high, low):
    return jnp.concatenate([jnp.concatenate([high, high], axis=1), jnp.concatenate([low, low], axis=1)], axis=0)


def rows_back_kernel(
    count, drows_ref, dmix_ref, conv_ref, dt_ref, cum_ref, rows_ref, held_ref, later_ref, *refs
):
    message_refs = refs[:count]
    spre_ref, grad_rows_out, later_out, first_out, entering, total, heads = refs[count:]
    b = pl.program_id(0)
    size, width = conv_ref.shape
    state = held_ref.shape[1]

    @pl.when(b == 0)
    def _():
        heads[...] = head_map(width)
        for span in spans(width):
            coming = jnp.zeros((state, LANES), f32)
            passed = jnp.zeros((EDGE, LANES), f32)
            for ref in message_refs:
                coming = coming + jnp.exp(passed[0:1]) * ref[:state, span]
                passed = passed + ref[state:, span]
            entering[:, span] = coming
        total[...] = jnp.zeros(total.shape, f32)

    wide = spread(jnp.concatenate([cum_ref[...], dt_ref[...]], axis=0), heads[...])
    toward_b, toward_c, laters, helds = [], [], [], []
    for span in spans(width):
        cum_part = wide[:size, span]
        end = cum_part[size - 1 : size]
        later = later_ref[0, :, span] + jnp.exp(total[0:1, span]) * entering[:, span]
        later_out[0, :, span] = later
        total[:, span] = total[:, span] + end
        driven = conv_ref[:, span] * wide[size:, span]
        toward_b.append(both_parts(jnp.exp(end - cum_part) * driven))
        laters.append(stacked(*split2(later)))
        toward_c.append(both_parts(jnp.exp(cum_part) * dmix_ref[:, span]))
        helds.append(stacked(*split2(held_ref[0, :, span])))
    side = lambda parts: jnp.concatenate(parts, axis=1)
    grad_rows_out[:, :LANES] = drows_ref[:, :LANES] + fold(dot(side(toward_b), side(laters), NT))
    grad_rows_out[:, LANES:] = drows_ref[:, LANES:] + fold(dot(side(toward_c), side(helds), NT))

    @pl.when(b == pl.num_programs(0) - 1)
    def _():
        first_out[:, : 2 * LANES] = grad_rows_out[:EDGE]
        first_out[:, 2 * LANES :] = spre_ref[...]


def rows_back(grad_rows, grad_mixed, conv, dt, cum, state_rows, held, later, messages, spre):
    tokens, inner = conv.shape
    blocks, state, _ = held.shape
    state_block = pl.BlockSpec((1, state, inner), lambda b: (blocks - 1 - b, 0, 0))
    deep = rows(BLOCK, inner, blocks)
    deep_state = pl.BlockSpec((1, state, inner), lambda b: (blocks - 1 - b, 0, 0))
    narrow = rows(BLOCK, LANES, blocks)
    both = rows(BLOCK, 2 * state, blocks)
    return pl.pallas_call(
        functools.partial(rows_back_kernel, len(messages)),
        grid=(blocks,),
        in_specs=[
            both, deep, deep, narrow, narrow, both, deep_state, deep_state,
            *[whole(m.shape) for m in messages],
            pl.BlockSpec((EDGE, 2 * state), lambda b: (0, 0)),
        ],
        out_specs=[both, state_block, whole((EDGE, 4 * state))],
        out_shape=[
            jax.ShapeDtypeStruct((tokens, 2 * state), f32),
            pltpu.HBM(held.shape, f32),
            jax.ShapeDtypeStruct((EDGE, 4 * state), f32),
        ],
        scratch_shapes=[pltpu.VMEM((state, inner), f32), pltpu.VMEM((EDGE, inner), f32), pltpu.VMEM((LANES, inner), bf16)],
        compiler_params=params(24),
        cost_estimate=cost(0),
    )(*map(in_hbm, (grad_rows, grad_mixed, conv, dt, cum, state_rows, held, later, *messages, spre)))


def finish_kernel(
    blocks, driven_ref, dmix_ref, mixed_ref, pre_ref, value_ref, dt_ref, cum_ref, step_ref, rows_ref, held_ref, end_ref, later_ref,
    vhalo_ref, kernel_ref, skip_ref, bias_ref, log_ref,
    grad_value_out, grad_step_out, last_out, first_out, kernel_out, small_out,
    held_next, pre_next, skip_sum, heads, kernel_sum, heads_t, edge_rows,
):
    b = pl.program_id(0)
    size, width = mixed_ref.shape
    state = held_ref.shape[1]
    final = b == blocks - 1

    @pl.when(b == 0)
    def _():
        heads[...] = head_map(width)
        heads_t[...] = (iota((width, LANES), 1) == iota((width, LANES), 0) // HEAD_DIM).astype(f32).astype(bf16)
        held_next[...] = end_ref[...]
        pre_next[...] = jnp.zeros(pre_next.shape, f32)
        kernel_sum[...] = jnp.zeros(kernel_sum.shape, f32)
        small_out[...] = jnp.zeros(small_out.shape, f32)
        skip_sum[...] = jnp.zeros(skip_sum.shape, f32)

    dt = dt_ref[...]
    cum = cum_ref[...]
    skip_row = jnp.broadcast_to(repeated(skip_ref[...]), (EDGE, LANES))
    wide = spread(jnp.concatenate([cum, dt, skip_row], axis=0), heads[...])
    b_parts = both_parts(rows_ref[:, :LANES])
    taps = kernel_ref[...].astype(f32)
    levels, throughs, boundaries = [], [], []
    for span in spans(width):
        cum_part = wide[:size, span]
        dt_wide = wide[size : 2 * size, span]
        skip = wide[2 * size : 2 * size + 1, span]
        end = cum_part[size - 1 : size]
        later = later_ref[0, :, span]
        held = held_ref[0, :, span]
        tail = jnp.exp(end - cum_part)
        dmix = dmix_ref[:, span]
        pre = pre_ref[:, span]
        pre_sig = sig(pre)
        conv = pre * pre_sig
        driven = conv * dt_wide
        later_high, later_low = split2(later)
        across = jnp.concatenate([later_high, later_low], axis=1)
        ddriven = driven_ref[:, span] + tail * fold(dot(b_parts, jnp.concatenate([across, across], axis=0)))
        skip_sum[:, span] = skip_sum[:, span] + by_eights(dmix * conv)
        levels.append(both_parts(dmix * (mixed_ref[:, span] - skip * conv) - driven * ddriven))
        throughs.append(both_parts(ddriven * conv))
        boundaries.append(both_parts(by_eights(later * held_next[:, span])))
        held_next[:, span] = held

        dpre = (ddriven * dt_wide + skip * dmix) * (pre_sig * (1.0 + pre * (1.0 - pre_sig)))
        extended = jnp.concatenate([dpre, pre_next[:, span]], axis=0)
        pre_next[:, span] = dpre[:EDGE]
        value = value_ref[:, span].astype(f32)
        dvalue = jnp.zeros((size, LANES), f32)
        for k in range(CONV):
            shifted = extended[CONV - 1 - k : CONV - 1 - k + size]
            dvalue = dvalue + taps[k : k + 1, span] * shifted
            kernel_sum[k, :, span] = kernel_sum[k, :, span] + by_eights(value * shifted)
        grad_value_out[:, span] = dvalue.astype(bf16)
        edge_rows[:, span] = dvalue[-2 * EDGE :]

    side = lambda parts: jnp.concatenate(parts, axis=1)
    picks = jnp.concatenate([heads_t[span] for span in spans(width) for _ in range(2)], axis=0)
    reduced = dot(jnp.concatenate([side(levels), side(throughs), side(boundaries)], axis=0), picks)
    level, through, boundary = reduced[:size], reduced[size : 2 * size], reduced[2 * size :]
    boundary = jnp.sum(boundary, axis=0, keepdims=True)
    upper = (iota((size, size), 1) >= iota((size, size), 0)).astype(f32).astype(bf16)
    ddecay = exact_dot(upper, level, NN) + boundary
    rate = jnp.exp(repeated(log_ref[...]))
    dstep = (through - ddecay * rate) * sig(step_ref[...] + repeated(bias_ref[...]))
    grad_step_out[...] = dstep[:, : grad_step_out.shape[1]].astype(bf16)
    small_out[1:2] = small_out[1:2] + jnp.sum(dstep, axis=0, keepdims=True)
    small_out[2:3] = small_out[2:3] + jnp.sum(-ddecay * dt * rate, axis=0, keepdims=True)

    @pl.when(b == 0)
    def _():
        last_out[...] = edge_rows[...]

    @pl.when(final)
    def _():
        first = pre_next[...]
        first_out[...] = first
        ahead = jnp.concatenate([jnp.zeros((EDGE, width), f32), first], axis=0)
        halo = vhalo_ref[...].astype(f32)[-EDGE:]
        kernel_out[...] = jnp.zeros(kernel_out.shape, f32)
        for k in range(CONV):
            shifted = ahead[CONV - 1 - k : CONV - 1 - k + EDGE]
            kernel_out[k : k + 1] = jnp.sum(kernel_sum[k] + halo * shifted, axis=0, keepdims=True)
        high, middle, low = split3(skip_sum[...])
        summed = dot(high, heads[...], NT) + (dot(middle, heads[...], NT) + dot(low, heads[...], NT))
        small_out[0:1] = jnp.sum(summed, axis=0, keepdims=True)


def finish(plan, count, wide_operands, grad_driven, grad_mixed, mixed, pre, value_in, dt, cum, step_raw, state_rows, held, end_state, later,
           vhalo, input_kernel, skip_gain, step_bias, decay_log):
    tokens, inner = mixed.shape
    blocks, state, _ = held.shape
    head_count = skip_gain.shape[1]
    width = wide_operands[0].shape[1]
    tile = width // count
    at = lambda b: jnp.maximum(blocks - 1 - b, 0)
    by_rows = lambda cols: pl.BlockSpec((BLOCK, cols), lambda b, plan: (at(b), 0))
    state_block = pl.BlockSpec((1, state, inner), lambda b, plan: (at(b), 0, 0))
    moving = pl.BlockSpec((tokens, tile), lambda b, plan: (0, jnp.bitwise_xor(plan[1], jnp.maximum(b - blocks, 0))))
    still = pl.BlockSpec((tokens, tile), lambda b, plan: (0, plan[0]))
    wide, narrow = by_rows(inner), by_rows(LANES)
    operands = (grad_driven, grad_mixed, mixed, pre, value_in, dt, cum, step_raw, state_rows, held, end_state, later,
                vhalo, input_kernel, skip_gain, step_bias, decay_log)
    outs = [
        (wide, jax.ShapeDtypeStruct((tokens, inner), bf16)),
        (by_rows(head_count), jax.ShapeDtypeStruct((tokens, head_count), bf16)),
    ]
    for shape in ((2 * EDGE, inner), (EDGE, inner), (EDGE, inner), (EDGE, LANES), *[(2 * tile, tile)] * 4):
        outs.append((pl.BlockSpec(shape, lambda b, plan: (0, 0)), jax.ShapeDtypeStruct(shape, f32)))

    def body(plan_ref, *refs):
        b = pl.program_id(0)
        ins, wide_ins, rest = refs[:17], refs[17:25], refs[25:]

        @pl.when(b < blocks)
        def _():
            finish_kernel(blocks, *ins, *rest[:6], *rest[10:])

        @pl.when(b >= blocks)
        def _():
            wide_weights_kernel(b - blocks, *wide_ins, *rest[6:10])

    return scalar_call(
        body, plan, tuple(map(in_hbm, (*operands, *wide_operands))),
        [wide, wide, wide, wide, wide, narrow, narrow, narrow, by_rows(2 * state), state_block, all_of(end_state), state_block,
         *[all_of(a) for a in operands[12:]], moving, moving, still, still, still, still, moving, moving],
        [o[0] for o in outs], [o[1] for o in outs], grid=(blocks + count,),
        scratch=[
            pltpu.VMEM((state, inner), f32),
            pltpu.VMEM((EDGE, inner), f32),
            pltpu.VMEM((EDGE, inner), f32),
            pltpu.VMEM((LANES, inner), bf16),
            pltpu.VMEM((CONV, EDGE, inner), f32),
            pltpu.VMEM((inner, LANES), bf16),
            pltpu.VMEM((2 * EDGE, inner), f32),
        ],
        limit=44, micros=0,
    )


def from_before(value, axis, by=1):
    count = lax.axis_size(axis)
    return lax.ppermute(value, axis, [(i, i + by) for i in range(count - by)])


def from_after(value, axis, by=1):
    count = lax.axis_size(axis)
    return lax.ppermute(value, axis, [(i + by, i) for i in range(count - by)])


def from_all(value, axis):
    count = lax.axis_size(axis)
    return [lax.ppermute(value, axis, [(i, (i + by) % count) for i in range(count)]) for by in range(1, count)]


def after(first, then):
    return lax.optimization_barrier((first, then))[1]


def swapped(value, axis, flip):
    return lax.ppermute(value, axis, [(i, i ^ flip) for i in range(lax.axis_size(axis))])


def own_part(array, axis_name, dim):
    size = array.shape[dim] // lax.axis_size(axis_name)
    return lax.dynamic_slice_in_dim(array, lax.axis_index(axis_name) * size, size, dim)


def first_kernel(plan_ref, part_ref, out_ref):
    out_ref[...] = part_ref[0].astype(bf16)


def line_first(parts, axis):
    count, tokens, width = parts.shape
    plan = jnp.where(lax.axis_index(axis) == 0, count - 1, 0).astype(jnp.int32).reshape(1)
    tile = min(tokens, 512)
    sent = pl.pallas_call(
        first_kernel,
        grid_spec=pltpu.PrefetchScalarGridSpec(
            num_scalar_prefetch=1,
            grid=(tokens // tile,),
            in_specs=[pl.BlockSpec((1, tile, width), lambda b, plan: (plan[0], b, 0))],
            out_specs=pl.BlockSpec((tile, width), lambda b, plan: (b, 0)),
        ),
        out_shape=jax.ShapeDtypeStruct((tokens, width), bf16),
        compiler_params=params(8),
        cost_estimate=cost(0),
    )(plan, in_hbm(parts))
    return sent


def line_step(parts, step, arrived, axis):
    count, tokens, width = parts.shape
    place = lax.axis_index(axis)
    plan = jnp.clip(jnp.stack([count - step + place, step - count + place]), 0, count - 1).astype(jnp.int32)
    if step == 2:
        arrived = [arrived, arrived]

    def body(plan_ref, up_ref, down_ref, up_in, down_in, up_out, down_out):
        up, down = up_in[...].astype(f32), down_in[...].astype(f32)
        if step == 2:
            up = jnp.where(plan_ref[2] == 1, up, 0.0)
            down = jnp.where(plan_ref[2] == count - 2, down, 0.0)
        up_out[...] = (up_ref[0] + up).astype(bf16)
        down_out[...] = (down_ref[0] + down).astype(bf16)

    tile = min(tokens, 512)
    block = pl.BlockSpec((tile, width), lambda b, plan: (b, 0))
    up, down = pl.pallas_call(
        body,
        grid_spec=pltpu.PrefetchScalarGridSpec(
            num_scalar_prefetch=1,
            grid=(tokens // tile,),
            in_specs=[
                pl.BlockSpec((1, tile, width), lambda b, plan: (plan[0], b, 0)),
                pl.BlockSpec((1, tile, width), lambda b, plan: (plan[1], b, 0)),
                block,
                block,
            ],
            out_specs=[block, block],
        ),
        out_shape=[jax.ShapeDtypeStruct((tokens, width), bf16)] * 2,
        compiler_params=params(12),
        cost_estimate=cost(0),
    )(jnp.concatenate([plan, place.astype(jnp.int32).reshape(1)]), in_hbm(parts), in_hbm(parts), *arrived)
    return (up, down), [
        lax.ppermute(up, axis, [(k, k + 1) for k in range(step)]),
        lax.ppermute(down, axis, [(count - 1 - k, count - 2 - k) for k in range(step)]),
    ]


def input_kernel_body(
    pieces, plan_ref, gate_ref, value_ref, narrow_ref, x_ref, gain_ref, gate_w, value_w, state_w, step_w, part_out, row_out, col_out, narrow_w
):
    b = pl.program_id(0)
    size = value_ref.shape[0]

    @pl.when(b == 0)
    def _():
        col_out[...] = jnp.zeros(col_out.shape, f32)
        state2, steps = state_w.shape[1], step_w.shape[0]
        mine = take_columns(plan_ref[0], pieces, state2)
        beside = (iota((steps, LANES), 0) + state2 // pieces == iota((steps, LANES), 1)).astype(f32).astype(bf16)
        narrow_w[...] = (dot(state_w[...], mine) + dot(step_w[...], beside, TN)).astype(bf16)

    gate = gate_ref[...]
    value = value_ref[...]
    narrow = narrow_ref[...]
    x = x_ref[...].astype(f32)
    scaling = lax.rsqrt(jnp.mean(x * x, axis=-1, keepdims=True) + epsilon)
    part = x.shape[1] // pieces
    row = jnp.zeros((size, LANES), f32)
    for j in range(pieces):
        span = slice(j * part, (j + 1) * part)
        partial = dot(gate, gate_w[span, :], NT) + dot(value, value_w[span, :], NT) + dot(narrow, narrow_w[span, :], NT)
        part_out[j] = partial
        pulled = partial * x[:, span]
        gained = pulled * gain_ref[:, span]
        for inside in spans(part):
            row = row + gained[:, inside]
        col_out[:, span] = col_out[:, span] + by_eights(pulled * scaling)
    row_out[...] = exact_dot(jnp.ones((EDGE, LANES), bf16), row, NT)


def scalar_call(body, plan, operands, in_specs, out_specs, out_shape, grid=(1,), scratch=(), limit=16, micros=2):
    return pl.pallas_call(
        body,
        grid_spec=pltpu.PrefetchScalarGridSpec(
            num_scalar_prefetch=1, grid=grid, in_specs=in_specs, out_specs=out_specs, scratch_shapes=list(scratch)
        ),
        out_shape=out_shape,
        compiler_params=pltpu.CompilerParams(dimension_semantics=("arbitrary",) * len(grid), vmem_limit_bytes=limit * 1024 * 1024),
        cost_estimate=cost(micros),
    )(plan, *operands)


def all_of(a):
    return pl.BlockSpec(a.shape, lambda *_: (0,) * len(a.shape))


def take_columns(at, count, width):
    part = width // count
    lane = iota((width, LANES), 1)
    return ((iota((width, LANES), 0) == lane + at * part) & (lane < part)).astype(f32).astype(bf16)


def extended_rows(x, beyond):
    return jnp.concatenate([x, beyond, jnp.zeros((EDGE, x.shape[1]), f32)], axis=0)


def pieces_kernel(count, plan_ref, rows_ref, ahead_ref, *outs):
    tokens, state2 = rows_ref.shape
    extended = extended_rows(rows_ref[...], ahead_ref[:, :state2])
    size = extended.shape[0] // 2
    picks = [take_columns(lax.rem(plan_ref[0] + k, count), count, state2) for k in range(count)]
    none = jnp.zeros((state2, LANES // 2), bf16)
    half = LANES // 2
    upper = jnp.concatenate([jnp.concatenate([p[:, :half], none], axis=1) for p in picks], axis=1)
    lower = jnp.concatenate([jnp.concatenate([none, p[:, :half]], axis=1) for p in picks], axis=1)
    both = dot_exact(extended[:size], upper) + dot_exact(extended[size:], lower)
    for k, out in enumerate(outs):
        out[...] = both[:, k * LANES : (k + 1) * LANES]


def dot_exact(x, ones):
    high, middle, low = split3(x)
    return dot(high, ones) + (dot(middle, ones) + dot(low, ones))


def pieces_of(place, count, grad_rows, ahead):
    tokens, state2 = grad_rows.shape
    shape = jax.ShapeDtypeStruct((tokens // 2 + EDGE, LANES), f32)
    return scalar_call(
        functools.partial(pieces_kernel, count), place, (grad_rows, ahead), [all_of(grad_rows), all_of(ahead)],
        [all_of(shape)] * count, [shape] * count, limit=12, micros=0,
    )


def complete_kernel(ahead_ref, last_ref, taps_ref, value_ref, out_ref):
    fixed = last_ref[...]
    taps = taps_ref[...].astype(f32)
    extended = jnp.concatenate([jnp.zeros(last_ref.shape, f32), ahead_ref[...]], axis=0)
    for k in range(CONV):
        fixed = fixed + taps[k : k + 1] * extended[CONV - 1 - k : CONV - 1 - k + last_ref.shape[0]]
    out_ref[...] = fixed.astype(bf16)


def complete(ahead, last_rows, taps, grad_value):
    tokens, inner = grad_value.shape
    size = last_rows.shape[0]
    final_rows = pl.BlockSpec((size, inner), lambda b: (tokens // size - 1, 0))
    return pl.pallas_call(
        complete_kernel,
        grid=(1,),
        in_specs=[whole(ahead.shape), whole(last_rows.shape), whole(taps.shape), final_rows],
        out_specs=final_rows,
        out_shape=jax.ShapeDtypeStruct(grad_value.shape, bf16),
        input_output_aliases={3: 0},
        compiler_params=params(4),
        cost_estimate=cost(0),
    )(ahead, last_rows, taps, grad_value)


def three_parts(x):
    return jnp.concatenate(split3(x), axis=0)


def three_sum(parts):
    size = parts.shape[0] // 3
    parts = parts.astype(f32)
    return parts[:size] + (parts[size : 2 * size] + parts[2 * size :])


PACK = 16
SMALL = 48


def state_kernel_body(count, plan_ref, *refs):
    grads = refs[:count]
    spre_ref, input_ref, halo_ref, ahead_ref, taps_ref, step_ref, out_ref, taps_out = refs[count:]
    tokens, state2 = spre_ref.shape
    part = state2 // count
    pick = take_columns(plan_ref[0], count, state2)
    total = grads[0][...]
    for ref in grads[1:]:
        total = total + ref[...]
    total = jnp.concatenate([total, pltpu.roll(total, LANES // 2, 1)], axis=0)
    total = jnp.where(iota(total.shape, 1) < part, total, 0.0)
    pre = dot_exact(extended_rows(spre_ref[...], ahead_ref[:, state2:]), pick)
    s = sig(pre)
    through = total * (s * (1.0 + pre * (1.0 - s)))
    taps = dot(taps_ref[...], pick)
    inputs = dot(jnp.concatenate([halo_ref[...], input_ref[...]], axis=0), pick)
    steps = step_ref.shape[1]
    place = (iota((steps, LANES), 0) + part == iota((steps, LANES), 1)).astype(f32).astype(bf16)
    grad = dot(step_ref[...], place)
    own = through[:tokens]
    first = halo_ref.shape[0] - CONV + 1
    taps_out[...] = jnp.zeros(taps_out.shape, f32)
    for k in range(CONV):
        grad = grad + taps[k : k + 1] * through[CONV - 1 - k : CONV - 1 - k + tokens]
        taps_out[k : k + 1] = jnp.sum(own * inputs[first + k : first + k + tokens], axis=0, keepdims=True)
    out_ref[...] = grad.astype(bf16)


def state_back(place, grads, spre, state_in, halo, ahead, taps, grad_step):
    count = len(grads)
    tokens = spre.shape[0]
    shapes = [jax.ShapeDtypeStruct((tokens, LANES), bf16), jax.ShapeDtypeStruct((EDGE, LANES), f32)]
    operands = (*grads, spre, state_in, halo, ahead, taps, grad_step)
    return scalar_call(
        functools.partial(state_kernel_body, count), place, operands, [all_of(a) for a in operands],
        [all_of(a) for a in shapes], shapes, limit=16, micros=0,
    )


def sums_kernel(count, plan_ref, row_ref, col_ref, taps_ref, out_ref):
    state2 = out_ref.shape[1]
    tokens, width = row_ref.shape[1], col_ref.shape[1]
    packed = [row_ref[:1, i : i + state2] for i in range(0, tokens, state2)]
    col = jnp.sum(col_ref[...], axis=0, keepdims=True)
    packed += [col[:, i : i + state2] for i in range(0, width, state2)]
    high, middle, low = split3(taps_ref[:CONV])
    pick = take_columns(plan_ref[0], count, state2)
    packed.append(dot(high, pick, NT) + (dot(middle, pick, NT) + dot(low, pick, NT)))
    packed = jnp.concatenate(packed, axis=0)
    out_ref[...] = jnp.concatenate([packed, jnp.zeros((PACK - packed.shape[0], state2), f32)], axis=0)


def sums_of(place, count, row_sums, col_sums, taps_grad, state2):
    shape = jax.ShapeDtypeStruct((PACK, state2), f32)
    operands = (row_sums, col_sums, taps_grad)
    return scalar_call(
        functools.partial(sums_kernel, count), place, operands, [all_of(a) for a in operands], all_of(shape), shape,
        limit=8, micros=0,
    )


def small_kernel(count, given, tokens, plan_ref, *refs):
    parts, (kernel_ref, gain_ref, small_ref, sums_out, out_ref) = refs[:given], refs[given:]
    sums = parts[0][...]
    for ref in parts[1:]:
        sums = sums + ref[...]
    sums_out[...] = sums
    state2 = sums.shape[1]
    wide = state2 // LANES
    inner = kernel_ref.shape[1]
    rows_of = [kernel_ref[k : k + 1, span] for k in range(CONV) for span in spans(inner)]
    gain = jnp.sum(gain_ref[...], axis=0, keepdims=True)
    rows_of += [gain[:, span] for span in spans(inner)]
    rows_of += [small_ref[i : i + 1] for i in range(3)]
    first = tokens // state2
    last = PACK - 2 - CONV
    cols = [sums[r : r + 1, i * LANES : (i + 1) * LANES] for r in range(first, last) for i in range(wide)]
    quarter = len(cols) // count
    for i in range(quarter):
        chosen = jnp.zeros((1, LANES), f32)
        for q in range(count):
            chosen = jnp.where(plan_ref[0] == q, cols[q * quarter + i], chosen)
        rows_of.append(chosen)
    rows_of += [sums[last + k : last + k + 1, i * LANES : (i + 1) * LANES] for k in range(CONV) for i in range(wide)]
    rows_of.append(jnp.zeros((SMALL - len(rows_of), LANES), f32))
    out_ref[...] = jnp.concatenate(rows_of, axis=0)


def small_sums(place, count, tokens, parts, kernel_grad, gain_grad, small):
    shapes = [jax.ShapeDtypeStruct(parts[0].shape, f32), jax.ShapeDtypeStruct((SMALL, LANES), f32)]
    operands = tuple(map(in_hbm, (*parts, kernel_grad, gain_grad, small)))
    return scalar_call(
        functools.partial(small_kernel, count, len(parts), tokens), place, operands, [all_of(a) for a in operands],
        [all_of(a) for a in shapes], shapes, limit=8, micros=0,
    )


def wide_weights_kernel(k, normed_a, normed_b, gate_a, gate_b, out_a, out_b, cot_a, cot_b, *outs):
    tile = normed_a.shape[1]
    gate_keep, gate_send, out_keep, out_send = outs
    gate = dot(normed_a[...], gate_a[...], TN) + dot(normed_b[...], gate_b[...], TN)
    out = dot(out_a[...], cot_a[...], TN) + dot(out_b[...], cot_b[...], TN)
    targets = ((gate_keep, 0, out_keep, 0), (gate_send, 0, out_keep, 1), (gate_keep, 1, out_send, 0), (gate_send, 1, out_send, 1))
    for i, (gate_ref, gate_at, out_ref, out_at) in enumerate(targets):

        @pl.when(k == i)
        def _(gate_ref=gate_ref, gate_at=gate_at, out_ref=out_ref, out_at=out_at):
            gate_ref[gate_at * tile : (gate_at + 1) * tile] = gate
            out_ref[out_at * tile : (out_at + 1) * tile] = out


def value_weights_kernel(k, normed_a, normed_b, value_a, value_b, first_keep, first_send, second_keep, second_send):
    total = dot(normed_a[...], value_a[...], TN) + dot(normed_b[...], value_b[...], TN)
    half = total.shape[0] // 2
    targets = ((first_keep, 0, second_keep, 0), (first_send, 0, second_keep, 1), (first_keep, 1, second_send, 0), (first_send, 1, second_send, 1))
    for i, (first_ref, first_at, second_ref, second_at) in enumerate(targets):

        @pl.when(k == i)
        def _(first_ref=first_ref, first_at=first_at, second_ref=second_ref, second_at=second_at):
            first_ref[first_at * half : (first_at + 1) * half] = total[:half]
            second_ref[second_at * half : (second_at + 1) * half] = total[half:]


def input_partials(place, pieces, grad_gate, grad_value, narrow, residual, pre_gain, gate_weight, input_weight, state_weight, step_weight):
    tokens, width = residual.shape
    inner = grad_gate.shape[1]
    tile = min(tokens, 256)
    by_rows = lambda cols: pl.BlockSpec((tile, cols), lambda b, plan: (b, 0))
    return scalar_call(
        functools.partial(input_kernel_body, pieces), place,
        (in_hbm(grad_gate), grad_value, narrow, in_hbm(residual), pre_gain, gate_weight, input_weight, state_weight, step_weight),
        [
            by_rows(inner), by_rows(inner), by_rows(narrow.shape[1]), by_rows(width),
            *[all_of(a) for a in (pre_gain, gate_weight, input_weight, state_weight, step_weight)],
        ],
        [
            pl.BlockSpec((pieces, tile, width // pieces), lambda b, plan: (0, b, 0)),
            pl.BlockSpec((EDGE, tile), lambda b, plan: (0, b)),
            pl.BlockSpec((EDGE, width), lambda b, plan: (0, 0)),
        ],
        [
            pltpu.HBM((pieces, tokens, width // pieces), f32),
            jax.ShapeDtypeStruct((EDGE, tokens), f32),
            jax.ShapeDtypeStruct((EDGE, width), f32),
        ],
        grid=(tokens // tile,), scratch=[pltpu.VMEM((width, LANES), bf16)], limit=36, micros=0,
    )


def value_weights(plan, count, normed, grad_value):
    tokens, width = normed[0].shape
    tile = width // count
    half = grad_value[0].shape[1] // 2
    moving = pl.BlockSpec((tokens, tile), lambda k, plan: (0, jnp.bitwise_xor(plan[1], k)))
    still = pl.BlockSpec((tokens, half), lambda k, plan: (0, plan[0]))
    shape = jax.ShapeDtypeStruct((tile, half), f32)

    def body(plan_ref, *refs):
        value_weights_kernel(pl.program_id(0), *refs)

    return scalar_call(
        body, plan, (*map(in_hbm, normed), *grad_value), [moving, moving, still, still],
        [all_of(shape)] * 4, [shape] * 4, grid=(count,), limit=20, micros=0,
    )


def narrow_weights_kernel(plan_ref, normed_a, normed_b, narrow_a, narrow_b, small_a, small_b, keep_out, send_out):
    k = pl.program_id(0)
    tile = normed_a.shape[1]
    total = dot(narrow_a[...], normed_a[...], TN) + dot(narrow_b[...], normed_b[...], TN)
    small = small_a[...] + small_b[...]
    per_row = tile // LANES
    size = keep_out.shape[0] // 2
    for i, (ref, at) in enumerate(((keep_out, 0), (send_out, 0), (keep_out, size), (send_out, size))):

        @pl.when(k == i)
        def _(ref=ref, at=at):
            ref[at : at + LANES] = total
            for j in range(per_row):
                ref[at + LANES : at + size, j * LANES : (j + 1) * LANES] = small[j * SMALL // per_row : (j + 1) * SMALL // per_row]


def narrow_weights(plan, count, normed, narrow, small):
    tokens, width = normed[0].shape
    tile = width // count
    moving = pl.BlockSpec((tokens, tile), lambda k, plan: (0, jnp.bitwise_xor(plan[1], k)))
    shape = jax.ShapeDtypeStruct((2 * (LANES + SMALL * LANES // tile), tile), f32)
    return scalar_call(
        narrow_weights_kernel, plan, (*map(in_hbm, normed), *narrow, *small), [moving, moving, *[all_of(a) for a in (*narrow, *small)]],
        [all_of(shape)] * 2, [shape] * 2, grid=(count,), limit=16, micros=0,
    )


def pair_kernel(keep_ref, got_ref, stay_out, away_out):
    size = stay_out.shape[0]
    stay_out[...] = keep_ref[:size] + got_ref[:size]
    away_out[...] = keep_ref[size:] + got_ref[size:]


def pair_sums(keep, got):
    shape = jax.ShapeDtypeStruct((keep.shape[0] // 2, keep.shape[1]), f32)
    return pl.pallas_call(
        pair_kernel,
        out_shape=[shape, shape],
        compiler_params=pltpu.CompilerParams(vmem_limit_bytes=6 * 1024 * 1024),
        cost_estimate=cost(0),
    )(keep, got)


def over_dp(total):
    step = 2
    while step < lax.axis_size("dp"):
        total = total + swapped(total, "dp", step)
        step *= 2
    return total


def halves_kernel(own_a, own_b, got_a, got_b, stay_out, away_a, away_b):
    half = away_a.shape[0]
    stay_out[:half] = own_a[:half] + got_a[:half]
    stay_out[half:] = own_b[:half] + got_b[:half]
    away_a[...] = own_a[half:] + got_a[half:]
    away_b[...] = own_b[half:] + got_b[half:]


def halves(own_a, own_b, got_a, got_b):
    size, cols = own_a.shape
    half = jax.ShapeDtypeStruct((size // 2, cols), f32)
    return pl.pallas_call(
        halves_kernel,
        out_shape=[pltpu.HBM((size, cols), f32), *[pltpu.HBM(half.shape, f32)] * 2],
        compiler_params=pltpu.CompilerParams(vmem_limit_bytes=16 * 1024 * 1024),
        cost_estimate=cost(0),
    )(*map(in_hbm, (own_a, own_b, got_a, got_b)))


def add_kernel(stay, got_a, got_b, out):
    half = got_a.shape[0]
    out[:half] = (stay[:half] + got_a[...]).astype(out.dtype)
    out[half:] = (stay[half:] + got_b[...]).astype(out.dtype)


def add_halves(stay, got_a, got_b, dtype):
    return pl.pallas_call(
        add_kernel,
        out_shape=jax.ShapeDtypeStruct(stay.shape, dtype),
        compiler_params=pltpu.CompilerParams(vmem_limit_bytes=16 * 1024 * 1024),
        cost_estimate=cost(0),
    )(stay, got_a, got_b)


def summed(stay, got_a, got_b):
    if lax.axis_size("dp") == 2:
        return add_halves(stay, got_a, got_b, bf16)
    return over_dp(add_halves(stay, got_a, got_b, f32)).astype(bf16)


def ordered(first, here, there):
    here, there = here.astype(f32), there.astype(f32)
    return jnp.where(first, here, there), jnp.where(first, there, here)


def joined_kernel(*refs):
    *parts, out, done = refs
    rows = parts[0].shape[0]
    copies = [
        pltpu.make_async_copy(part, out.at[pl.ds(i * rows, rows)], done.at[i]) for i, part in enumerate(parts)
    ]
    for copy in copies:
        copy.start()
    for copy in copies:
        copy.wait()


def joined(*parts):
    rows, width = parts[0].shape
    return pl.pallas_call(
        joined_kernel,
        out_shape=pltpu.HBM((len(parts) * rows, width), parts[0].dtype),
        in_specs=[pl.BlockSpec(memory_space=pl.ANY)] * len(parts),
        out_specs=pl.BlockSpec(memory_space=pl.ANY),
        scratch_shapes=[pltpu.SemaphoreType.DMA((len(parts),))],
        compiler_params=pltpu.CompilerParams(vmem_limit_bytes=2**20),
    )(*parts)


def wide_together_kernel(plan_ref, here, there, gate_out, out_out):
    tile = gate_out.shape[0]
    k = pl.program_id(0)
    first = plan_ref[0] == 0
    half = gate_out.shape[1] // 2
    span = pl.ds(pl.multiple_of(k * 2 * tile, 2 * EDGE), tile)
    gate_out[:, :half], gate_out[:, half:] = ordered(first, here[span], there[span])
    span = pl.ds(pl.multiple_of(k * 2 * tile + tile, 2 * EDGE), tile)
    out_out[:tile], out_out[tile:] = ordered(first, here[span], there[span])


def wide_together(plan, count, here, there):
    tile = here.shape[0] // (2 * count)
    width, inner = tile * count, 2 * here.shape[1]
    return scalar_call(
        wide_together_kernel, plan, (here, there), [all_of(here), all_of(there)],
        [pl.BlockSpec((tile, inner), lambda q, plan: (q, 0)), pl.BlockSpec((inner, tile), lambda q, plan: (0, q))],
        [jax.ShapeDtypeStruct((width, inner), f32), jax.ShapeDtypeStruct((inner, width), f32)],
        grid=(count,), limit=24, micros=0,
    )


def narrow_together_kernel(plan_ref, here, there, input_out, state_out, step_out):
    tile = input_out.shape[0]
    k = jnp.bitwise_xor(pl.program_id(0), plan_ref[1])
    half = input_out.shape[1] // 2
    start = pl.multiple_of(k * (tile + LANES), 2 * EDGE)
    span = pl.ds(start, tile)
    input_out[:, :half], input_out[:, half:] = ordered(plan_ref[0] == 0, here[span], there[span])
    rest = here[pl.ds(pl.multiple_of(start + tile, 2 * EDGE), LANES)].astype(f32)
    states = state_out.shape[0]
    state_out[...] = rest[:states]
    step_out[...] = rest[states : states + step_out.shape[0]]


def narrow_together(plan, count, here, there, state_part, steps):
    tile = here.shape[0] // count - LANES
    width, inner = tile * count, 2 * here.shape[1]
    by_lane = lambda size: pl.BlockSpec((size, tile), lambda q, plan: (0, q))
    return scalar_call(
        narrow_together_kernel, plan, (here, there), [all_of(here), all_of(there)],
        [pl.BlockSpec((tile, inner), lambda q, plan: (q, 0)), by_lane(state_part), by_lane(steps)],
        [
            jax.ShapeDtypeStruct((width, inner), f32),
            jax.ShapeDtypeStruct((state_part, width), f32),
            jax.ShapeDtypeStruct((steps, width), f32),
        ],
        grid=(count,), limit=20, micros=0,
    )


def final_kernel(count, plan_ref, part_ref, up_ref, down_ref, x_ref, mine_ref, cot_ref, gain_ref, sums_ref, out_ref):
    b = pl.program_id(0)
    size, part = up_ref.shape
    x = x_ref[...].astype(f32)
    width = x.shape[1]
    scaling = lax.rsqrt(jnp.mean(x * x, axis=-1, keepdims=True) + epsilon)
    row = jnp.zeros((1, size), f32)
    for q in range(count):
        row = jnp.where(b == q, sums_ref[q : q + 1], row)
    pull = column(row) * ((scaling * scaling * scaling) / width)
    for span in spans(part):
        normed_grad = part_ref[0, :, span] + up_ref[:, span].astype(f32) + down_ref[:, span].astype(f32)
        out_ref[:, span] = (
            cot_ref[:, span].astype(f32) + scaling * gain_ref[:, span] * normed_grad - mine_ref[:, span].astype(f32) * pull
        )


def final(place, parts, arrived, residual, cotangent, pre_gain, sums):
    count, tokens, part = parts.shape
    size = sums.shape[1]
    mine = pl.BlockSpec((size, part), lambda b, plan: (b, plan[0]))
    own = pl.BlockSpec((size, part), lambda b, plan: (b, 0))
    return scalar_call(
        functools.partial(final_kernel, tokens // size), place,
        (in_hbm(parts), *arrived, in_hbm(residual), in_hbm(residual), in_hbm(cotangent), pre_gain, sums),
        [
            pl.BlockSpec((1, size, part), lambda b, plan: (plan[0], b, 0)),
            own,
            own,
            pl.BlockSpec((size, residual.shape[1]), lambda b, plan: (b, 0)),
            mine,
            mine,
            pl.BlockSpec((1, part), lambda b, plan: (0, plan[0])),
            all_of(sums),
        ],
        own,
        jax.ShapeDtypeStruct((tokens, part), f32),
        grid=(tokens // size,), limit=16, micros=0,
    )


def per_device(residual, pre_gain, gate_weight, input_weight, state_weight, step_weight, input_kernel, state_kernel,
               step_bias, decay_log, skip_gain, norm_gain, out_weight, cotangent):
    residual, cotangent = residual[0], cotangent[0]
    tokens, width = residual.shape
    tensor_size = lax.axis_size("tensor")
    ctx_size = lax.axis_size("ctx")
    inner = gate_weight.shape[1]
    inner_total = inner * tensor_size
    head_count = step_weight.shape[1]
    state2 = state_weight.shape[1]
    state_part = state2 // tensor_size
    row = lambda v: v.reshape(1, -1)
    plan = jnp.stack([lax.axis_index("dp") % 2, lax.axis_index("ctx"), lax.axis_index("tensor")]).astype(jnp.int32)
    place = lax.axis_index("tensor").astype(jnp.int32).reshape(1)

    halo = from_before(residual[-2 * EDGE :], "ctx")
    other_cotangent = swapped(cotangent, "dp", 1)
    step_weight = step_weight.T
    normed, value_in, state_in, step_raw = project(residual, row(pre_gain), input_weight, state_weight, step_weight)
    other_normed = swapped(normed, "dp", 1)
    conv, pre, state_rows, spre, dt, cum, cumt, held, message, vhalo, shalo = local_states(
        value_in, state_in, step_raw, halo, row(pre_gain), input_weight, state_weight, input_kernel, state_kernel,
        row(step_bias), row(decay_log)
    )
    messages = [from_before(message, "ctx", by) for by in range(1, ctx_size)]
    gate_in, grad_normed = beside(after(message, normed), gate_weight, cotangent, out_weight)
    intra = inner_forward(head_count, conv, dt, state_rows, cum, cumt, row(skip_gain))
    messages = after((gate_in, intra, other_cotangent), messages)
    mixed, sums, held, end_state = combine(
        intra, state_rows, cum, held, message, messages, gate_in, grad_normed, row(norm_gain)
    )
    all_sums = [sums, *after(other_normed, from_all(sums, "tensor"))]
    normed_out, grad_gate, grad_mixed, later, message, gain_grad = gate_back(
        mixed, gate_in, grad_normed, state_rows, cum, row(norm_gain), all_sums, inner_total
    )
    messages = [from_after(message, "ctx", by) for by in range(1, ctx_size)]

    partial_out, grad_driven, grad_rows = inner_back(
        normed_out, out_weight, conv, dt, state_rows, cum, cumt, after(message, grad_mixed)
    )
    messages = after(grad_driven, messages)
    partial_out, gate_there, out_there = after(messages, (partial_out, grad_gate, normed_out))
    resid_part = own_part(residual, "tensor", 1).astype(f32)
    branch = lax.psum_scatter(partial_out, "tensor", scatter_dimension=1, tiled=True)
    other_gate = swapped(gate_there, "dp", 1)
    other_out = swapped(out_there, "dp", 1)
    grad_rows, later, first_rows = rows_back(grad_rows, grad_mixed, conv, dt, cum, state_rows, held, later, messages, spre)
    ahead = from_after(first_rows, "ctx")
    pieces = list(pieces_of(place, tensor_size, grad_rows, ahead))
    arrived = [
        lax.ppermute(pieces[k], "tensor", [(i, (i + k) % tensor_size) for i in range(tensor_size)]) for k in range(1, tensor_size)
    ]
    (grad_value, grad_step, last_rows, first_rows, kernel_grad, small, gate_keep, gate_send, out_keep, out_send) = finish(
        plan, ctx_size, (normed, other_normed, grad_gate, other_gate, normed_out, other_out, cotangent, other_cotangent),
        grad_driven, after(pieces[0], grad_mixed), mixed, pre, value_in, dt, cum, step_raw, state_rows, held, end_state, later,
        vhalo, input_kernel, row(skip_gain), row(step_bias), row(decay_log)
    )
    ahead_value = from_after(first_rows, "ctx")
    arrived = after(first_rows, arrived)
    narrow, taps_grad = state_back(place, [pieces[0], *arrived], spre, state_in, shalo, ahead, state_kernel, grad_step)
    grad_value = complete(after(narrow, ahead_value), last_rows, input_kernel, grad_value)
    gate_send, out_send = after(arrived, (gate_send, out_send))
    gate_got, out_got = swapped(gate_send, "ctx", 1), swapped(out_send, "ctx", 2)
    other_value = swapped(grad_value, "dp", 1)
    other_narrow = swapped(narrow, "dp", 1)
    gate_send, out_send = after(grad_value, (gate_send, out_send))
    gate_got, out_got = swapped(gate_send, "ctx", 1), swapped(out_send, "ctx", 2)
    first_keep, first_send, second_keep, second_send = value_weights(
        plan, ctx_size, (normed, other_normed), (grad_value, other_value)
    )
    first_got, second_got = swapped(first_send, "ctx", 1), swapped(second_send, "ctx", 2)
    parts, row_sums, col_sums = input_partials(
        place, tensor_size, grad_gate, after((first_keep, other_narrow), grad_value), narrow, residual, row(pre_gain), gate_weight,
        input_weight, state_weight, step_weight
    )
    packed = sums_of(place, tensor_size, row_sums, col_sums, taps_grad, state2)
    packed = [packed, *from_all(packed, "tensor")]
    sent = line_first(after(packed[0], parts), "tensor")
    packed, sent = after(sent, packed), after(packed, sent)
    moving = lax.ppermute(sent, "tensor", [(0, 1), (tensor_size - 1, tensor_size - 2)])
    wide_stay, gate_away, out_away = halves(gate_keep, out_keep, *after(sent, (gate_got, out_got)))
    gate_got, out_got = swapped(gate_away, "ctx", 2), swapped(out_away, "ctx", 1)
    value_stay, first_away, second_away = halves(first_keep, second_keep, *after(wide_stay, (first_got, second_got)))
    first_got, second_got = swapped(first_away, "ctx", 2), swapped(second_away, "ctx", 1)
    sums, small = small_sums(place, tensor_size, tokens, after(value_stay, packed), kernel_grad, gain_grad, small)
    other_small = swapped(small, "dp", 1)
    narrow_keep, narrow_send = narrow_weights(
        after(small, plan), ctx_size, (normed, other_normed), (narrow, other_narrow), (small, other_small)
    )
    narrow_got = swapped(narrow_send, "ctx", 1)
    moving, gate_got, out_got, first_got, second_got = lax.optimization_barrier(
        after(narrow_keep, (moving, gate_got, out_got, first_got, second_got))
    )
    sent, moving = line_step(parts, 2, moving, "tensor")
    value_chunk = summed(value_stay, *after(sent, (first_got, second_got)))
    wide_chunk = summed(wide_stay, *after(value_chunk, (gate_got, out_got)))
    wide_here = lax.all_gather(wide_chunk, "ctx", tiled=True)
    output = (resid_part + after(wide_chunk, branch)).astype(bf16)
    moving, narrow_got, output = lax.optimization_barrier(after(wide_chunk, (moving, narrow_got, output)))
    narrow_stay, narrow_away = pair_sums(narrow_keep, narrow_got)
    narrow_got = swapped(narrow_away, "ctx", 2)
    sent, moving = line_step(parts, 3, after(narrow_stay, moving), "tensor")
    narrow_total = over_dp(narrow_stay + after(sent, narrow_got))
    chunk = jnp.concatenate([value_chunk, narrow_total[:LANES].astype(bf16)], axis=0)
    chunks = [swapped(chunk, "ctx", k) for k in range(1, ctx_size)]
    small_total = narrow_total[LANES:]
    small_total = jnp.concatenate([small_total[:, i : i + LANES] for i in range(0, small_total.shape[1], LANES)], axis=0)
    wide_rows = inner // LANES
    at = CONV * wide_rows
    kernel_grad = small_total[:at].reshape(CONV, inner)
    gain_grad = small_total[at : at + wide_rows].reshape(inner)
    at += wide_rows
    small = small_total[at : at + 3, :head_count]
    at += 3
    gain_rows = width // tensor_size // LANES
    pre_gain_grad = small_total[at : at + gain_rows].reshape(width // tensor_size)
    at += gain_rows
    taps_grad = small_total[at : at + CONV * state2 // LANES].reshape(CONV, state2)
    smalls = (pre_gain_grad, kernel_grad, taps_grad, small[1], small[2], small[0], gain_grad)
    moving, smalls = lax.optimization_barrier((moving, smalls))
    input_grad = final(place, parts, moving, residual, cotangent, row(pre_gain), sums)
    chunks = lax.optimization_barrier(after(input_grad, chunks))
    narrow_here = joined(chunk, *chunks)
    narrow_there = swapped(narrow_here, "dp", 1)
    wide_here = after(chunks, wide_here)
    wide_there = swapped(wide_here, "dp", 1)
    gate_weight_grad, out_weight_grad = wide_together(after(narrow_here, plan), ctx_size, wide_here, wide_there)
    input_weight_grad, state_weight_grad, step_weight_grad = narrow_together(
        plan, ctx_size, narrow_here, after(gate_weight_grad, narrow_there), state_part, head_count
    )
    return (
        output[None],
        input_grad[None],
        smalls[0],
        gate_weight_grad,
        input_weight_grad,
        state_weight_grad.T,
        step_weight_grad.T,
        *smalls[1:],
        out_weight_grad,
    )


def solution(mesh):
    in_specs = (
        P("dp", "ctx", None),
        P(),
        P(None, "tensor"),
        P(None, "tensor"),
        P(),
        P(None, "tensor"),
        P(None, "tensor"),
        P(),
        P("tensor"),
        P("tensor"),
        P("tensor"),
        P("tensor"),
        P("tensor", None),
        P("dp", "ctx", None),
    )
    out_specs = (
        P("dp", "ctx", "tensor"),
        P("dp", "ctx", "tensor"),
        P("tensor"),
        P(None, "tensor"),
        P(None, "tensor"),
        P(None, "tensor"),
        P(None, "tensor"),
        P(None, "tensor"),
        P(),
        P("tensor"),
        P("tensor"),
        P("tensor"),
        P("tensor"),
        P("tensor", None),
    )
    return jax.shard_map(per_device, mesh=mesh, in_specs=in_specs, out_specs=out_specs, check_vma=False)
```
